128 devices in a mesh: row: 4 (over y), col: 32 (over z, x, core).
Axes of the slice: x: 4, y: 4, z: 4, core: 2. Of those that a mesh axis runs over, the one named last changes fastest.
Arguments:
- ladder_amps: bfloat16 [6144, 8192], P('row', 'col'), may hold values from -6 to 6
- ladder_integrals: bfloat16 [8192, 4096], P('row', 'col'), may hold values from -0.0625 to 0.0625
- cycle_amps: bfloat16 [32, 320, 4096], P(None, 'col', 'row'), may hold values from -6 to 6
- cycle_integrals: bfloat16 [20480, 12288], P('row', 'col'), may hold values from -0.0390625 to 0.0390625
- amp_screen: int32 [32, 2], P('row'), may hold values 0 or 1
- integral_screen: int32 [128, 64], P('row', 'col'), may hold values 0 or 1
- occupied_i: float32 [32], P('row'), may hold values from -3 to -0.5
- occupied_j: float32 [192], replicated, may hold values from -3 to -0.5
- virtual_a: float32 [64], P('col'), may hold values from 0.5 to 3
- virtual_b: float32 [64], replicated, may hold values from 0.5 to 3
Outputs:
- update: float32 [6144, 4096], P('row', 'col')
The draws below stay inside these ranges and needn't reach their ends.
All inputs are finite; a program needn't handle non-finite values. No bound on the sum of `amp_screen` or of `integral_screen` on one device may be relied on, other than what follows from the above.
Results may differ from the reference program's by a relative error of at most 0.0023.
Values may be sent and summed in bfloat16 or wider, within the bound.
A program may use at most 192 MiB of HBM per device.

```python
import jax
import jax.numpy as jnp

O = 320
TILE = 64
OI = 32
LT = 2
OJ = 192


def with_ends(array, own_key, smallest, high):
    longest = array.shape.index(max(array.shape))
    spots = []
    for shift in (0, 1):
        where = [jax.random.randint(jax.random.fold_in(own_key, axis), (), 0, length) for axis, length in enumerate(array.shape)]
        where[longest] = (where[longest] + shift) % array.shape[longest]
        spots.append(tuple(where))
    return array.at[spots[0]].set(smallest).at[spots[1]].set(high)


def steps_of(stream_key, shape, cuts, least, top_value):
    gain = 1.0
    for dim, parts in cuts:
        steps = jax.random.uniform(jax.random.fold_in(jax.random.fold_in(stream_key, 6), dim), (parts,), jnp.float32, least / len(cuts), top_value / len(cuts))
        gain = gain * jnp.repeat(jnp.exp(steps), shape[dim] // parts).reshape((-1,) + (1,) * (len(shape) - 1 - dim))
    return gain


def gaussian(own_key, dims, deviation, bound, shards=(), kind=jnp.bfloat16):
    values = deviation * jax.random.normal(own_key, dims, jnp.float32)
    if shards:
        values = values * steps_of(own_key, dims, shards, -0.22, 0.18)
    return jnp.clip(values, -bound, bound).astype(kind)


def setup_inputs(seed: int = 0) -> dict:
    key_of = jax.random.split(jax.random.key(seed), 11)
    ladder_amps = gaussian(key_of[0], (OI * OJ, LT * TILE * TILE), 1.0, 6.0, ((0, 4), (1, 32)))
    ladder_integrals = gaussian(key_of[1], (LT * TILE * TILE, TILE * TILE), (LT * TILE * TILE) ** -0.5, 0.0625, ((0, 4), (1, 32)))
    cycle_amps = gaussian(key_of[2], (OI, O, TILE * TILE), 1.0, 6.0, ((1, 32), (2, 4)))
    cycle_integrals = gaussian(key_of[3], (O * TILE, OJ * TILE), (O * TILE) ** -0.5, 0.0390625, ((0, 4), (1, 32)))
    amp_screen = with_ends((jax.random.randint(key_of[4], (OI, LT), 0, 4) < 3).astype(jnp.int32), jax.random.fold_in(key_of[4], 1), 0, 1)
    integral_screen = with_ends((jax.random.randint(key_of[5], (LT * TILE, TILE), 0, 4) < 3).astype(jnp.int32), jax.random.fold_in(key_of[5], 1), 0, 1)
    occupied_i = jnp.clip(-3.0 + 2.5 * jax.random.uniform(key_of[6], (OI,), jnp.float32) ** steps_of(key_of[6], (OI,), ((0, 4),), -0.2, 0.2), -3.0, -0.5)
    occupied_j = jnp.clip(jax.random.uniform(key_of[7], (OJ,), jnp.float32, -3.0, -0.5), -3.0, -0.5)
    virtual_a = jnp.clip(0.5 + 2.5 * jax.random.uniform(key_of[8], (TILE,), jnp.float32) ** steps_of(key_of[8], (TILE,), ((0, 32),), -0.2, 0.2), 0.5, 3.0)
    virtual_b = jnp.clip(jax.random.uniform(key_of[9], (TILE,), jnp.float32, 0.5, 3.0), 0.5, 3.0)
    return {"ladder_amps": ladder_amps, "ladder_integrals": ladder_integrals, "cycle_amps": cycle_amps, "cycle_integrals": cycle_integrals, "amp_screen": amp_screen, "integral_screen": integral_screen, "occupied_i": occupied_i, "occupied_j": occupied_j, "virtual_a": virtual_a, "virtual_b": virtual_b}


def reference(ladder_amps, ladder_integrals, cycle_amps, cycle_integrals, amp_screen, integral_screen, occupied_i, occupied_j, virtual_a, virtual_b):
    amp_mask = jnp.repeat(jnp.repeat(amp_screen, OJ, axis=0), TILE * TILE, axis=1).astype(jnp.bfloat16)
    screened_amps = ladder_amps * amp_mask
    int_mask = jnp.repeat(jnp.repeat(integral_screen, TILE, axis=0), TILE, axis=1).astype(jnp.bfloat16)
    screened_integrals = ladder_integrals * int_mask
    ladder_term = jnp.dot(screened_amps, screened_integrals, preferred_element_type=jnp.float32)
    cycle_cols = cycle_amps.reshape(OI, O, TILE, TILE).transpose(0, 2, 1, 3).reshape(OI * TILE, O * TILE)
    cycle_term = jnp.dot(cycle_cols, cycle_integrals, preferred_element_type=jnp.float32).astype(jnp.bfloat16)
    cycle_back = cycle_term.reshape(OI, TILE, OJ, TILE).transpose(0, 2, 1, 3).reshape(OI * OJ, TILE * TILE)
    residual = ladder_term + cycle_back.astype(jnp.float32)
    virtual_sum = (virtual_a[:, None] + virtual_b[None, :]).reshape(-1)
    occupied_sum = (occupied_i[:, None] + occupied_j[None, :]).reshape(-1)
    denominator = virtual_sum[None, :] - occupied_sum[:, None]
    return residual / denominator
```

```python
import functools

import jax
import jax.numpy as jnp
from jax import lax
from jax.experimental import pallas as pl
from jax.experimental.pallas import tpu as pltpu
from jax.sharding import PartitionSpec as P

MESH = pl.DeviceIdType.MESH
N = 4
SENDS = 160


def kernel(
    s_ref,
    la_ref,
    lb_ref,
    cb_ref,
    lad_ref,
    fin_ref,
    a_buf,
    la_buf,
    lb_buf,
    lc,
    lc_a,
    lc_b,
    cc,
    cc_a,
    cc_b,
    outb,
    fin,
    send_sem,
    a_sem,
    la_sem,
    lx_sem,
    lb_sem,
    lc_sem,
    cc_sem,
    fin_sem,
    local_sem,
):
    y = lax.axis_index("row")
    col = lax.axis_index("col")
    z = col // 8
    x = (col // 2) % N
    c = col % 2

    def wrap(value):
        return lax.rem(value + 2 * N, N)

    def device(yy, zz, xx, core):
        return (yy, zz * 8 + xx * 2 + core)

    sibling = device(y, z, x, 1 - c)
    partner = device(z, y, x, c)
    rows, depth = s_ref.shape
    half_rows = rows // 2

    barrier = pltpu.get_barrier_semaphore()

    def greet(other):
        pl.semaphore_signal(barrier, inc=1, device_id=other, device_id_type=MESH)

    for step in range(1, 8 * N):
        greet((y, lax.rem(col + step, 8 * N)))
    for step in range(1, N):
        greet((wrap(y + step), col))

    @pl.when(y != z)
    def _():
        greet(partner)
        pl.semaphore_wait(barrier, 8 * N + N - 1)

    @pl.when(y == z)
    def _():
        pl.semaphore_wait(barrier, 8 * N + N - 2)

    started = []

    def send(src, dst, sem, other):
        copy = pltpu.make_async_remote_copy(
            src_ref=src,
            dst_ref=dst,
            send_sem=send_sem.at[len(started)],
            recv_sem=sem,
            device_id=other,
            device_id_type=MESH,
        )
        copy.start()
        started.append(copy)

    def arrived(dst, sem):
        pltpu.make_async_remote_copy(
            src_ref=dst,
            dst_ref=dst,
            send_sem=send_sem.at[0],
            recv_sem=sem,
            device_id=sibling,
            device_id_type=MESH,
        ).wait_recv()

    def a_slot(p1, p2, h=None):
        zz, xx = c * p1 + (1 - c) * p2, c * p2 + (1 - c) * p1
        if h is None:
            return a_buf.at[zz, xx, c], a_sem.at[zz, xx, c, 0]
        return a_buf.at[zz, xx, c, pl.ds(h * half_rows, half_rows)], a_sem.at[zz, xx, c, h]

    la_half = la_ref.shape[0] // 2

    def la_slot(zz, core, h=None):
        if h is None:
            return la_buf.at[zz, core], la_sem.at[zz, core, 0]
        return la_buf.at[zz, core, pl.ds(h * la_half, la_half)], la_sem.at[zz, core, h]

    lb_rows = lb_buf.shape[1]
    lb_half = lb_rows // 2

    def lb_slot(yy, h):
        return lb_buf.at[yy, pl.ds(h * lb_half, lb_half)], lb_sem.at[yy, h]

    def ring_start(slot, at, plus, minus):
        for h, other in ((0, plus), (1, minus), (1, plus), (0, minus)):
            ref, sem = slot(at, h)
            send(ref, ref, sem, other)

    def ring_near(slot, at, plus, minus):
        ref, sem = slot(wrap(at - 1), 0)
        arrived(ref, sem)
        send(ref, ref, sem, plus)
        ref, sem = slot(wrap(at + 1), 1)
        arrived(ref, sem)
        send(ref, ref, sem, minus)
        arrived(*slot(wrap(at - 1), 1))
        arrived(*slot(wrap(at + 1), 0))

    def ring_far(slot, at):
        for h in range(2):
            arrived(*slot(wrap(at + 2), h))

    def share(ref, sem):
        send(ref, ref, sem, sibling)

    p1, p2 = c * z + (1 - c) * x, c * x + (1 - c) * z
    d1_plus = device(y, wrap(z + c), wrap(x + 1 - c), c)
    d1_minus = device(y, wrap(z - c), wrap(x - 1 + c), c)
    d2_plus = device(y, wrap(z + 1 - c), wrap(x + c), c)
    d2_minus = device(y, wrap(z - 1 + c), wrap(x - c), c)
    z_plus, z_minus = device(y, wrap(z + 1), x, c), device(y, wrap(z - 1), x, c)
    x_plus, x_minus = device(y, z, wrap(x + 1), c), device(y, z, wrap(x - 1), c)
    y_plus, y_minus = (wrap(y + 1), col), (wrap(y - 1), col)

    def own_block(h):
        part = pl.ds(h * half_rows, half_rows)
        return s_ref.at[part], a_buf.at[y, x, c, part], a_sem.at[y, x, c, h]

    @pl.when(y != z)
    def _():
        for h in range(2):
            src, dst, sem = own_block(h)
            pltpu.make_async_remote_copy(
                src_ref=src,
                dst_ref=dst,
                send_sem=send_sem.at[SENDS - 1 - h],
                recv_sem=sem,
                device_id=partner,
                device_id_type=MESH,
            ).start()

    @pl.when(y == z)
    def _():
        a_buf[z, x, c] = s_ref[...]

    width = lb_ref.shape[1]
    for step in range(1, N):
        to = wrap(x + step)
        send(
            lb_ref.at[pl.ds(pl.multiple_of(to * lb_rows, lb_rows), lb_rows)],
            lb_buf.at[y, :, pl.ds(pl.multiple_of(x * width, width), width)],
            lx_sem.at[x],
            device(y, z, to, c),
        )
    keep_lb = pltpu.make_async_copy(
        lb_ref.at[pl.ds(pl.multiple_of(x * lb_rows, lb_rows), lb_rows)],
        lb_buf.at[y, :, pl.ds(pl.multiple_of(x * width, width), width)],
        local_sem.at[0],
    )
    keep_lb.start()
    keep_la = pltpu.make_async_copy(la_ref, la_buf.at[z, c], local_sem.at[1])
    keep_la.start()
    keep_la.wait()
    ring_start(lambda p, h: la_slot(p, c, h), z, z_plus, z_minus)
    share(*la_slot(z, c))

    @pl.when(y != z)
    def _():
        for h in range(2):
            src, _, _ = own_block(h)
            dst, sem = a_buf.at[z, x, c, pl.ds(h * half_rows, half_rows)], a_sem.at[z, x, c, h]
            copy = pltpu.make_async_remote_copy(
                src_ref=src,
                dst_ref=dst,
                send_sem=send_sem.at[SENDS - 1 - h],
                recv_sem=sem,
                device_id=partner,
                device_id_type=MESH,
            )
            copy.wait_send()
            copy.wait_recv()

    def first(p, h=None):
        return a_slot(p, p2, h)

    def second(q):
        return lambda p, h=None: a_slot(q, p, h)

    ring_start(first, p1, d1_plus, d1_minus)
    ring_start(second(p1), p2, d2_plus, d2_minus)
    share(*a_slot(p1, p2))

    keep_lb.wait()
    for step in range(1, N):
        source = wrap(x + step)
        arrived(lb_buf.at[y, :, pl.ds(pl.multiple_of(source * width, width), width)], lx_sem.at[source])
    ring_start(lb_slot, y, y_plus, y_minus)

    ring_near(first, p1, d1_plus, d1_minus)
    for q in (wrap(p1 - 1), wrap(p1 + 1)):
        ring_start(second(q), p2, d2_plus, d2_minus)
        share(*a_slot(q, p2))

    ring_near(lambda p, h: la_slot(p, c, h), z, z_plus, z_minus)
    for q in (wrap(z - 1), wrap(z + 1)):
        share(*la_slot(q, c))
    ring_near(lb_slot, y, y_plus, y_minus)

    ring_far(first, p1)
    q = wrap(p1 + 2)
    ring_start(second(q), p2, d2_plus, d2_minus)
    share(*a_slot(q, p2))

    def second_near(q):
        ring_near(second(q), p2, d2_plus, d2_minus)
        for p in (wrap(p2 - 1), wrap(p2 + 1)):
            share(*a_slot(q, p))

    def second_far(q):
        ring_far(second(q), p2)
        share(*a_slot(q, wrap(p2 + 2)))

    second_near(p1)

    ring_far(lambda p, h: la_slot(p, c, h), z)
    share(*la_slot(wrap(z + 2), c))
    ring_far(lb_slot, y)
    for step in range(N):
        arrived(*la_slot(wrap(z + step), 1 - c))

    tile = 256
    lk = la_ref.shape[1]

    @pl.loop(0, la_ref.shape[0] // tile)
    def _(m):
        part = pl.ds(pl.multiple_of(m * tile, tile), tile)
        total = jnp.zeros((tile, lb_buf.shape[2]), jnp.float32)
        for zz in range(N):
            for core in range(2):
                total += jnp.dot(
                    la_buf[zz, core, part, :],
                    lb_buf[zz, pl.ds(core * lk, lk), :],
                    preferred_element_type=jnp.float32,
                )
        for xx in range(N):
            lc[xx, part, :] = total[:, xx * width : (xx + 1) * width]

    def reduce_start(ref, land, sem, at, plus, minus):
        half = ref.shape[1] // 2
        for h, other in ((0, plus), (1, minus)):
            send(ref.at[wrap(at + 2), pl.ds(h * half, half)], land.at[h], sem.at[h], other)

    def reduce_middle(ref, land_a, land_b, sem, at, plus, minus):
        half = ref.shape[1] // 2
        for h, to, other in ((0, wrap(at + 1), plus), (1, wrap(at - 1), minus)):
            arrived(land_a.at[h], sem.at[h])
            part = pl.ds(h * half, half)
            ref[to, part, :] = ref[to, part, :] + land_a[h]
            send(ref.at[to], land_b.at[h], sem.at[2 + h], other)

    def reduce_end(ref, land_b, sem, at):
        for h in range(2):
            arrived(land_b.at[h], sem.at[2 + h])
        return ref[at] + land_b[0] + land_b[1]

    reduce_start(lc, lc_a, lc_sem, x, x_plus, x_minus)

    second_far(p1)
    second_near(wrap(p1 - 1))
    reduce_middle(lc, lc_a, lc_b, lc_sem, x, x_plus, x_minus)
    second_near(wrap(p1 + 1))
    second_near(wrap(p1 + 2))
    second_far(wrap(p1 - 1))
    second_far(wrap(p1 + 1))
    second_far(wrap(p1 + 2))

    lad_ref[...] = reduce_end(lc, lc_b, lc_sem, x)

    offsets = (0, 1, 3, 2)

    def block(k):
        zz = wrap(z + offsets[k])
        for xx in range(N):
            arrived(a_buf.at[zz, xx, 1 - c], a_sem.at[zz, xx, 1 - c, 0])

        @pl.loop(0, rows // tile)
        def _(m):
            part = pl.ds(pl.multiple_of(m * tile, tile), tile)
            total = jnp.zeros((tile, cb_ref.shape[1]), jnp.float32)
            for xx in range(N):
                for core in range(2):
                    total += jnp.dot(
                        a_buf[zz, xx, core, part, :],
                        cb_ref[pl.ds((xx * 2 + core) * depth, depth), :],
                        preferred_element_type=jnp.float32,
                    )
            quarter = rows // N
            for n in range(tile // quarter):
                cc[k, m * (tile // quarter) + n] = total[n * quarter : (n + 1) * quarter]

        reduce_start(cc.at[k], cc_a.at[k], cc_sem.at[k], y, y_plus, y_minus)

    def block_middle(k):
        reduce_middle(cc.at[k], cc_a.at[k], cc_b.at[k], cc_sem.at[k], y, y_plus, y_minus)

    piece = rows // N // 8

    def block_end(k):
        total = reduce_end(cc.at[k], cc_b.at[k], cc_sem.at[k], y)
        outb[k] = total.astype(outb.dtype)
        zz = wrap(z + offsets[k])
        mine = x * 2 + c
        for step in range(1 if k == 0 else 0, 8):
            to = lax.rem(mine + step, 8)
            send(
                outb.at[k, pl.ds(pl.multiple_of(to * piece, piece), piece)],
                fin.at[col],
                fin_sem.at[col],
                (y, zz * 8 + to),
            )
        if k == 0:
            fin[col] = outb[k, pl.ds(pl.multiple_of(mine * piece, piece), piece), :]

    block(0)
    block(1)
    block_middle(0)
    block(2)
    block_middle(1)
    block_end(0)
    block(3)
    block_middle(2)
    block_end(1)
    block_middle(3)
    block_end(2)
    block_end(3)

    for step in range(1, 8 * N):
        source = lax.rem(col + step, 8 * N)
        arrived(fin.at[source], fin_sem.at[source])
    fin_ref[...] = fin[...]
    for copy in started:
        copy.wait_send()


def per_device(
    ladder_amps,
    ladder_integrals,
    cycle_amps,
    cycle_integrals,
    amp_screen,
    integral_screen,
    occupied_i,
    occupied_j,
    virtual_a,
    virtual_b,
):
    tile = virtual_b.shape[0]
    pair_count = occupied_j.shape[0]
    local_i = occupied_i.shape[0]
    local_a = virtual_a.shape[0]
    col = lax.axis_index("col")
    col_count = lax.axis_size("col")

    local_cols = ladder_amps.shape[1]
    mine = lax.dynamic_slice_in_dim(amp_screen, (col * local_cols) // (tile * tile), 1, axis=1)
    amp_mask = jnp.broadcast_to(mine[:, None, :], (local_i, pair_count, 1)).reshape(-1, 1)
    la = ladder_amps * amp_mask.astype(jnp.bfloat16)
    int_mask = jnp.repeat(jnp.repeat(integral_screen, tile, axis=0), tile, axis=1).astype(jnp.bfloat16)
    lb = ladder_integrals * int_mask

    all_i, local_k, _ = cycle_amps.shape
    s = cycle_amps.reshape(N, all_i // N, local_k, 8, local_a, tile).transpose(0, 3, 1, 4, 2, 5)
    s = s.reshape(all_i * 8 * local_a, local_k * tile)

    rows, depth = s.shape
    nc = cycle_integrals.shape[1]
    lm, lk = la.shape
    lrows, ln = lb.shape
    quarter = rows // N
    piece = quarter // 8
    f32, bf16 = jnp.float32, jnp.bfloat16
    dma = pltpu.SemaphoreType.DMA
    vmem = pl.BlockSpec(memory_space=pltpu.VMEM)
    ladder, cycle = pl.pallas_call(
        kernel,
        out_shape=(
            jax.ShapeDtypeStruct((lm, ln), f32),
            jax.ShapeDtypeStruct((col_count, piece, nc), bf16),
        ),
        in_specs=[vmem] * 4,
        out_specs=(vmem, vmem),
        scratch_shapes=[
            pltpu.VMEM((N, N, 2, rows, depth), bf16),
            pltpu.VMEM((N, 2, lm, lk), bf16),
            pltpu.VMEM((N, lrows // N, N * ln), bf16),
            pltpu.VMEM((N, lm, ln), f32),
            pltpu.VMEM((2, lm // 2, ln), f32),
            pltpu.VMEM((2, lm, ln), f32),
            pltpu.VMEM((N, N, quarter, nc), f32),
            pltpu.VMEM((N, 2, quarter // 2, nc), f32),
            pltpu.VMEM((N, 2, quarter, nc), f32),
            pltpu.VMEM((N, quarter, nc), bf16),
            pltpu.VMEM((col_count, piece, nc), bf16),
            dma((SENDS,)),
            dma((N, N, 2, 2)),
            dma((N, 2, 2)),
            dma((N,)),
            dma((N, 2)),
            dma((4,)),
            dma((N, 4)),
            dma((col_count,)),
            dma((2,)),
        ],
        compiler_params=pltpu.CompilerParams(
            collective_id=0, has_side_effects=True, vmem_limit_bytes=56 * 2**20
        ),
        cost_estimate=pl.CostEstimate(
            flops=2 * (N * rows * N * 2 * depth * nc + lm * N * 2 * lk * N * ln),
            bytes_accessed=8 * 2**20,
            transcendentals=0,
        ),
    )(s, la, lb, cycle_integrals)

    j_local = nc // tile
    cycle = cycle.reshape(col_count, local_i, local_a, j_local, tile).transpose(1, 0, 3, 2, 4)
    cycle = cycle.reshape(local_i * pair_count, local_a * tile)
    residual = ladder + cycle.astype(f32)
    virtual_sum = (virtual_a[:, None] + virtual_b[None, :]).reshape(-1)
    occupied_sum = (occupied_i[:, None] + occupied_j[None, :]).reshape(-1)
    denominator = virtual_sum[None, :] - occupied_sum[:, None]
    return residual / denominator


def solution(mesh):
    placed = (
        P("row", "col"),
        P("row", "col"),
        P(None, "col", "row"),
        P("row", "col"),
        P("row", None),
        P("row", "col"),
        P("row"),
        P(),
        P("col"),
        P(),
    )
    return jax.shard_map(
        per_device, mesh=mesh, in_specs=placed, out_specs=P("row", "col"), check_vma=False
    )
```

```python
import functools

import jax
import jax.numpy as jnp
from jax import lax
from jax.experimental import pallas as pl
from jax.experimental.pallas import tpu as pltpu
from jax.sharding import PartitionSpec as P

MESH = pl.DeviceIdType.MESH
N = 4
SENDS = 280
GROUPS = 4


def axis_order(core):
    return (core, core, core, core)


def kernel(
    s_ref,
    la_ref,
    lb_ref,
    cb_ref,
    lad_ref,
    fin_ref,
    middle,
    a_buf,
    la_buf,
    lb_buf,
    lc,
    lc_a,
    lc_b,
    cc,
    cc_a,
    cc_b,
    outb,
    fin,
    send_sem,
    middle_sem,
    a_sem,
    la_sem,
    lx_sem,
    lb_sem,
    lc_sem,
    cc_sem,
    fin_sem,
    local_sem,
):
    y = lax.axis_index("row")
    col = lax.axis_index("col")
    z = col // 8
    x = (col // 2) % N
    c = col % 2

    def wrap(value):
        return lax.rem(value + 2 * N, N)

    def device(yy, zz, xx, core):
        return (yy, zz * 8 + xx * 2 + core)

    sibling = device(y, z, x, 1 - c)
    rows, depth = s_ref.shape
    group = rows // GROUPS
    half = group // 2

    barrier = pltpu.get_barrier_semaphore()

    def greet(other):
        pl.semaphore_signal(barrier, inc=1, device_id=other, device_id_type=MESH)

    for step in range(1, 8 * N):
        greet((y, lax.rem(col + step, 8 * N)))
    for step in range(1, N):
        greet((wrap(y + step), col))

    pl.semaphore_wait(barrier, 8 * N + N - 2)

    started = []

    def send(src, dst, sem, other):
        copy = pltpu.make_async_remote_copy(
            src_ref=src,
            dst_ref=dst,
            send_sem=send_sem.at[len(started)],
            recv_sem=sem,
            device_id=other,
            device_id_type=MESH,
        )
        copy.start()
        started.append(copy)

    def arrived(dst, sem):
        pltpu.make_async_remote_copy(
            src_ref=dst,
            dst_ref=dst,
            send_sem=send_sem.at[0],
            recv_sem=sem,
            device_id=sibling,
            device_id_type=MESH,
        ).wait_recv()

    def a_slot(zz, xx, g, h=None):
        if h is None:
            return a_buf.at[zz, xx, c, pl.ds(g * group, group)], a_sem.at[zz, xx, c, g, 0]
        return a_buf.at[zz, xx, c, pl.ds(g * group + h * half, half)], a_sem.at[zz, xx, c, g, h]

    la_half = la_ref.shape[0] // 2

    def la_slot(zz, core, h=None):
        if h is None:
            return la_buf.at[zz, core], la_sem.at[zz, core, 0]
        return la_buf.at[zz, core, pl.ds(h * la_half, la_half)], la_sem.at[zz, core, h]

    lb_rows = lb_buf.shape[1]
    lb_half = lb_rows // 2

    def lb_slot(yy, h):
        return lb_buf.at[yy, pl.ds(h * lb_half, lb_half)], lb_sem.at[yy, h]

    def ring_start(slot, at, plus, minus):
        for h, other in ((0, plus), (1, minus), (1, plus), (0, minus)):
            ref, sem = slot(at, h)
            send(ref, ref, sem, other)

    def ring_near(slot, at, plus, minus):
        ref, sem = slot(wrap(at - 1), 0)
        arrived(ref, sem)
        send(ref, ref, sem, plus)
        ref, sem = slot(wrap(at + 1), 1)
        arrived(ref, sem)
        send(ref, ref, sem, minus)
        arrived(*slot(wrap(at - 1), 1))
        arrived(*slot(wrap(at + 1), 0))

    def ring_far(slot, at):
        for h in range(2):
            arrived(*slot(wrap(at + 2), h))

    def share(ref, sem):
        send(ref, ref, sem, sibling)

    z_plus, z_minus = device(y, wrap(z + 1), x, c), device(y, wrap(z - 1), x, c)
    x_plus, x_minus = device(y, z, wrap(x + 1), c), device(y, z, wrap(x - 1), c)
    y_plus, y_minus = (wrap(y + 1), col), (wrap(y - 1), col)

    def swapped(g, along=None):
        along = z if along is None else along
        return (y + along) % 2 + 2 * ((y // 2 + along // 2 + g % 2) % 2)

    def group_rows(g):
        return pl.ds(g * group, group)

    def over_z(g):
        part = group_rows(g)
        return pltpu.make_async_remote_copy(
            src_ref=s_ref.at[part],
            dst_ref=middle.at[part],
            send_sem=send_sem.at[SENDS - 1 - g],
            recv_sem=middle_sem.at[g],
            device_id=device(y, swapped(g), x, c),
            device_id_type=MESH,
        )

    def over_y(g, ref):
        part = group_rows(g)
        return pltpu.make_async_remote_copy(
            src_ref=ref.at[part],
            dst_ref=a_buf.at[z, x, c, part],
            send_sem=send_sem.at[SENDS - 1 - GROUPS - g],
            recv_sem=a_sem.at[z, x, c, g, 0],
            device_id=(swapped(g), col),
            device_id_type=MESH,
        )

    def start_over_z(g):
        @pl.when(y != 2 * (g % 2))
        def _():
            over_z(g).start()

    def start_over_y(g):
        still = 2 * (g % 2)

        @pl.when(y != still)
        def _():
            over_z(g).wait_recv()

            @pl.when(z != still)
            def _():
                over_y(g, middle).start()

            @pl.when(z == still)
            def _():
                a_buf[z, x, c, group_rows(g), :] = middle[group_rows(g), :]

        @pl.when(y == still)
        def _():
            @pl.when(z != still)
            def _():
                over_y(g, s_ref).start()

            @pl.when(z == still)
            def _():
                a_buf[z, x, c, group_rows(g), :] = s_ref[group_rows(g), :]

    def end_over_y(g):
        @pl.when(z != 2 * (g % 2))
        def _():
            over_y(g, middle).wait_recv()

    width = lb_ref.shape[1]
    for step in range(1, N):
        to = wrap(x + step)
        send(
            lb_ref.at[pl.ds(pl.multiple_of(to * lb_rows, lb_rows), lb_rows)],
            lb_buf.at[y, :, pl.ds(pl.multiple_of(x * width, width), width)],
            lx_sem.at[x],
            device(y, z, to, c),
        )
    keep_lb = pltpu.make_async_copy(
        lb_ref.at[pl.ds(pl.multiple_of(x * lb_rows, lb_rows), lb_rows)],
        lb_buf.at[y, :, pl.ds(pl.multiple_of(x * width, width), width)],
        local_sem.at[0],
    )
    keep_lb.start()
    keep_la = pltpu.make_async_copy(la_ref, la_buf.at[z, c], local_sem.at[1])
    keep_la.start()

    def la_own(p, h=None):
        return la_slot(p, c, h)

    def la_start():
        keep_la.wait()
        ring_start(la_own, z, z_plus, z_minus)
        share(*la_slot(z, c))

    def la_near():
        ring_near(la_own, z, z_plus, z_minus)
        for q in (wrap(z - 1), wrap(z + 1)):
            share(*la_slot(q, c))

    def la_far():
        ring_far(la_own, z)
        share(*la_slot(wrap(z + 2), c))

    def lb_start():
        keep_lb.wait()
        for step in range(1, N):
            source = wrap(x + step)
            arrived(lb_buf.at[y, :, pl.ds(pl.multiple_of(source * width, width), width)], lx_sem.at[source])
        ring_start(lb_slot, y, y_plus, y_minus)

    def lb_near():
        ring_near(lb_slot, y, y_plus, y_minus)

    def lb_far():
        ring_far(lb_slot, y)

    z_first = axis_order(c)

    def ring_of(is_z):
        dz, dx = is_z, 1 - is_z
        plus = device(y, wrap(z + dz), wrap(x + dx), c)
        minus = device(y, wrap(z - dz), wrap(x - dx), c)
        return is_z * z + (1 - is_z) * x, plus, minus

    def first(g):
        f = z_first[g]
        return (lambda q, h=None: a_slot(f * q + (1 - f) * z, f * x + (1 - f) * q, g, h)), ring_of(f)

    def second(g, k):
        f = z_first[g]
        p = wrap(f * z + (1 - f) * x + (0, 3, 1, 2)[k])
        return (lambda q, h=None: a_slot(f * p + (1 - f) * q, f * q + (1 - f) * p, g, h)), ring_of(1 - f)

    def second_start(g, k):
        slot, ring = second(g, k)
        ring_start(slot, *ring)
        share(*slot(ring[0]))

    def second_near(g, k):
        slot, ring = second(g, k)
        ring_near(slot, *ring)
        for p in (wrap(ring[0] - 1), wrap(ring[0] + 1)):
            share(*slot(p))

    def second_far(g, k):
        slot, ring = second(g, k)
        ring_far(slot, ring[0])
        share(*slot(wrap(ring[0] + 2)))

    def first_start(g):
        end_over_y(g)
        slot, ring = first(g)
        ring_start(slot, *ring)
        second_start(g, 0)

    def first_near(g):
        slot, ring = first(g)
        ring_near(slot, *ring)
        second_start(g, 1)
        second_start(g, 2)

    def first_far(g):
        slot, ring = first(g)
        ring_far(slot, ring[0])
        second_start(g, 3)

    def seconds_near(g):
        for k in range(N):
            second_near(g, k)

    def seconds_far(g):
        for k in range(N):
            second_far(g, k)

    tile = 256
    lk = la_ref.shape[1]

    def ladder():
        for step in range(N):
            arrived(*la_slot(wrap(z + step), 1 - c))

        @pl.loop(0, la_ref.shape[0] // tile)
        def _(m):
            part = pl.ds(pl.multiple_of(m * tile, tile), tile)
            total = jnp.zeros((tile, lb_buf.shape[2]), jnp.float32)
            for zz in range(N):
                for core in range(2):
                    total += jnp.dot(
                        la_buf[zz, core, part, :],
                        lb_buf[zz, pl.ds(core * lk, lk), :],
                        preferred_element_type=jnp.float32,
                    )
            for xx in range(N):
                lc[xx, part, :] = total[:, xx * width : (xx + 1) * width]

        reduce_start(lc, lc_a, lc_sem, x, x_plus, x_minus)

    def ladder_middle():
        reduce_middle(lc, lc_a, lc_b, lc_sem, x, x_plus, x_minus)

    def ladder_end():
        lad_ref[...] = reduce_end(lc, lc_b, lc_sem, x)

    def reduce_start(ref, land, sem, at, plus, minus):
        size = ref.shape[1] // 2
        for h, other in ((0, plus), (1, minus)):
            send(ref.at[wrap(at + 2), pl.ds(h * size, size)], land.at[h], sem.at[h], other)

    def reduce_middle(ref, land_a, land_b, sem, at, plus, minus):
        size = ref.shape[1] // 2
        for h, to, other in ((0, wrap(at + 1), plus), (1, wrap(at - 1), minus)):
            arrived(land_a.at[h], sem.at[h])
            part = pl.ds(h * size, size)
            ref[to, part, :] = ref[to, part, :] + land_a[h]
            send(ref.at[to], land_b.at[h], sem.at[2 + h], other)

    def reduce_end(ref, land_b, sem, at):
        for h in range(2):
            arrived(land_b.at[h], sem.at[2 + h])
        return ref[at] + land_b[0] + land_b[1]

    quarter = group // N
    pairs = 8 // GROUPS
    piece = quarter // pairs
    mine = x * 2 + c

    def cycle(g):
        for zz in range(N):
            for xx in range(N):
                arrived(a_buf.at[zz, xx, 1 - c, group_rows(g)], a_sem.at[zz, xx, 1 - c, g, 0])
        total = jnp.zeros((rows // GROUPS * N, cb_ref.shape[1]), jnp.float32)
        for xx in range(N):
            for core in range(2):
                left = jnp.concatenate([a_buf[zz, xx, core, group_rows(g), :] for zz in range(N)], axis=0)
                total += jnp.dot(
                    left,
                    cb_ref[pl.ds((xx * 2 + core) * depth, depth), :],
                    preferred_element_type=jnp.float32,
                )
        for zz in range(N):
            owner = swapped(g, zz)
            for n in range(N):
                cc[g, n, owner] = total[zz * group + n * quarter : zz * group + (n + 1) * quarter]
        reduce_start(cc.at[g], cc_a.at[g], cc_sem.at[g], y, y_plus, y_minus)

    def cycle_middle(g):
        reduce_middle(cc.at[g], cc_a.at[g], cc_b.at[g], cc_sem.at[g], y, y_plus, y_minus)

    def last_copy(g):
        turn = lax.rem(mine, pairs)
        return pltpu.make_async_remote_copy(
            src_ref=outb.at[g, z, pl.ds(pl.multiple_of(turn * piece, piece), piece)],
            dst_ref=fin.at[col],
            send_sem=send_sem.at[SENDS - 1 - 2 * GROUPS - g],
            recv_sem=fin_sem.at[col],
            device_id=(y, z * 8 + g * pairs + turn),
            device_id_type=MESH,
        )

    def cycle_end(g):
        outb[g] = reduce_end(cc.at[g], cc_b.at[g], cc_sem.at[g], y).astype(outb.dtype)
        for zstep in range(N):
            zz = wrap(z + zstep)
            for step in range(pairs):
                if zstep == 0 and step == 0:
                    continue
                turn = lax.rem(mine + step, pairs)
                send(
                    outb.at[g, zz, pl.ds(pl.multiple_of(turn * piece, piece), piece)],
                    fin.at[col],
                    fin_sem.at[col],
                    (y, zz * 8 + g * pairs + turn),
                )

        @pl.when(mine // pairs == g)
        def _():
            fin[col] = outb[g, z, pl.ds(pl.multiple_of(lax.rem(mine, pairs) * piece, piece), piece), :]

        @pl.when(mine // pairs != g)
        def _():
            last_copy(g).start()

    for g in range(GROUPS):
        start_over_z(g)
    la_start()
    start_over_y(0)
    first_start(0)
    start_over_y(1)
    lb_start()
    first_near(0)
    start_over_y(2)
    start_over_y(3)
    first_far(0)
    first_start(1)
    lb_near()
    seconds_near(0)
    first_near(1)
    first_far(1)
    la_near()
    lb_far()
    first_start(2)
    seconds_far(0)
    seconds_near(1)
    cycle(0)
    first_near(2)
    first_far(2)
    la_far()
    ladder()
    first_start(3)
    cycle_middle(0)
    seconds_far(1)
    cycle(1)
    seconds_near(2)
    cycle_end(0)
    first_near(3)
    first_far(3)
    ladder_middle()
    cycle_middle(1)
    seconds_far(2)
    cycle(2)
    cycle_end(1)
    ladder_end()
    seconds_near(3)
    cycle_middle(2)
    seconds_far(3)
    cycle(3)
    cycle_end(2)
    cycle_middle(3)
    cycle_end(3)

    for step in range(1, 8 * N):
        source = lax.rem(col + step, 8 * N)
        arrived(fin.at[source], fin_sem.at[source])
    fin_ref[...] = fin[...]
    for copy in started:
        copy.wait_send()
    for g in range(GROUPS):

        @pl.when(y != 2 * (g % 2))
        def _():
            over_z(g).wait_send()

        @pl.when(z != 2 * (g % 2))
        def _():
            over_y(g, middle).wait_send()

        @pl.when(mine // pairs != g)
        def _():
            last_copy(g).wait_send()


def per_device(
    ladder_amps,
    ladder_integrals,
    cycle_amps,
    cycle_integrals,
    amp_screen,
    integral_screen,
    occupied_i,
    occupied_j,
    virtual_a,
    virtual_b,
):
    tile = virtual_b.shape[0]
    pair_count = occupied_j.shape[0]
    local_i = occupied_i.shape[0]
    local_a = virtual_a.shape[0]
    col = lax.axis_index("col")
    col_count = lax.axis_size("col")

    local_cols = ladder_amps.shape[1]
    mine = lax.dynamic_slice_in_dim(amp_screen, (col * local_cols) // (tile * tile), 1, axis=1)
    amp_mask = jnp.broadcast_to(mine[:, None, :], (local_i, pair_count, 1)).reshape(-1, 1)
    la = ladder_amps * amp_mask.astype(jnp.bfloat16)
    int_mask = jnp.repeat(jnp.repeat(integral_screen, tile, axis=0), tile, axis=1).astype(jnp.bfloat16)
    lb = ladder_integrals * int_mask

    all_i, local_k, _ = cycle_amps.shape
    s = cycle_amps.reshape(N, all_i // N, local_k, GROUPS, 8 // GROUPS, local_a, tile)
    s = s.transpose(3, 0, 4, 1, 5, 2, 6)
    s = s.reshape(all_i * 8 * local_a, local_k * tile)

    rows, depth = s.shape
    nc = cycle_integrals.shape[1]
    lm, lk = la.shape
    lrows, ln = lb.shape
    quarter = rows // GROUPS // N
    piece = rows // N // 8
    f32, bf16 = jnp.float32, jnp.bfloat16
    dma = pltpu.SemaphoreType.DMA
    vmem = pl.BlockSpec(memory_space=pltpu.VMEM)
    ladder, cycle = pl.pallas_call(
        kernel,
        out_shape=(
            jax.ShapeDtypeStruct((lm, ln), f32),
            jax.ShapeDtypeStruct((col_count, piece, nc), bf16),
        ),
        in_specs=[vmem] * 4,
        out_specs=(vmem, vmem),
        scratch_shapes=[
            pltpu.VMEM((rows, depth), bf16),
            pltpu.VMEM((N, N, 2, rows, depth), bf16),
            pltpu.VMEM((N, 2, lm, lk), bf16),
            pltpu.VMEM((N, lrows // N, N * ln), bf16),
            pltpu.VMEM((N, lm, ln), f32),
            pltpu.VMEM((2, lm // 2, ln), f32),
            pltpu.VMEM((2, lm, ln), f32),
            pltpu.VMEM((GROUPS, N, N, quarter, nc), f32),
            pltpu.VMEM((GROUPS, 2, N // 2, quarter, nc), f32),
            pltpu.VMEM((GROUPS, 2, N, quarter, nc), f32),
            pltpu.VMEM((GROUPS, N, quarter, nc), bf16),
            pltpu.VMEM((col_count, piece, nc), bf16),
            dma((SENDS,)),
            dma((GROUPS,)),
            dma((N, N, 2, GROUPS, 2)),
            dma((N, 2, 2)),
            dma((N,)),
            dma((N, 2)),
            dma((4,)),
            dma((GROUPS, 4)),
            dma((col_count,)),
            dma((2,)),
        ],
        compiler_params=pltpu.CompilerParams(
            collective_id=0, has_side_effects=True, vmem_limit_bytes=56 * 2**20
        ),
        cost_estimate=pl.CostEstimate(
            flops=2 * (N * rows * N * 2 * depth * nc + lm * N * 2 * lk * N * ln),
            bytes_accessed=8 * 2**20,
            transcendentals=0,
        ),
    )(s, la, lb, cycle_integrals)

    j_local = nc // tile
    cycle = cycle.reshape(col_count, local_i, local_a, j_local, tile).transpose(1, 0, 3, 2, 4)
    cycle = cycle.reshape(local_i * pair_count, local_a * tile)
    residual = ladder + cycle.astype(f32)
    virtual_sum = (virtual_a[:, None] + virtual_b[None, :]).reshape(-1)
    occupied_sum = (occupied_i[:, None] + occupied_j[None, :]).reshape(-1)
    denominator = virtual_sum[None, :] - occupied_sum[:, None]
    return residual / denominator


def solution(mesh):
    placed = (
        P("row", "col"),
        P("row", "col"),
        P(None, "col", "row"),
        P("row", "col"),
        P("row", None),
        P("row", "col"),
        P("row"),
        P(),
        P("col"),
        P(),
    )
    return jax.shard_map(
        per_device, mesh=mesh, in_specs=placed, out_specs=P("row", "col"), check_vma=False
    )
```

```python
import functools

import jax
import jax.numpy as jnp
from jax import lax
from jax.experimental import pallas as pl
from jax.experimental.pallas import tpu as pltpu
from jax.sharding import PartitionSpec as P

MESH = pl.DeviceIdType.MESH
N = 4
SENDS = 280
GROUPS = 4


def axis_order(core):
    return (1, 1, core, 0)


def kernel(
    tile_size,
    amps_hbm,
    la_hbm,
    lb_hbm,
    cb_hbm,
    amp_screen,
    integral_screen,
    out_ref,
    amps,
    amps_wide,
    s_ref,
    la_ref,
    lb_ref,
    cb_ref,
    middle,
    a_buf,
    la_buf,
    lb_buf,
    lc,
    lc_a,
    lc_b,
    cc,
    cc_a,
    cc_b,
    outb,
    fin,
    send_sem,
    middle_sem,
    a_sem,
    la_sem,
    lx_sem,
    lb_sem,
    lc_sem,
    cc_sem,
    fin_sem,
    local_sem,
):
    y = lax.axis_index("row")
    col = lax.axis_index("col")
    z = col // 8
    x = (col // 2) % N
    c = col % 2

    def wrap(value):
        return lax.rem(value + 2 * N, N)

    def device(yy, zz, xx, core):
        return (yy, zz * 8 + xx * 2 + core)

    sibling = device(y, z, x, 1 - c)
    copies = [
        pltpu.make_async_copy(src, dst, local_sem.at[n])
        for n, (src, dst) in enumerate(((amps_hbm, amps), (la_hbm, la_ref), (lb_hbm, lb_ref), (cb_hbm, cb_ref)))
    ]
    for copy in copies:
        copy.start()

    rows, depth = s_ref.shape
    group = rows // GROUPS
    half = group // 2

    barrier = pltpu.get_barrier_semaphore()

    def greet(other):
        pl.semaphore_signal(barrier, inc=1, device_id=other, device_id_type=MESH)

    for step in range(1, 8 * N):
        greet((y, lax.rem(col + step, 8 * N)))
    for step in range(1, N):
        greet((wrap(y + step), col))

    blocks, local_k, lanes = amps.shape[0] // 8, amps.shape[1], 128
    stride = amps_wide.shape[1] // amps.shape[0]
    low = lax.broadcasted_iota(jnp.int32, (8, lanes), 1) < lanes // 2

    def joined(left, right):
        first_halves = jnp.where(low, left, pltpu.roll(right, lanes // 2, 1))
        second_halves = jnp.where(low, pltpu.roll(left, lanes // 2, 1), right)
        return first_halves, second_halves

    copies[0].wait()
    for i in range(amps.shape[0]):
        for t in range(8):
            wide = amps[i, :, t * lanes : (t + 1) * lanes].astype(jnp.float32)
            amps_wide[t, pl.ds(i * stride, local_k), :] = wide

    @pl.loop(0, blocks)
    def _(ib):
        for t in range(8):
            pairs = 8 // GROUPS
            row = (t // pairs) * group + ib * (group // blocks) + (t % pairs) * 16
            for m in range(local_k // 2):
                left, right = (
                    amps_wide[t, pl.ds(ib * 8 * stride + k, 8, stride=stride), :]
                    for k in (2 * m, 2 * m + 1)
                )
                s_ref[pl.ds(pl.multiple_of(row, 16), 16), m * lanes : (m + 1) * lanes] = jnp.concatenate(
                    joined(left, right), axis=0
                ).astype(s_ref.dtype)

    copies[1].wait()
    ladder_tile = (col * la_ref.shape[1]) // tile_size
    pair_count = la_ref.shape[0] // amp_screen.shape[0]
    for i in range(amp_screen.shape[0]):
        part = pl.ds(i * pair_count, pair_count)
        keep = amp_screen[i, ladder_tile].astype(jnp.float32).astype(la_ref.dtype)
        la_buf[z, c, part, :] = la_ref[part, :] * keep
    copies[2].wait()
    side = lb_ref.shape[0] // integral_screen.shape[0]
    for p in range(integral_screen.shape[0]):
        part = pl.ds(p * side, side)
        keep = jnp.where(low[:1], integral_screen[p, 0], integral_screen[p, 1])
        lb_ref[part, :] = lb_ref[part, :] * keep.astype(jnp.float32).astype(lb_ref.dtype)

    pl.semaphore_wait(barrier, 8 * N + N - 2)

    started = []

    def send(src, dst, sem, other):
        copy = pltpu.make_async_remote_copy(
            src_ref=src,
            dst_ref=dst,
            send_sem=send_sem.at[len(started)],
            recv_sem=sem,
            device_id=other,
            device_id_type=MESH,
        )
        copy.start()
        started.append(copy)

    def arrived(dst, sem):
        pltpu.make_async_remote_copy(
            src_ref=dst,
            dst_ref=dst,
            send_sem=send_sem.at[0],
            recv_sem=sem,
            device_id=sibling,
            device_id_type=MESH,
        ).wait_recv()

    def a_slot(zz, xx, g, h=None):
        if h is None:
            return a_buf.at[zz, xx, c, pl.ds(g * group, group)], a_sem.at[zz, xx, c, g, 0]
        return a_buf.at[zz, xx, c, pl.ds(g * group + h * half, half)], a_sem.at[zz, xx, c, g, h]

    la_half = la_ref.shape[0] // 2

    def la_slot(zz, core, h=None):
        if h is None:
            return la_buf.at[zz, core], la_sem.at[zz, core, 0]
        return la_buf.at[zz, core, pl.ds(h * la_half, la_half)], la_sem.at[zz, core, h]

    lb_rows = lb_buf.shape[1]
    lb_half = lb_rows // 2

    def lb_slot(yy, h):
        return lb_buf.at[yy, pl.ds(h * lb_half, lb_half)], lb_sem.at[yy, h]

    def ring_start(slot, at, plus, minus):
        for h, other in ((0, plus), (1, minus), (1, plus), (0, minus)):
            ref, sem = slot(at, h)
            send(ref, ref, sem, other)

    def ring_forward(slot, at, plus, minus):
        for h, source, other in ((0, wrap(at - 1), plus), (1, wrap(at + 1), minus)):
            ref, sem = slot(source, h)
            arrived(ref, sem)
            send(ref, ref, sem, other)

    def ring_near(slot, at):
        arrived(*slot(wrap(at - 1), 1))
        arrived(*slot(wrap(at + 1), 0))

    def ring_far(slot, at):
        for h in range(2):
            arrived(*slot(wrap(at + 2), h))

    def share(ref, sem):
        send(ref, ref, sem, sibling)

    z_plus, z_minus = device(y, wrap(z + 1), x, c), device(y, wrap(z - 1), x, c)
    x_plus, x_minus = device(y, z, wrap(x + 1), c), device(y, z, wrap(x - 1), c)
    y_plus, y_minus = (wrap(y + 1), col), (wrap(y - 1), col)

    def swapped(g, along=None):
        along = z if along is None else along
        return (y + along) % 2 + 2 * ((y // 2 + along // 2 + g % 2) % 2)

    def group_rows(g):
        return pl.ds(g * group, group)

    def over_z(g):
        part = group_rows(g)
        return pltpu.make_async_remote_copy(
            src_ref=s_ref.at[part],
            dst_ref=middle.at[part],
            send_sem=send_sem.at[SENDS - 1 - g],
            recv_sem=middle_sem.at[g],
            device_id=device(y, swapped(g), x, c),
            device_id_type=MESH,
        )

    def over_y(g, ref):
        part = group_rows(g)
        return pltpu.make_async_remote_copy(
            src_ref=ref.at[part],
            dst_ref=a_buf.at[z, x, c, part],
            send_sem=send_sem.at[SENDS - 1 - GROUPS - g],
            recv_sem=a_sem.at[z, x, c, g, 0],
            device_id=(swapped(g), col),
            device_id_type=MESH,
        )

    def start_over_z(g):
        @pl.when(y != 2 * (g % 2))
        def _():
            over_z(g).start()

    def start_over_y(g):
        still = 2 * (g % 2)

        @pl.when(y != still)
        def _():
            over_z(g).wait_recv()

            @pl.when(z != still)
            def _():
                over_y(g, middle).start()

            @pl.when(z == still)
            def _():
                a_buf[z, x, c, group_rows(g), :] = middle[group_rows(g), :]

        @pl.when(y == still)
        def _():
            @pl.when(z != still)
            def _():
                over_y(g, s_ref).start()

            @pl.when(z == still)
            def _():
                a_buf[z, x, c, group_rows(g), :] = s_ref[group_rows(g), :]

    def end_over_y(g):
        @pl.when(z != 2 * (g % 2))
        def _():
            over_y(g, middle).wait_recv()

    width = lb_ref.shape[1]
    def lb_exchange():
        for step in range(1, N):
            to = wrap(x + step)
            send(
                lb_ref.at[pl.ds(pl.multiple_of(to * lb_rows, lb_rows), lb_rows)],
                lb_buf.at[y, :, pl.ds(pl.multiple_of(x * width, width), width)],
                lx_sem.at[x],
                device(y, z, to, c),
            )

    keep_lb = pltpu.make_async_copy(
        lb_ref.at[pl.ds(pl.multiple_of(x * lb_rows, lb_rows), lb_rows)],
        lb_buf.at[y, :, pl.ds(pl.multiple_of(x * width, width), width)],
        local_sem.at[4],
    )
    keep_lb.start()

    def la_own(p, h=None):
        return la_slot(p, c, h)

    def la_start():
        ring_start(la_own, z, z_plus, z_minus)
        share(*la_slot(z, c))

    def la_forward():
        ring_forward(la_own, z, z_plus, z_minus)

    def la_near():
        ring_near(la_own, z)
        for q in (wrap(z - 1), wrap(z + 1)):
            share(*la_slot(q, c))

    def la_far():
        ring_far(la_own, z)
        share(*la_slot(wrap(z + 2), c))

    def lb_start():
        keep_lb.wait()
        for step in range(1, N):
            source = wrap(x + step)
            arrived(lb_buf.at[y, :, pl.ds(pl.multiple_of(source * width, width), width)], lx_sem.at[source])
        ring_start(lb_slot, y, y_plus, y_minus)

    def lb_forward():
        ring_forward(lb_slot, y, y_plus, y_minus)

    def lb_end():
        ring_near(lb_slot, y)
        ring_far(lb_slot, y)

    z_first = axis_order(c)

    def ring_of(is_z):
        dz, dx = is_z, 1 - is_z
        plus = device(y, wrap(z + dz), wrap(x + dx), c)
        minus = device(y, wrap(z - dz), wrap(x - dx), c)
        return is_z * z + (1 - is_z) * x, plus, minus

    def first(g):
        f = z_first[g]
        return (lambda q, h=None: a_slot(f * q + (1 - f) * z, f * x + (1 - f) * q, g, h)), ring_of(f)

    def second(g, k):
        f = z_first[g]
        p = wrap(f * z + (1 - f) * x + (0, 3, 1, 2)[k])
        return (lambda q, h=None: a_slot(f * p + (1 - f) * q, f * q + (1 - f) * p, g, h)), ring_of(1 - f)

    def second_start(g, k):
        slot, ring = second(g, k)
        ring_start(slot, *ring)
        share(*slot(ring[0]))

    def second_forward(g, k):
        slot, ring = second(g, k)
        ring_forward(slot, *ring)

    def second_near(g, k):
        slot, ring = second(g, k)
        ring_near(slot, ring[0])
        for p in (wrap(ring[0] - 1), wrap(ring[0] + 1)):
            share(*slot(p))

    def second_far(g, k):
        slot, ring = second(g, k)
        ring_far(slot, ring[0])
        share(*slot(wrap(ring[0] + 2)))

    def first_start(g):
        end_over_y(g)
        slot, ring = first(g)
        ring_start(slot, *ring)
        second_start(g, 0)

    def first_forward(g):
        slot, ring = first(g)
        ring_forward(slot, *ring)

    def first_near(g):
        slot, ring = first(g)
        ring_near(slot, ring[0])
        second_start(g, 1)
        second_start(g, 2)

    def first_far(g):
        slot, ring = first(g)
        ring_far(slot, ring[0])
        second_start(g, 3)

    tile = 256
    lk = la_ref.shape[1]

    def ladder():
        for step in range(N):
            arrived(*la_slot(wrap(z + step), 1 - c))

        @pl.loop(0, la_ref.shape[0] // tile)
        def _(m):
            part = pl.ds(pl.multiple_of(m * tile, tile), tile)
            total = jnp.zeros((tile, lb_buf.shape[2]), jnp.float32)
            for zz in range(N):
                for core in range(2):
                    total += jnp.dot(
                        la_buf[zz, core, part, :],
                        lb_buf[zz, pl.ds(core * lk, lk), :],
                        preferred_element_type=jnp.float32,
                    )
            for xx in range(N):
                lc[xx, part, :] = total[:, xx * width : (xx + 1) * width]

        reduce_start(lc, lc_a, lc_sem, x, x_plus, x_minus)

    def ladder_middle():
        reduce_middle(lc, lc_a, lc_b, lc_sem, x, x_plus, x_minus)

    def ladder_end():
        out_ref[...] = reduce_end(lc, lc_b, lc_sem, x)

    def reduce_start(ref, land, sem, at, plus, minus):
        size = ref.shape[1] // 2
        for h, other in ((0, plus), (1, minus)):
            send(ref.at[wrap(at + 2), pl.ds(h * size, size)], land.at[h], sem.at[h], other)

    def reduce_middle(ref, land_a, land_b, sem, at, plus, minus):
        size = ref.shape[1] // 2
        for h, to, other in ((0, wrap(at + 1), plus), (1, wrap(at - 1), minus)):
            arrived(land_a.at[h], sem.at[h])
            part = pl.ds(h * size, size)
            ref[to, part, :] = ref[to, part, :] + land_a[h]
            send(ref.at[to], land_b.at[h], sem.at[2 + h], other)

    def reduce_end(ref, land_b, sem, at):
        for h in range(2):
            arrived(land_b.at[h], sem.at[2 + h])
        return ref[at] + land_b[0] + land_b[1]

    quarter = group // N
    pairs = 8 // GROUPS
    piece = quarter // pairs
    mine = x * 2 + c

    def cycle(g):
        for zz in range(N):
            for xx in range(N):
                arrived(a_buf.at[zz, xx, 1 - c, group_rows(g)], a_sem.at[zz, xx, 1 - c, g, 0])
        total = jnp.zeros((rows // GROUPS * N, cb_ref.shape[1]), jnp.float32)
        for xx in range(N):
            for core in range(2):
                left = jnp.concatenate([a_buf[zz, xx, core, group_rows(g), :] for zz in range(N)], axis=0)
                total += jnp.dot(
                    left,
                    cb_ref[pl.ds((xx * 2 + core) * depth, depth), :],
                    preferred_element_type=jnp.float32,
                )
        for zz in range(N):
            owner = swapped(g, zz)
            for n in range(N):
                cc[g, n, owner] = total[zz * group + n * quarter : zz * group + (n + 1) * quarter]
        reduce_start(cc.at[g], cc_a.at[g], cc_sem.at[g], y, y_plus, y_minus)

    def cycle_middle(g):
        reduce_middle(cc.at[g], cc_a.at[g], cc_b.at[g], cc_sem.at[g], y, y_plus, y_minus)

    def last_copy(g):
        turn = lax.rem(mine, pairs)
        return pltpu.make_async_remote_copy(
            src_ref=outb.at[g, z, pl.ds(pl.multiple_of(turn * piece, piece), piece)],
            dst_ref=fin.at[col],
            send_sem=send_sem.at[SENDS - 1 - 2 * GROUPS - g],
            recv_sem=fin_sem.at[col],
            device_id=(y, z * 8 + g * pairs + turn),
            device_id_type=MESH,
        )

    def cycle_end(g):
        outb[g] = reduce_end(cc.at[g], cc_b.at[g], cc_sem.at[g], y).astype(outb.dtype)
        for zstep in range(N):
            zz = wrap(z + zstep)
            for step in range(pairs):
                if zstep == 0 and step == 0:
                    continue
                turn = lax.rem(mine + step, pairs)
                send(
                    outb.at[g, zz, pl.ds(pl.multiple_of(turn * piece, piece), piece)],
                    fin.at[col],
                    fin_sem.at[col],
                    (y, zz * 8 + g * pairs + turn),
                )

        @pl.when(mine // pairs == g)
        def _():
            fin[col] = outb[g, z, pl.ds(pl.multiple_of(lax.rem(mine, pairs) * piece, piece), piece), :]

        @pl.when(mine // pairs != g)
        def _():
            last_copy(g).start()

    start_over_z(2)
    start_over_z(0)
    start_over_z(1)
    start_over_z(3)
    lb_exchange()
    start_over_y(2)
    start_over_y(0)
    first_start(2)
    start_over_y(1)
    first_start(1)
    lb_start()
    first_start(0)
    first_forward(1)
    la_start()
    second_forward(0, 0)
    first_forward(0)
    first_near(1)
    start_over_y(3)
    second_forward(1, 1)
    second_forward(1, 0)
    la_forward()
    first_forward(2)
    first_far(1)
    first_near(0)
    second_forward(1, 3)
    second_far(0, 0)
    first_far(0)
    lb_forward()
    la_near()
    first_near(2)
    first_start(3)
    second_far(1, 1)
    la_far()
    second_near(0, 0)
    second_near(1, 1)
    second_forward(0, 3)
    second_forward(1, 2)
    second_near(1, 0)
    second_forward(2, 1)
    second_near(1, 3)
    second_near(1, 2)
    second_far(1, 0)
    second_forward(0, 2)
    second_forward(0, 1)
    second_far(1, 3)
    second_near(0, 2)
    first_forward(3)
    lb_end()
    first_near(3)
    ladder()
    second_far(1, 2)
    second_forward(3, 1)
    second_far(0, 3)
    second_forward(3, 0)
    second_near(0, 1)
    second_far(2, 1)
    second_forward(2, 2)
    second_near(0, 3)
    second_forward(3, 2)
    second_near(3, 2)
    second_near(3, 1)
    first_far(2)
    second_far(0, 2)
    second_far(0, 1)
    second_near(3, 0)
    first_far(3)
    copies[3].wait()
    cycle(1)
    second_near(2, 2)
    cycle(0)
    second_forward(3, 3)
    second_far(3, 1)
    second_far(3, 0)
    second_near(3, 3)
    second_forward(2, 0)
    cycle_middle(1)
    second_near(2, 1)
    second_far(2, 2)
    second_far(3, 2)
    second_forward(2, 3)
    second_far(3, 3)
    second_near(2, 0)
    second_near(2, 3)
    cycle_middle(0)
    second_far(2, 0)
    ladder_middle()
    second_far(2, 3)
    cycle(3)
    cycle(2)
    cycle_middle(3)
    cycle_middle(2)
    cycle_end(0)
    cycle_end(1)
    cycle_end(3)
    ladder_end()
    cycle_end(2)

    for step in range(1, 8 * N):
        source = lax.rem(col + step, 8 * N)
        arrived(fin.at[source], fin_sem.at[source])

    @pl.loop(0, 8 * N)
    def _(source):
        for m in range(fin.shape[2] // lanes):
            both = fin[source, :, m * lanes : (m + 1) * lanes].astype(jnp.float32)
            for n, value in enumerate(joined(both[:8], both[8:])):
                at = pl.ds(source * (fin.shape[2] // lanes * 2) + 2 * m + n, 8, stride=pair_count)
                out_ref[at, :] = out_ref[at, :] + value

    for copy in started:
        copy.wait_send()
    for g in range(GROUPS):

        @pl.when(y != 2 * (g % 2))
        def _():
            over_z(g).wait_send()

        @pl.when(z != 2 * (g % 2))
        def _():
            over_y(g, middle).wait_send()

        @pl.when(mine // pairs != g)
        def _():
            last_copy(g).wait_send()


def per_device(
    ladder_amps,
    ladder_integrals,
    cycle_amps,
    cycle_integrals,
    amp_screen,
    integral_screen,
    occupied_i,
    occupied_j,
    virtual_a,
    virtual_b,
):
    tile = virtual_b.shape[0]
    col_count = lax.axis_size("col")
    all_i, local_k, ac = cycle_amps.shape
    rows, depth = all_i * ac // tile, local_k * tile
    nc = cycle_integrals.shape[1]
    lm, lk = ladder_amps.shape
    lrows, ln = ladder_integrals.shape
    quarter = rows // GROUPS // N
    piece = rows // N // 8
    padded_k = -(-local_k // 8) * 8
    f32, bf16 = jnp.float32, jnp.bfloat16
    dma = pltpu.SemaphoreType.DMA
    hbm, smem = pl.BlockSpec(memory_space=pl.ANY), pl.BlockSpec(memory_space=pltpu.SMEM)
    residual = pl.pallas_call(
        functools.partial(kernel, tile * tile),
        out_shape=jax.ShapeDtypeStruct((lm, ln), f32),
        in_specs=[hbm] * 4 + [smem] * 2,
        out_specs=pl.BlockSpec(memory_space=pltpu.VMEM),
        scratch_shapes=[
            pltpu.VMEM((all_i, local_k, ac), bf16),
            pltpu.VMEM((8, all_i * padded_k, ac // 8), f32),
            pltpu.VMEM((rows, depth), bf16),
            pltpu.VMEM((lm, lk), bf16),
            pltpu.VMEM((lrows, ln), bf16),
            pltpu.VMEM(cycle_integrals.shape, bf16),
            pltpu.VMEM((rows, depth), bf16),
            pltpu.VMEM((N, N, 2, rows, depth), bf16),
            pltpu.VMEM((N, 2, lm, lk), bf16),
            pltpu.VMEM((N, lrows // N, N * ln), bf16),
            pltpu.VMEM((N, lm, ln), f32),
            pltpu.VMEM((2, lm // 2, ln), f32),
            pltpu.VMEM((2, lm, ln), f32),
            pltpu.VMEM((GROUPS, N, N, quarter, nc), f32),
            pltpu.VMEM((GROUPS, 2, N // 2, quarter, nc), f32),
            pltpu.VMEM((GROUPS, 2, N, quarter, nc), f32),
            pltpu.VMEM((GROUPS, N, quarter, nc), bf16),
            pltpu.VMEM((col_count, piece, nc), bf16),
            dma((SENDS,)),
            dma((GROUPS,)),
            dma((N, N, 2, GROUPS, 2)),
            dma((N, 2, 2)),
            dma((N,)),
            dma((N, 2)),
            dma((4,)),
            dma((GROUPS, 4)),
            dma((col_count,)),
            dma((5,)),
        ],
        compiler_params=pltpu.CompilerParams(
            collective_id=0, has_side_effects=True, vmem_limit_bytes=56 * 2**20
        ),
        cost_estimate=pl.CostEstimate(
            flops=2 * (N * rows * N * 2 * depth * nc + lm * N * 2 * lk * N * ln),
            bytes_accessed=8 * 2**20,
            transcendentals=0,
        ),
    )(cycle_amps, ladder_amps, ladder_integrals, cycle_integrals, amp_screen, integral_screen)

    virtual_sum = (virtual_a[:, None] + virtual_b[None, :]).reshape(-1)
    occupied_sum = (occupied_i[:, None] + occupied_j[None, :]).reshape(-1)
    denominator = virtual_sum[None, :] - occupied_sum[:, None]
    return residual / denominator


def solution(mesh):
    placed = (
        P("row", "col"),
        P("row", "col"),
        P(None, "col", "row"),
        P("row", "col"),
        P("row", None),
        P("row", "col"),
        P("row"),
        P(),
        P("col"),
        P(),
    )
    return jax.shard_map(
        per_device, mesh=mesh, in_specs=placed, out_specs=P("row", "col"), check_vma=False
    )
```

```python
import functools

import jax
import jax.numpy as jnp
from jax import lax
from jax.experimental import pallas as pl
from jax.experimental.pallas import tpu as pltpu
from jax.sharding import PartitionSpec as P

MESH = pl.DeviceIdType.MESH
N = 4
SENDS = 296
GROUPS = 4


def axis_order(core):
    return (1, 1, core, 0)


def kernel(
    tile_size,
    amps_hbm,
    la_hbm,
    lb_hbm,
    cb_hbm,
    amp_screen,
    integral_screen,
    occupied_i,
    occupied_j,
    virtual_a,
    virtual_b,
    out_ref,
    amps,
    screened,
    gaps,
    ladder_ji,
    s_ref,
    la_ref,
    lb_ref,
    cb_ref,
    middle,
    a_buf,
    la_buf,
    lb_buf,
    lc,
    lc_a,
    lc_b,
    cc,
    cc_a,
    cc_b,
    outb,
    fin,
    send_sem,
    middle_sem,
    a_sem,
    la_sem,
    lx_sem,
    lb_sem,
    lc_sem,
    cc_sem,
    fin_sem,
    local_sem,
):
    y = lax.axis_index("row")
    col = lax.axis_index("col")
    z = col // 8
    x = (col // 2) % N
    c = col % 2

    def wrap(value):
        return lax.rem(value + 2 * N, N)

    def device(yy, zz, xx, core):
        return (yy, zz * 8 + xx * 2 + core)

    sibling = device(y, z, x, 1 - c)
    copies = [
        pltpu.make_async_copy(src, dst, local_sem.at[n])
        for n, (src, dst) in enumerate(((amps_hbm, amps), (la_hbm, la_ref), (lb_hbm, lb_ref), (cb_hbm, cb_ref)))
    ]
    for copy in copies:
        copy.start()

    rows, depth = s_ref.shape
    group = rows // GROUPS
    half = group // 2

    barrier = pltpu.get_barrier_semaphore()

    def greet(other):
        pl.semaphore_signal(barrier, inc=1, device_id=other, device_id_type=MESH)

    for step in range(1, 8 * N):
        greet((y, lax.rem(col + step, 8 * N)))
    for step in range(1, N):
        greet((wrap(y + step), col))

    local_k, blocks, lanes = amps.shape[0], amps.shape[1] // 8, 128
    low = lax.broadcasted_iota(jnp.int32, (1, lanes), 1) < lanes // 2

    def joined(left, right):
        first_halves = jnp.where(low, left, pltpu.roll(right, lanes // 2, 1))
        second_halves = jnp.where(low, pltpu.roll(left, lanes // 2, 1), right)
        return first_halves, second_halves

    pairs = 8 // GROUPS

    def permute(g):
        for t in range(g * pairs, (g + 1) * pairs):
            row = g * group + (t % pairs) * 16
            for m in range(local_k // 2):
                left, right = (
                    amps[k, :, t * lanes : (t + 1) * lanes].astype(jnp.float32) for k in (2 * m, 2 * m + 1)
                )
                both = joined(left, right)
                for ib in range(blocks):
                    s_ref[pl.ds(row + ib * (group // blocks), 16), m * lanes : (m + 1) * lanes] = jnp.concatenate(
                        [value[ib * 8 : (ib + 1) * 8] for value in both], axis=0
                    ).astype(s_ref.dtype)

    copies[0].wait()
    permute(0)

    pair_count = la_ref.shape[0] // amp_screen.shape[1]
    ladder_tile = (col * la_ref.shape[1]) // tile_size

    def screen_amps():
        copies[1].wait()
        for i in range(amp_screen.shape[1]):
            part = pl.ds(i * pair_count, pair_count)
            keep = amp_screen[ladder_tile, i].astype(jnp.float32).astype(la_ref.dtype)
            la_buf[z, c, part, :] = la_ref[part, :] * keep

    def screen_integrals():
        copies[2].wait()
        side = lb_ref.shape[0] // integral_screen.shape[1]
        for p in range(integral_screen.shape[1]):
            part = pl.ds(p * side, side)
            keep = jnp.where(low, integral_screen[0, p], integral_screen[1, p])
            screened[part, :] = lb_ref[part, :] * keep.astype(jnp.float32).astype(lb_ref.dtype)

    def energies():
        lane = lax.broadcasted_iota(jnp.int32, (8, lanes), 1)
        row = lax.broadcasted_iota(jnp.int32, (8, lanes), 0)
        side = virtual_b.shape[0]
        virtual = jnp.zeros((8, lanes), jnp.float32)
        for b in range(side):
            virtual = jnp.where(lax.rem(lane, side) == b, virtual_b[b], virtual)
        virtual = virtual + jnp.where(low, virtual_a[0], virtual_a[1])
        occupied = jnp.zeros((8, lanes), jnp.float32)
        for i in range(occupied_i.shape[0]):
            occupied = jnp.where(row == i, occupied_i[i], occupied)
        for j in range(occupied_j.shape[0]):
            gaps[j] = virtual - (occupied + occupied_j[j])

    pl.semaphore_wait(barrier, 8 * N + N - 2)

    started = []

    def send(src, dst, sem, other):
        copy = pltpu.make_async_remote_copy(
            src_ref=src,
            dst_ref=dst,
            send_sem=send_sem.at[len(started)],
            recv_sem=sem,
            device_id=other,
            device_id_type=MESH,
        )
        copy.start()
        started.append(copy)

    def arrived(dst, sem):
        pltpu.make_async_remote_copy(
            src_ref=dst,
            dst_ref=dst,
            send_sem=send_sem.at[0],
            recv_sem=sem,
            device_id=sibling,
            device_id_type=MESH,
        ).wait_recv()

    def a_slot(zz, xx, g, h=None):
        if h is None:
            return a_buf.at[zz, xx, c, pl.ds(g * group, group)], a_sem.at[zz, xx, c, g, 0]
        return a_buf.at[zz, xx, c, pl.ds(g * group + h * half, half)], a_sem.at[zz, xx, c, g, h]

    la_half = la_ref.shape[0] // 2

    def la_slot(zz, core, h=None):
        if h is None:
            return la_buf.at[zz, core], la_sem.at[zz, core, 0]
        return la_buf.at[zz, core, pl.ds(h * la_half, la_half)], la_sem.at[zz, core, h]

    lb_rows = lb_buf.shape[1]
    lb_half = lb_rows // 2

    def lb_slot(yy, h):
        return lb_buf.at[yy, pl.ds(h * lb_half, lb_half)], lb_sem.at[yy, h]

    def ring_start(slot, at, plus, minus):
        for h, other in ((0, plus), (1, minus), (1, plus), (0, minus)):
            ref, sem = slot(at, h)
            send(ref, ref, sem, other)

    def ring_forward(slot, at, plus, minus):
        for h, source, other in ((0, wrap(at - 1), plus), (1, wrap(at + 1), minus)):
            ref, sem = slot(source, h)
            arrived(ref, sem)
            send(ref, ref, sem, other)

    def ring_near(slot, at):
        arrived(*slot(wrap(at - 1), 1))
        arrived(*slot(wrap(at + 1), 0))

    def ring_far(slot, at):
        for h in range(2):
            arrived(*slot(wrap(at + 2), h))

    def share(ref, sem):
        send(ref, ref, sem, sibling)

    z_plus, z_minus = device(y, wrap(z + 1), x, c), device(y, wrap(z - 1), x, c)
    x_plus, x_minus = device(y, z, wrap(x + 1), c), device(y, z, wrap(x - 1), c)
    y_plus, y_minus = (wrap(y + 1), col), (wrap(y - 1), col)

    def swapped(g, along=None):
        along = z if along is None else along
        return (y + along) % 2 + 2 * ((y // 2 + along // 2 + g % 2) % 2)

    def group_rows(g):
        return pl.ds(g * group, group)

    def over_z(g, h):
        part = pl.ds(g * group + h * half, half)
        return pltpu.make_async_remote_copy(
            src_ref=s_ref.at[part],
            dst_ref=middle.at[part],
            send_sem=send_sem.at[SENDS - 1 - 2 * g - h],
            recv_sem=middle_sem.at[g, h],
            device_id=device(y, swapped(g), x, c),
            device_id_type=MESH,
        )

    def over_y(g, h, ref):
        part = pl.ds(g * group + h * half, half)
        return pltpu.make_async_remote_copy(
            src_ref=ref.at[part],
            dst_ref=a_buf.at[z, x, c, part],
            send_sem=send_sem.at[SENDS - 1 - 2 * GROUPS - 2 * g - h],
            recv_sem=a_sem.at[z, x, c, g, h],
            device_id=(swapped(g), col),
            device_id_type=MESH,
        )

    def start_over_z(g):
        if g > 0:
            permute(g)

        @pl.when(y != 2 * (g % 2))
        def _():
            for h in range(2):
                over_z(g, h).start()

    def start_over_y(g):
        still = 2 * (g % 2)

        def onward(h, ref):
            @pl.when(z != still)
            def _():
                over_y(g, h, ref).start()

            @pl.when(z == still)
            def _():
                part = pl.ds(g * group + h * half, half)
                a_buf[z, x, c, part, :] = ref[part, :]

        @pl.when(y != still)
        def _():
            for h in range(2):
                over_z(g, h).wait_recv()
                onward(h, middle)

        @pl.when(y == still)
        def _():
            for h in range(2):
                onward(h, s_ref)

    def end_over_y(g, h):
        @pl.when(z != 2 * (g % 2))
        def _():
            over_y(g, h, middle).wait_recv()

    width = lb_ref.shape[1]
    def lb_exchange():
        screen_integrals()
        keep_lb.start()
        for step in range(1, N):
            to = wrap(x + step)
            send(
                screened.at[pl.ds(pl.multiple_of(to * lb_rows, lb_rows), lb_rows)],
                lb_buf.at[y, :, pl.ds(pl.multiple_of(x * width, width), width)],
                lx_sem.at[x],
                device(y, z, to, c),
            )

    keep_lb = pltpu.make_async_copy(
        screened.at[pl.ds(pl.multiple_of(x * lb_rows, lb_rows), lb_rows)],
        lb_buf.at[y, :, pl.ds(pl.multiple_of(x * width, width), width)],
        local_sem.at[4],
    )

    def la_own(p, h=None):
        return la_slot(p, c, h)

    def la_start():
        screen_amps()
        ring_start(la_own, z, z_plus, z_minus)
        share(*la_slot(z, c))

    def la_forward():
        ring_forward(la_own, z, z_plus, z_minus)

    def la_near():
        ring_near(la_own, z)
        for q in (wrap(z - 1), wrap(z + 1)):
            share(*la_slot(q, c))

    def la_far():
        ring_far(la_own, z)
        share(*la_slot(wrap(z + 2), c))

    def lb_start():
        keep_lb.wait()
        for step in range(1, N):
            source = wrap(x + step)
            arrived(lb_buf.at[y, :, pl.ds(pl.multiple_of(source * width, width), width)], lx_sem.at[source])
        ring_start(lb_slot, y, y_plus, y_minus)

    def lb_forward():
        ring_forward(lb_slot, y, y_plus, y_minus)

    def lb_end():
        ring_near(lb_slot, y)
        ring_far(lb_slot, y)

    z_first = axis_order(c)

    def ring_of(is_z):
        dz, dx = is_z, 1 - is_z
        plus = device(y, wrap(z + dz), wrap(x + dx), c)
        minus = device(y, wrap(z - dz), wrap(x - dx), c)
        return is_z * z + (1 - is_z) * x, plus, minus

    def first(g):
        f = z_first[g]
        return (lambda q, h=None: a_slot(f * q + (1 - f) * z, f * x + (1 - f) * q, g, h)), ring_of(f)

    def second(g, k):
        f = z_first[g]
        p = wrap(f * z + (1 - f) * x + (0, 3, 1, 2)[k])
        return (lambda q, h=None: a_slot(f * p + (1 - f) * q, f * q + (1 - f) * p, g, h)), ring_of(1 - f)

    def second_start(g, k):
        slot, ring = second(g, k)
        ring_start(slot, *ring)
        share(*slot(ring[0]))

    def second_forward(g, k):
        slot, ring = second(g, k)
        ring_forward(slot, *ring)

    def second_near(g, k):
        slot, ring = second(g, k)
        ring_near(slot, ring[0])
        for p in (wrap(ring[0] - 1), wrap(ring[0] + 1)):
            share(*slot(p))

    def second_far(g, k):
        slot, ring = second(g, k)
        ring_far(slot, ring[0])
        share(*slot(wrap(ring[0] + 2)))

    def first_start(g):
        near = first(g), second(g, 0)
        for h in range(2):
            end_over_y(g, h)
            for slot, (at, plus, minus) in near:
                ref, sem = slot(at, h)
                for other in (plus, minus) if h == 0 else (minus, plus):
                    send(ref, ref, sem, other)
        slot, ring = near[1]
        share(*slot(ring[0]))

    def first_forward(g):
        slot, ring = first(g)
        ring_forward(slot, *ring)

    def first_near(g):
        slot, ring = first(g)
        ring_near(slot, ring[0])
        second_start(g, 1)
        second_start(g, 2)

    def first_far(g):
        slot, ring = first(g)
        ring_far(slot, ring[0])
        second_start(g, 3)

    tile = 256
    lk = la_ref.shape[1]

    def ladder():
        for step in range(N):
            arrived(*la_slot(wrap(z + step), 1 - c))

        @pl.loop(0, la_ref.shape[0] // tile)
        def _(m):
            part = pl.ds(pl.multiple_of(m * tile, tile), tile)
            total = jnp.zeros((tile, lb_buf.shape[2]), jnp.float32)
            for zz in range(N):
                for core in range(2):
                    total += jnp.dot(
                        la_buf[zz, core, part, :],
                        lb_buf[zz, pl.ds(core * lk, lk), :],
                        preferred_element_type=jnp.float32,
                    )
            for xx in range(N):
                lc[xx, part, :] = total[:, xx * width : (xx + 1) * width]

        reduce_start(lc, lc_a, lc_sem, x, x_plus, x_minus)

    def ladder_middle():
        reduce_middle(lc, lc_a, lc_b, lc_sem, x, x_plus, x_minus)

    def ladder_end():
        out_ref[...] = reduce_end(lc, lc_b, lc_sem, x)
        for j in range(pair_count):
            ladder_ji[j] = out_ref[pl.ds(j, 8, stride=pair_count), :]

    def reduce_start(ref, land, sem, at, plus, minus):
        size = ref.shape[1] // 2
        for h, other in ((0, plus), (1, minus)):
            send(ref.at[wrap(at + 2), pl.ds(h * size, size)], land.at[h], sem.at[h], other)

    def reduce_middle(ref, land_a, land_b, sem, at, plus, minus):
        size = ref.shape[1] // 2
        for h, to, other in ((0, wrap(at + 1), plus), (1, wrap(at - 1), minus)):
            arrived(land_a.at[h], sem.at[h])
            part = pl.ds(h * size, size)
            ref[to, part, :] = ref[to, part, :] + land_a[h]
            send(ref.at[to], land_b.at[h], sem.at[2 + h], other)

    def reduce_end(ref, land_b, sem, at):
        for h in range(2):
            arrived(land_b.at[h], sem.at[2 + h])
        return ref[at] + land_b[0] + land_b[1]

    quarter = group // N
    piece = quarter // pairs
    mine = x * 2 + c

    def cycle(g):
        for zz in range(N):
            for xx in range(N):
                arrived(a_buf.at[zz, xx, 1 - c, group_rows(g)], a_sem.at[zz, xx, 1 - c, g, 0])
        total = jnp.zeros((rows // GROUPS * N, cb_ref.shape[1]), jnp.float32)
        for xx in range(N):
            for core in range(2):
                left = jnp.concatenate([a_buf[zz, xx, core, group_rows(g), :] for zz in range(N)], axis=0)
                total += jnp.dot(
                    left,
                    cb_ref[pl.ds((xx * 2 + core) * depth, depth), :],
                    preferred_element_type=jnp.float32,
                )
        for zz in range(N):
            owner = swapped(g, zz)
            for n in range(N):
                cc[g, n, owner] = total[zz * group + n * quarter : zz * group + (n + 1) * quarter]
        reduce_start(cc.at[g], cc_a.at[g], cc_sem.at[g], y, y_plus, y_minus)

    def cycle_middle(g):
        reduce_middle(cc.at[g], cc_a.at[g], cc_b.at[g], cc_sem.at[g], y, y_plus, y_minus)

    def last_copy(g):
        turn = lax.rem(mine, pairs)
        return pltpu.make_async_remote_copy(
            src_ref=outb.at[g, z, pl.ds(pl.multiple_of(turn * piece, piece), piece)],
            dst_ref=fin.at[col],
            send_sem=send_sem.at[SENDS - 1 - 4 * GROUPS - g],
            recv_sem=fin_sem.at[col],
            device_id=(y, z * 8 + g * pairs + turn),
            device_id_type=MESH,
        )

    def cycle_end(g):
        outb[g] = reduce_end(cc.at[g], cc_b.at[g], cc_sem.at[g], y).astype(outb.dtype)
        for zstep in range(N):
            zz = wrap(z + zstep)
            for step in range(pairs):
                if zstep == 0 and step == 0:
                    continue
                turn = lax.rem(mine + step, pairs)
                send(
                    outb.at[g, zz, pl.ds(pl.multiple_of(turn * piece, piece), piece)],
                    fin.at[col],
                    fin_sem.at[col],
                    (y, zz * 8 + g * pairs + turn),
                )

        @pl.when(mine // pairs == g)
        def _():
            fin[col] = outb[g, z, pl.ds(pl.multiple_of(lax.rem(mine, pairs) * piece, piece), piece), :]

        @pl.when(mine // pairs != g)
        def _():
            last_copy(g).start()

    start_over_z(1)
    start_over_z(2)
    start_over_z(3)
    lb_exchange()
    start_over_y(1)
    start_over_z(0)
    start_over_y(2)
    first_start(1)
    energies()
    start_over_y(0)
    first_start(2)
    first_start(0)
    lb_start()
    first_forward(2)
    second_forward(1, 0)
    first_near(2)
    start_over_y(3)
    first_far(2)
    first_forward(0)
    first_near(0)
    la_start()
    lb_forward()
    second_far(1, 0)
    second_forward(0, 2)
    second_forward(0, 1)
    first_forward(1)
    second_forward(2, 3)
    first_far(0)
    second_forward(0, 0)
    la_forward()
    second_forward(0, 3)
    second_near(0, 0)
    lb_end()
    second_forward(2, 2)
    second_near(0, 1)
    first_start(3)
    second_far(2, 3)
    first_near(1)
    second_near(0, 3)
    second_forward(2, 1)
    second_far(0, 1)
    second_near(2, 2)
    second_far(0, 2)
    second_far(0, 3)
    second_far(0, 0)
    second_near(2, 3)
    second_near(0, 2)
    second_near(1, 0)
    first_far(1)
    first_forward(3)
    la_near()
    second_forward(2, 0)
    copies[3].wait()
    cycle(0)
    second_forward(1, 1)
    second_near(2, 0)
    la_far()
    second_near(1, 1)
    second_forward(3, 0)
    second_far(2, 2)
    second_near(3, 0)
    second_forward(1, 2)
    second_near(2, 1)
    cycle_middle(0)
    first_near(3)
    second_near(1, 2)
    second_forward(1, 3)
    first_far(3)
    second_far(2, 1)
    second_near(1, 3)
    second_far(2, 0)
    ladder()
    cycle(2)
    second_far(1, 1)
    second_far(1, 2)
    second_forward(3, 2)
    second_forward(3, 1)
    second_far(1, 3)
    second_forward(3, 3)
    second_far(3, 0)
    second_near(3, 1)
    second_near(3, 2)
    second_near(3, 3)
    cycle_middle(2)
    ladder_middle()
    second_far(3, 1)
    second_far(3, 2)
    second_far(3, 3)
    cycle(1)
    cycle(3)
    cycle_middle(1)
    cycle_end(0)
    cycle_end(2)
    cycle_middle(3)
    cycle_end(1)
    ladder_end()
    cycle_end(3)

    for step in range(1, 8 * N):
        source = lax.rem(col + step, 8 * N)
        arrived(fin.at[source], fin_sem.at[source])

    @pl.loop(0, 8 * N, unroll=4)
    def _(source):
        for m in range(fin.shape[2] // lanes):
            both = fin[source, :, m * lanes : (m + 1) * lanes].astype(jnp.float32)
            for n, value in enumerate(joined(both[:8], both[8:])):
                j = source * (fin.shape[2] // lanes * 2) + 2 * m + n
                out_ref[pl.ds(j, 8, stride=pair_count), :] = (ladder_ji[j] + value) / gaps[j]

    for copy in started:
        copy.wait_send()
    for g in range(GROUPS):

        @pl.when(y != 2 * (g % 2))
        def _():
            for h in range(2):
                over_z(g, h).wait_send()

        @pl.when(z != 2 * (g % 2))
        def _():
            for h in range(2):
                over_y(g, h, middle).wait_send()

        @pl.when(mine // pairs != g)
        def _():
            last_copy(g).wait_send()


def per_device(
    ladder_amps,
    ladder_integrals,
    cycle_amps,
    cycle_integrals,
    amp_screen,
    integral_screen,
    occupied_i,
    occupied_j,
    virtual_a,
    virtual_b,
):
    tile = virtual_b.shape[0]
    col_count = lax.axis_size("col")
    all_i, local_k, ac = cycle_amps.shape
    rows, depth = all_i * ac // tile, local_k * tile
    nc = cycle_integrals.shape[1]
    lm, lk = ladder_amps.shape
    lrows, ln = ladder_integrals.shape
    quarter = rows // GROUPS // N
    piece = rows // N // 8
    f32, bf16 = jnp.float32, jnp.bfloat16
    dma = pltpu.SemaphoreType.DMA
    hbm, smem = pl.BlockSpec(memory_space=pl.ANY), pl.BlockSpec(memory_space=pltpu.SMEM)
    return pl.pallas_call(
        functools.partial(kernel, tile * tile),
        out_shape=jax.ShapeDtypeStruct((lm, ln), f32),
        in_specs=[hbm] * 4 + [smem] * 6,
        out_specs=pl.BlockSpec(memory_space=pltpu.VMEM),
        scratch_shapes=[
            pltpu.VMEM((local_k, all_i, ac), bf16),
            pltpu.VMEM((lrows, ln), bf16),
            pltpu.VMEM((occupied_j.shape[0], occupied_i.shape[0], ln), f32),
            pltpu.VMEM((occupied_j.shape[0], occupied_i.shape[0], ln), f32),
            pltpu.VMEM((rows, depth), bf16),
            pltpu.VMEM((lm, lk), bf16),
            pltpu.VMEM((lrows, ln), bf16),
            pltpu.VMEM(cycle_integrals.shape, bf16),
            pltpu.VMEM((rows, depth), bf16),
            pltpu.VMEM((N, N, 2, rows, depth), bf16),
            pltpu.VMEM((N, 2, lm, lk), bf16),
            pltpu.VMEM((N, lrows // N, N * ln), bf16),
            pltpu.VMEM((N, lm, ln), f32),
            pltpu.VMEM((2, lm // 2, ln), f32),
            pltpu.VMEM((2, lm, ln), f32),
            pltpu.VMEM((GROUPS, N, N, quarter, nc), f32),
            pltpu.VMEM((GROUPS, 2, N // 2, quarter, nc), f32),
            pltpu.VMEM((GROUPS, 2, N, quarter, nc), f32),
            pltpu.VMEM((GROUPS, N, quarter, nc), bf16),
            pltpu.VMEM((col_count, piece, nc), bf16),
            dma((SENDS,)),
            dma((GROUPS, 2)),
            dma((N, N, 2, GROUPS, 2)),
            dma((N, 2, 2)),
            dma((N,)),
            dma((N, 2)),
            dma((4,)),
            dma((GROUPS, 4)),
            dma((col_count,)),
            dma((5,)),
        ],
        compiler_params=pltpu.CompilerParams(
            collective_id=0, has_side_effects=True, vmem_limit_bytes=56 * 2**20
        ),
        cost_estimate=pl.CostEstimate(
            flops=2 * (N * rows * N * 2 * depth * nc + lm * N * 2 * lk * N * ln),
            bytes_accessed=8 * 2**20,
            transcendentals=0,
        ),
    )(
        cycle_amps.transpose(1, 0, 2),
        ladder_amps,
        ladder_integrals,
        cycle_integrals,
        amp_screen.T,
        integral_screen.T,
        occupied_i,
        occupied_j,
        virtual_a,
        virtual_b,
    )


def solution(mesh):
    placed = (
        P("row", "col"),
        P("row", "col"),
        P(None, "col", "row"),
        P("row", "col"),
        P("row", None),
        P("row", "col"),
        P("row"),
        P(),
        P("col"),
        P(),
    )
    return jax.shard_map(
        per_device, mesh=mesh, in_specs=placed, out_specs=P("row", "col"), check_vma=False
    )
```

```python
import functools

import jax
import jax.numpy as jnp
from jax import lax
from jax.experimental import pallas as pl
from jax.experimental.pallas import tpu as pltpu
from jax.sharding import PartitionSpec as P

MESH = pl.DeviceIdType.MESH
N = 4
SENDS = 304
GROUPS = 4
LAST = GROUPS - 1


def axis_order(core):
    return (core, 1, 0, 1)


def kernel(
    tile_size,
    amps_hbm,
    la_hbm,
    lb_hbm,
    cb_hbm,
    amp_screen,
    integral_screen,
    occupied_i,
    occupied_j,
    virtual_a,
    virtual_b,
    out_ref,
    amps,
    screened,
    gaps,
    ladder_ji,
    s_ref,
    la_ref,
    lb_ref,
    cb_ref,
    middle,
    a_buf,
    la_buf,
    lb_buf,
    lc,
    lc_a,
    lc_b,
    cc,
    cc_a,
    cc_b,
    block_c,
    block_a,
    block_b,
    outb,
    fin,
    send_sem,
    middle_sem,
    a_sem,
    la_sem,
    lx_sem,
    lb_sem,
    lc_sem,
    cc_sem,
    block_sem,
    fin_sem,
    local_sem,
):
    y = lax.axis_index("row")
    col = lax.axis_index("col")
    z = col // 8
    x = (col // 2) % N
    c = col % 2

    def wrap(value):
        return lax.rem(value + 2 * N, N)

    def device(yy, zz, xx, core):
        return (yy, zz * 8 + xx * 2 + core)

    sibling = device(y, z, x, 1 - c)
    copies = [
        pltpu.make_async_copy(src, dst, local_sem.at[n])
        for n, (src, dst) in enumerate(((amps_hbm, amps), (la_hbm, la_ref), (lb_hbm, lb_ref), (cb_hbm, cb_ref)))
    ]
    for copy in copies:
        copy.start()

    rows, depth = s_ref.shape
    group = rows // GROUPS
    half = group // 2

    barrier = pltpu.get_barrier_semaphore()

    def greet(other):
        pl.semaphore_signal(barrier, inc=1, device_id=other, device_id_type=MESH)

    for step in range(1, 8 * N):
        greet((y, lax.rem(col + step, 8 * N)))
    for step in range(1, N):
        greet((wrap(y + step), col))

    local_k, blocks, lanes = amps.shape[0], amps.shape[1] // 8, 128
    low = lax.broadcasted_iota(jnp.int32, (1, lanes), 1) < lanes // 2

    def joined(left, right):
        first_halves = jnp.where(low, left, pltpu.roll(right, lanes // 2, 1))
        second_halves = jnp.where(low, pltpu.roll(left, lanes // 2, 1), right)
        return first_halves, second_halves

    pairs = 8 // GROUPS

    def permute(g):
        for t in range(g * pairs, (g + 1) * pairs):
            row = g * group + (t % pairs) * 16
            for m in range(local_k // 2):
                left, right = (
                    amps[k, :, t * lanes : (t + 1) * lanes].astype(jnp.float32) for k in (2 * m, 2 * m + 1)
                )
                both = joined(left, right)
                for ib in range(blocks):
                    s_ref[pl.ds(row + ib * (group // blocks), 16), m * lanes : (m + 1) * lanes] = jnp.concatenate(
                        [value[ib * 8 : (ib + 1) * 8] for value in both], axis=0
                    ).astype(s_ref.dtype)

    copies[0].wait()
    permute(0)

    pair_count = la_ref.shape[0] // amp_screen.shape[1]
    ladder_tile = (col * la_ref.shape[1]) // tile_size

    def screen_amps():
        copies[1].wait()
        for i in range(amp_screen.shape[1]):
            part = pl.ds(i * pair_count, pair_count)
            keep = amp_screen[ladder_tile, i].astype(jnp.float32).astype(la_ref.dtype)
            la_buf[z, c, part, :] = la_ref[part, :] * keep

    def screen_integrals():
        copies[2].wait()
        side = lb_ref.shape[0] // integral_screen.shape[1]
        for p in range(integral_screen.shape[1]):
            part = pl.ds(p * side, side)
            keep = jnp.where(low, integral_screen[0, p], integral_screen[1, p])
            screened[part, :] = lb_ref[part, :] * keep.astype(jnp.float32).astype(lb_ref.dtype)

    def energies():
        lane = lax.broadcasted_iota(jnp.int32, (8, lanes), 1)
        row = lax.broadcasted_iota(jnp.int32, (8, lanes), 0)
        side = virtual_b.shape[0]
        virtual = jnp.zeros((8, lanes), jnp.float32)
        for b in range(side):
            virtual = jnp.where(lax.rem(lane, side) == b, virtual_b[b], virtual)
        virtual = virtual + jnp.where(low, virtual_a[0], virtual_a[1])
        occupied = jnp.zeros((8, lanes), jnp.float32)
        for i in range(occupied_i.shape[0]):
            occupied = jnp.where(row == i, occupied_i[i], occupied)
        for j in range(occupied_j.shape[0]):
            gaps[j] = virtual - (occupied + occupied_j[j])

    pl.semaphore_wait(barrier, 8 * N + N - 2)

    started = []

    def send(src, dst, sem, other):
        copy = pltpu.make_async_remote_copy(
            src_ref=src,
            dst_ref=dst,
            send_sem=send_sem.at[len(started)],
            recv_sem=sem,
            device_id=other,
            device_id_type=MESH,
        )
        copy.start()
        started.append(copy)

    def arrived(dst, sem):
        pltpu.make_async_remote_copy(
            src_ref=dst,
            dst_ref=dst,
            send_sem=send_sem.at[0],
            recv_sem=sem,
            device_id=sibling,
            device_id_type=MESH,
        ).wait_recv()

    def a_slot(zz, xx, g, h=None):
        if h is None:
            return a_buf.at[zz, xx, c, pl.ds(g * group, group)], a_sem.at[zz, xx, c, g, 0]
        return a_buf.at[zz, xx, c, pl.ds(g * group + h * half, half)], a_sem.at[zz, xx, c, g, h]

    la_half = la_ref.shape[0] // 2

    def la_slot(zz, core, h=None):
        if h is None:
            return la_buf.at[zz, core], la_sem.at[zz, core, 0]
        return la_buf.at[zz, core, pl.ds(h * la_half, la_half)], la_sem.at[zz, core, h]

    lb_rows = lb_buf.shape[1]
    lb_half = lb_rows // 2

    def lb_slot(yy, h):
        return lb_buf.at[yy, pl.ds(h * lb_half, lb_half)], lb_sem.at[yy, h]

    def ring_start(slot, at, plus, minus):
        for h, other in ((0, plus), (1, minus), (1, plus), (0, minus)):
            ref, sem = slot(at, h)
            send(ref, ref, sem, other)

    def ring_forward(slot, at, plus, minus):
        for h, source, other in ((0, wrap(at - 1), plus), (1, wrap(at + 1), minus)):
            ref, sem = slot(source, h)
            arrived(ref, sem)
            send(ref, ref, sem, other)

    def ring_near(slot, at):
        arrived(*slot(wrap(at - 1), 1))
        arrived(*slot(wrap(at + 1), 0))

    def ring_far(slot, at):
        for h in range(2):
            arrived(*slot(wrap(at + 2), h))

    def share(ref, sem):
        send(ref, ref, sem, sibling)

    z_plus, z_minus = device(y, wrap(z + 1), x, c), device(y, wrap(z - 1), x, c)
    x_plus, x_minus = device(y, z, wrap(x + 1), c), device(y, z, wrap(x - 1), c)
    y_plus, y_minus = (wrap(y + 1), col), (wrap(y - 1), col)

    def swapped(g, along=None):
        along = z if along is None else along
        return (y + along) % 2 + 2 * ((y // 2 + along // 2 + g % 2) % 2)

    def group_rows(g):
        return pl.ds(g * group, group)

    def over_z(g, h):
        part = pl.ds(g * group + h * half, half)
        return pltpu.make_async_remote_copy(
            src_ref=s_ref.at[part],
            dst_ref=middle.at[part],
            send_sem=send_sem.at[SENDS - 1 - 2 * g - h],
            recv_sem=middle_sem.at[g, h],
            device_id=device(y, swapped(g), x, c),
            device_id_type=MESH,
        )

    def over_y(g, h, ref):
        part = pl.ds(g * group + h * half, half)
        return pltpu.make_async_remote_copy(
            src_ref=ref.at[part],
            dst_ref=a_buf.at[z, x, c, part],
            send_sem=send_sem.at[SENDS - 1 - 2 * GROUPS - 2 * g - h],
            recv_sem=a_sem.at[z, x, c, g, h],
            device_id=(swapped(g), col),
            device_id_type=MESH,
        )

    def start_over_z(g):
        if g > 0:
            permute(g)

        @pl.when(y != 2 * (g % 2))
        def _():
            for h in range(2):
                over_z(g, h).start()

    def start_over_y(g):
        still = 2 * (g % 2)

        def onward(h, ref):
            @pl.when(z != still)
            def _():
                over_y(g, h, ref).start()

            @pl.when(z == still)
            def _():
                part = pl.ds(g * group + h * half, half)
                a_buf[z, x, c, part, :] = ref[part, :]

        @pl.when(y != still)
        def _():
            for h in range(2):
                over_z(g, h).wait_recv()
                onward(h, middle)

        @pl.when(y == still)
        def _():
            for h in range(2):
                onward(h, s_ref)

    def end_over_y(g, h):
        @pl.when(z != 2 * (g % 2))
        def _():
            over_y(g, h, middle).wait_recv()

    width = lb_ref.shape[1]
    def lb_exchange():
        screen_integrals()
        keep_lb.start()
        for step in range(1, N):
            to = wrap(x + step)
            send(
                screened.at[pl.ds(pl.multiple_of(to * lb_rows, lb_rows), lb_rows)],
                lb_buf.at[y, :, pl.ds(pl.multiple_of(x * width, width), width)],
                lx_sem.at[x],
                device(y, z, to, c),
            )

    keep_lb = pltpu.make_async_copy(
        screened.at[pl.ds(pl.multiple_of(x * lb_rows, lb_rows), lb_rows)],
        lb_buf.at[y, :, pl.ds(pl.multiple_of(x * width, width), width)],
        local_sem.at[4],
    )

    def la_own(p, h=None):
        return la_slot(p, c, h)

    def la_start():
        screen_amps()
        ring_start(la_own, z, z_plus, z_minus)
        share(*la_slot(z, c))

    def la_forward():
        ring_forward(la_own, z, z_plus, z_minus)

    def la_near():
        ring_near(la_own, z)
        for q in (wrap(z - 1), wrap(z + 1)):
            share(*la_slot(q, c))

    def la_far():
        ring_far(la_own, z)
        share(*la_slot(wrap(z + 2), c))

    def lb_start():
        keep_lb.wait()
        for step in range(1, N):
            source = wrap(x + step)
            arrived(lb_buf.at[y, :, pl.ds(pl.multiple_of(source * width, width), width)], lx_sem.at[source])
        ring_start(lb_slot, y, y_plus, y_minus)

    def lb_forward():
        ring_forward(lb_slot, y, y_plus, y_minus)

    def lb_end():
        ring_near(lb_slot, y)
        ring_far(lb_slot, y)

    z_first = axis_order(c)

    def ring_of(is_z):
        dz, dx = is_z, 1 - is_z
        plus = device(y, wrap(z + dz), wrap(x + dx), c)
        minus = device(y, wrap(z - dz), wrap(x - dx), c)
        return is_z * z + (1 - is_z) * x, plus, minus

    def first(g):
        f = z_first[g]
        return (lambda q, h=None: a_slot(f * q + (1 - f) * z, f * x + (1 - f) * q, g, h)), ring_of(f)

    def second(g, k):
        f = z_first[g]
        p = wrap(f * z + (1 - f) * x + (0, 3, 1, 2)[k]) if g < LAST else swapped(g, k)
        return (lambda q, h=None: a_slot(f * p + (1 - f) * q, f * q + (1 - f) * p, g, h)), ring_of(1 - f)

    def second_start(g, k):
        slot, ring = second(g, k)
        ring_start(slot, *ring)
        share(*slot(ring[0]))

    def second_forward(g, k):
        slot, ring = second(g, k)
        ring_forward(slot, *ring)

    def second_near(g, k):
        slot, ring = second(g, k)
        ring_near(slot, ring[0])
        for p in (wrap(ring[0] - 1), wrap(ring[0] + 1)):
            share(*slot(p))

    def second_far(g, k):
        slot, ring = second(g, k)
        ring_far(slot, ring[0])
        share(*slot(wrap(ring[0] + 2)))

    def first_start(g):
        near = (first(g), second(g, 0)) if g < LAST else (first(g),)
        for h in range(2):
            end_over_y(g, h)
            for slot, (at, plus, minus) in near:
                ref, sem = slot(at, h)
                for other in (plus, minus) if h == 0 else (minus, plus):
                    send(ref, ref, sem, other)
        if g < LAST:
            slot, ring = near[1]
            share(*slot(ring[0]))

    def first_forward(g):
        slot, ring = first(g)
        ring_forward(slot, *ring)

    def first_near(g):
        slot, ring = first(g)
        ring_near(slot, ring[0])
        if g < LAST:
            second_start(g, 1)
            second_start(g, 2)

    def first_far(g):
        slot, ring = first(g)
        ring_far(slot, ring[0])
        if g < LAST:
            second_start(g, 3)

    tile = 256
    lk = la_ref.shape[1]

    def ladder():
        for step in range(N):
            arrived(*la_slot(wrap(z + step), 1 - c))

        @pl.loop(0, la_ref.shape[0] // tile)
        def _(m):
            part = pl.ds(pl.multiple_of(m * tile, tile), tile)
            total = jnp.zeros((tile, lb_buf.shape[2]), jnp.float32)
            for zz in range(N):
                for core in range(2):
                    total += jnp.dot(
                        la_buf[zz, core, part, :],
                        lb_buf[zz, pl.ds(core * lk, lk), :],
                        preferred_element_type=jnp.float32,
                    )
            for xx in range(N):
                lc[xx, part, :] = total[:, xx * width : (xx + 1) * width]

        reduce_start(lc, lc_a, lc_sem, x, x_plus, x_minus)

    def ladder_middle():
        reduce_middle(lc, lc_a, lc_b, lc_sem, x, x_plus, x_minus)

    def ladder_end():
        out_ref[...] = reduce_end(lc, lc_b, lc_sem, x)
        for j in range(pair_count):
            ladder_ji[j] = out_ref[pl.ds(j, 8, stride=pair_count), :]

    def reduce_start(ref, land, sem, at, plus, minus):
        size = ref.shape[1] // 2
        for h, other in ((0, plus), (1, minus)):
            send(ref.at[wrap(at + 2), pl.ds(h * size, size)], land.at[h], sem.at[h], other)

    def reduce_middle(ref, land_a, land_b, sem, at, plus, minus):
        size = ref.shape[1] // 2
        for h, to, other in ((0, wrap(at + 1), plus), (1, wrap(at - 1), minus)):
            arrived(land_a.at[h], sem.at[h])
            part = pl.ds(h * size, size)
            ref[to, part, :] = ref[to, part, :] + land_a[h]
            send(ref.at[to], land_b.at[h], sem.at[2 + h], other)

    def reduce_end(ref, land_b, sem, at):
        for h in range(2):
            arrived(land_b.at[h], sem.at[2 + h])
        return ref[at] + land_b[0] + land_b[1]

    quarter = group // N
    piece = quarter // pairs
    mine = x * 2 + c

    def cycle(g):
        for zz in range(N):
            for xx in range(N):
                arrived(a_buf.at[zz, xx, 1 - c, group_rows(g)], a_sem.at[zz, xx, 1 - c, g, 0])
        total = jnp.zeros((rows // GROUPS * N, cb_ref.shape[1]), jnp.float32)
        for xx in range(N):
            for core in range(2):
                left = jnp.concatenate([a_buf[zz, xx, core, group_rows(g), :] for zz in range(N)], axis=0)
                total += jnp.dot(
                    left,
                    cb_ref[pl.ds((xx * 2 + core) * depth, depth), :],
                    preferred_element_type=jnp.float32,
                )
        for zz in range(N):
            owner = swapped(g, zz)
            for n in range(N):
                cc[g, n, owner] = total[zz * group + n * quarter : zz * group + (n + 1) * quarter]
        reduce_start(cc.at[g], cc_a.at[g], cc_sem.at[g], y, y_plus, y_minus)

    def cycle_middle(g):
        reduce_middle(cc.at[g], cc_a.at[g], cc_b.at[g], cc_sem.at[g], y, y_plus, y_minus)

    def last_copy(g):
        turn = lax.rem(mine, pairs)
        return pltpu.make_async_remote_copy(
            src_ref=outb.at[g, z, pl.ds(pl.multiple_of(turn * piece, piece), piece)],
            dst_ref=fin.at[col],
            send_sem=send_sem.at[SENDS - 1 - 4 * GROUPS - g],
            recv_sem=fin_sem.at[col],
            device_id=(y, z * 8 + g * pairs + turn),
            device_id_type=MESH,
        )

    def cycle_end(g):
        outb[g] = reduce_end(cc.at[g], cc_b.at[g], cc_sem.at[g], y).astype(outb.dtype)
        for zstep in range(N):
            zz = wrap(z + zstep)
            for step in range(pairs):
                if zstep == 0 and step == 0:
                    continue
                turn = lax.rem(mine + step, pairs)
                send(
                    outb.at[g, zz, pl.ds(pl.multiple_of(turn * piece, piece), piece)],
                    fin.at[col],
                    fin_sem.at[col],
                    (y, zz * 8 + g * pairs + turn),
                )

        @pl.when(mine // pairs == g)
        def _():
            fin[col] = outb[g, z, pl.ds(pl.multiple_of(lax.rem(mine, pairs) * piece, piece), piece), :]

        @pl.when(mine // pairs != g)
        def _():
            last_copy(g).start()

    def block(k):
        zz = swapped(LAST, k)
        for xx in range(N):
            arrived(a_buf.at[zz, xx, 1 - c, group_rows(LAST)], a_sem.at[zz, xx, 1 - c, LAST, 0])
        total = jnp.zeros((group, cb_ref.shape[1]), jnp.float32)
        for xx in range(N):
            for core in range(2):
                total += jnp.dot(
                    a_buf[zz, xx, core, group_rows(LAST), :],
                    cb_ref[pl.ds((xx * 2 + core) * depth, depth), :],
                    preferred_element_type=jnp.float32,
                )
        for n in range(N):
            block_c[k, n] = total[n * quarter : (n + 1) * quarter]
        reduce_start(block_c.at[k], block_a.at[k], block_sem.at[k], y, y_plus, y_minus)

    def block_middle(k):
        reduce_middle(block_c.at[k], block_a.at[k], block_b.at[k], block_sem.at[k], y, y_plus, y_minus)

    def block_copy(k, n):
        other = k * 8 + LAST * pairs + n
        copy = pltpu.make_async_remote_copy(
            src_ref=outb.at[LAST, k, pl.ds(n * piece, piece)],
            dst_ref=fin.at[col],
            send_sem=send_sem.at[SENDS - 1 - 5 * GROUPS - pairs * k - n],
            recv_sem=fin_sem.at[col],
            device_id=(y, other),
            device_id_type=MESH,
        )
        return other, copy

    def block_end(k):
        outb[LAST, k] = reduce_end(block_c.at[k], block_b.at[k], block_sem.at[k], y).astype(outb.dtype)
        for n in range(pairs):
            other, copy = block_copy(k, n)

            @pl.when(col == other)
            def _():
                fin[col] = outb[LAST, k, pl.ds(n * piece, piece), :]

            @pl.when(col != other)
            def _():
                copy.start()

    start_over_z(0)
    lb_exchange()
    start_over_z(1)
    start_over_z(2)
    start_over_y(0)
    start_over_z(3)
    start_over_y(1)
    first_start(0)
    energies()
    first_start(1)
    start_over_y(3)
    first_forward(0)
    second_forward(1, 0)
    first_start(3)
    first_forward(1)
    first_near(1)
    start_over_y(2)
    first_forward(3)
    la_start()
    second_near(1, 0)
    second_forward(1, 1)
    first_far(1)
    second_forward(1, 3)
    second_near(1, 1)
    lb_start()
    first_near(3)
    second_forward(1, 2)
    second_near(1, 3)
    second_far(1, 0)
    first_far(3)
    second_start(3, 1)
    second_start(3, 0)
    second_far(1, 1)
    second_far(1, 3)
    first_near(0)
    second_far(1, 2)
    second_near(1, 2)
    second_forward(3, 1)
    la_forward()
    lb_forward()
    copies[3].wait()
    cycle(1)
    second_forward(3, 0)
    second_forward(0, 2)
    first_far(0)
    first_start(2)
    second_start(3, 3)
    second_near(0, 2)
    second_near(3, 1)
    lb_end()
    second_far(3, 0)
    second_far(3, 1)
    la_near()
    cycle_middle(1)
    second_near(3, 0)
    second_forward(0, 0)
    block(1)
    second_near(0, 0)
    second_forward(0, 1)
    second_near(0, 1)
    la_far()
    first_forward(2)
    block(0)
    second_forward(0, 3)
    first_near(2)
    second_forward(3, 3)
    second_start(3, 2)
    second_near(3, 3)
    ladder()
    second_far(0, 2)
    second_far(0, 1)
    second_far(0, 0)
    second_near(0, 3)
    block_middle(0)
    second_far(0, 3)
    second_forward(2, 0)
    second_forward(3, 2)
    block_middle(1)
    second_far(3, 3)
    first_far(2)
    cycle(0)
    second_forward(2, 2)
    block(3)
    second_near(3, 2)
    second_forward(2, 1)
    second_forward(2, 3)
    second_near(2, 1)
    second_near(2, 3)
    second_near(2, 0)
    ladder_middle()
    second_far(2, 0)
    second_near(2, 2)
    second_far(2, 2)
    cycle_middle(0)
    second_far(3, 2)
    second_far(2, 1)
    block_middle(3)
    second_far(2, 3)
    cycle(2)
    block(2)
    block_end(3)
    cycle_middle(2)
    block_end(1)
    block_end(0)
    block_middle(2)
    cycle_end(1)
    cycle_end(0)
    cycle_end(2)
    block_end(2)
    ladder_end()

    for step in range(1, 8 * N):
        source = lax.rem(col + step, 8 * N)
        arrived(fin.at[source], fin_sem.at[source])

    @pl.loop(0, 8 * N, unroll=4)
    def _(source):
        for m in range(fin.shape[2] // lanes):
            both = fin[source, :, m * lanes : (m + 1) * lanes].astype(jnp.float32)
            for n, value in enumerate(joined(both[:8], both[8:])):
                j = source * (fin.shape[2] // lanes * 2) + 2 * m + n
                out_ref[pl.ds(j, 8, stride=pair_count), :] = (ladder_ji[j] + value) / gaps[j]

    for copy in started:
        copy.wait_send()
    for g in range(GROUPS):

        @pl.when(y != 2 * (g % 2))
        def _():
            for h in range(2):
                over_z(g, h).wait_send()

        @pl.when(z != 2 * (g % 2))
        def _():
            for h in range(2):
                over_y(g, h, middle).wait_send()

        if g < LAST:

            @pl.when(mine // pairs != g)
            def _():
                last_copy(g).wait_send()

    for k in range(N):
        for n in range(pairs):
            other, copy = block_copy(k, n)

            @pl.when(col != other)
            def _():
                copy.wait_send()


def per_device(
    ladder_amps,
    ladder_integrals,
    cycle_amps,
    cycle_integrals,
    amp_screen,
    integral_screen,
    occupied_i,
    occupied_j,
    virtual_a,
    virtual_b,
):
    tile = virtual_b.shape[0]
    col_count = lax.axis_size("col")
    all_i, local_k, ac = cycle_amps.shape
    rows, depth = all_i * ac // tile, local_k * tile
    nc = cycle_integrals.shape[1]
    lm, lk = ladder_amps.shape
    lrows, ln = ladder_integrals.shape
    quarter = rows // GROUPS // N
    piece = rows // N // 8
    f32, bf16 = jnp.float32, jnp.bfloat16
    dma = pltpu.SemaphoreType.DMA
    hbm, smem = pl.BlockSpec(memory_space=pl.ANY), pl.BlockSpec(memory_space=pltpu.SMEM)
    return pl.pallas_call(
        functools.partial(kernel, tile * tile),
        out_shape=jax.ShapeDtypeStruct((lm, ln), f32),
        in_specs=[hbm] * 4 + [smem] * 6,
        out_specs=pl.BlockSpec(memory_space=pltpu.VMEM),
        scratch_shapes=[
            pltpu.VMEM((local_k, all_i, ac), bf16),
            pltpu.VMEM((lrows, ln), bf16),
            pltpu.VMEM((occupied_j.shape[0], occupied_i.shape[0], ln), f32),
            pltpu.VMEM((occupied_j.shape[0], occupied_i.shape[0], ln), f32),
            pltpu.VMEM((rows, depth), bf16),
            pltpu.VMEM((lm, lk), bf16),
            pltpu.VMEM((lrows, ln), bf16),
            pltpu.VMEM(cycle_integrals.shape, bf16),
            pltpu.VMEM((rows, depth), bf16),
            pltpu.VMEM((N, N, 2, rows, depth), bf16),
            pltpu.VMEM((N, 2, lm, lk), bf16),
            pltpu.VMEM((N, lrows // N, N * ln), bf16),
            pltpu.VMEM((N, lm, ln), f32),
            pltpu.VMEM((2, lm // 2, ln), f32),
            pltpu.VMEM((2, lm, ln), f32),
            pltpu.VMEM((LAST, N, N, quarter, nc), f32),
            pltpu.VMEM((LAST, 2, N // 2, quarter, nc), f32),
            pltpu.VMEM((LAST, 2, N, quarter, nc), f32),
            pltpu.VMEM((N, N, quarter, nc), f32),
            pltpu.VMEM((N, 2, quarter // 2, nc), f32),
            pltpu.VMEM((N, 2, quarter, nc), f32),
            pltpu.VMEM((GROUPS, N, quarter, nc), bf16),
            pltpu.VMEM((col_count, piece, nc), bf16),
            dma((SENDS,)),
            dma((GROUPS, 2)),
            dma((N, N, 2, GROUPS, 2)),
            dma((N, 2, 2)),
            dma((N,)),
            dma((N, 2)),
            dma((4,)),
            dma((LAST, 4)),
            dma((N, 4)),
            dma((col_count,)),
            dma((5,)),
        ],
        compiler_params=pltpu.CompilerParams(
            collective_id=0, has_side_effects=True, vmem_limit_bytes=56 * 2**20
        ),
        cost_estimate=pl.CostEstimate(
            flops=2 * (N * rows * N * 2 * depth * nc + lm * N * 2 * lk * N * ln),
            bytes_accessed=8 * 2**20,
            transcendentals=0,
        ),
    )(
        cycle_amps.transpose(1, 0, 2),
        ladder_amps,
        ladder_integrals,
        cycle_integrals,
        amp_screen.T,
        integral_screen.T,
        occupied_i,
        occupied_j,
        virtual_a,
        virtual_b,
    )


def solution(mesh):
    placed = (
        P("row", "col"),
        P("row", "col"),
        P(None, "col", "row"),
        P("row", "col"),
        P("row", None),
        P("row", "col"),
        P("row"),
        P(),
        P("col"),
        P(),
    )
    return jax.shard_map(
        per_device, mesh=mesh, in_specs=placed, out_specs=P("row", "col"), check_vma=False
    )
```

```python
import functools

import jax
import jax.numpy as jnp
from jax import lax
from jax.experimental import pallas as pl
from jax.experimental.pallas import tpu as pltpu
from jax.sharding import PartitionSpec as P

MESH = pl.DeviceIdType.MESH
N = 4
SENDS = 304
GROUPS = 4
LAST = GROUPS - 1


def axis_order(core):
    return (core, 1, 0, 1)


def kernel(
    tile_size,
    amps_hbm,
    la_hbm,
    lb_hbm,
    cb_hbm,
    amp_screen,
    integral_screen,
    occupied_i,
    occupied_j,
    virtual_a,
    virtual_b,
    out_ref,
    amps,
    screened,
    gaps,
    ladder_ji,
    s_ref,
    la_ref,
    lb_ref,
    cb_ref,
    middle,
    a_buf,
    la_buf,
    lb_buf,
    lc,
    lc_a,
    lc_b,
    cc,
    cc_a,
    cc_b,
    block_c,
    block_a,
    block_b,
    outb,
    fin,
    send_sem,
    middle_sem,
    a_sem,
    la_sem,
    lx_sem,
    lb_sem,
    lc_sem,
    cc_sem,
    block_sem,
    fin_sem,
    local_sem,
):
    y = lax.axis_index("row")
    col = lax.axis_index("col")
    z = col // 8
    x = (col // 2) % N
    c = col % 2

    def wrap(value):
        return lax.rem(value + 2 * N, N)

    def device(yy, zz, xx, core):
        return (yy, zz * 8 + xx * 2 + core)

    sibling = device(y, z, x, 1 - c)
    copies = [
        pltpu.make_async_copy(src, dst, local_sem.at[n])
        for n, (src, dst) in enumerate(((amps_hbm, amps), (la_hbm, la_ref), (lb_hbm, lb_ref), (cb_hbm, cb_ref)))
    ]
    for copy in copies:
        copy.start()

    rows, depth = s_ref.shape
    group = rows // GROUPS
    half = group // 2

    barrier = pltpu.get_barrier_semaphore()

    def greet(other):
        pl.semaphore_signal(barrier, inc=1, device_id=other, device_id_type=MESH)

    for step in range(1, N):
        greet(device(wrap(y + step), z, x, c))
        greet(device(y, wrap(z + step), x, c))
        greet(device(y, z, wrap(x + step), c))
    greet(sibling)

    local_k, blocks, lanes = amps.shape[0], amps.shape[1] // 8, 128
    low = lax.broadcasted_iota(jnp.int32, (1, lanes), 1) < lanes // 2

    def joined(left, right):
        first_halves = jnp.where(low, left, pltpu.roll(right, lanes // 2, 1))
        second_halves = jnp.where(low, pltpu.roll(left, lanes // 2, 1), right)
        return first_halves, second_halves

    pairs = 8 // GROUPS

    def permute(g):
        for t in range(g * pairs, (g + 1) * pairs):
            row = g * group + (t % pairs) * 16
            for m in range(local_k // 2):
                left, right = (
                    amps[k, :, t * lanes : (t + 1) * lanes].astype(jnp.float32) for k in (2 * m, 2 * m + 1)
                )
                both = joined(left, right)
                for ib in range(blocks):
                    s_ref[pl.ds(row + ib * (group // blocks), 16), m * lanes : (m + 1) * lanes] = jnp.concatenate(
                        [value[ib * 8 : (ib + 1) * 8] for value in both], axis=0
                    ).astype(s_ref.dtype)

    copies[0].wait()
    permute(0)

    pair_count = la_ref.shape[0] // amp_screen.shape[1]
    ladder_tile = (col * la_ref.shape[1]) // tile_size

    def screen_amps():
        copies[1].wait()
        for i in range(amp_screen.shape[1]):
            part = pl.ds(i * pair_count, pair_count)
            keep = amp_screen[ladder_tile, i].astype(jnp.float32).astype(la_ref.dtype)
            la_buf[z, c, part, :] = la_ref[part, :] * keep

    def screen_integrals():
        copies[2].wait()
        side = lb_ref.shape[0] // integral_screen.shape[1]
        for p in range(integral_screen.shape[1]):
            part = pl.ds(p * side, side)
            keep = jnp.where(low, integral_screen[0, p], integral_screen[1, p])
            screened[part, :] = lb_ref[part, :] * keep.astype(jnp.float32).astype(lb_ref.dtype)

    def energies():
        lane = lax.broadcasted_iota(jnp.int32, (8, lanes), 1)
        row = lax.broadcasted_iota(jnp.int32, (8, lanes), 0)
        side = virtual_b.shape[0]
        virtual = jnp.zeros((8, lanes), jnp.float32)
        for b in range(side):
            virtual = jnp.where(lax.rem(lane, side) == b, virtual_b[b], virtual)
        virtual = virtual + jnp.where(low, virtual_a[0], virtual_a[1])
        occupied = jnp.zeros((8, lanes), jnp.float32)
        for i in range(occupied_i.shape[0]):
            occupied = jnp.where(row == i, occupied_i[i], occupied)
        for j in range(occupied_j.shape[0]):
            gaps[j] = virtual - (occupied + occupied_j[j])

    pl.semaphore_wait(barrier, 3 * (N - 1) + 1)

    started = []

    def send(src, dst, sem, other):
        copy = pltpu.make_async_remote_copy(
            src_ref=src,
            dst_ref=dst,
            send_sem=send_sem.at[len(started)],
            recv_sem=sem,
            device_id=other,
            device_id_type=MESH,
        )
        copy.start()
        started.append(copy)

    def arrived(dst, sem):
        pltpu.make_async_remote_copy(
            src_ref=dst,
            dst_ref=dst,
            send_sem=send_sem.at[0],
            recv_sem=sem,
            device_id=sibling,
            device_id_type=MESH,
        ).wait_recv()

    def a_slot(zz, xx, g, h=None):
        if h is None:
            return a_buf.at[zz, xx, c, pl.ds(g * group, group)], a_sem.at[zz, xx, c, g, 0]
        return a_buf.at[zz, xx, c, pl.ds(g * group + h * half, half)], a_sem.at[zz, xx, c, g, h]

    la_half = la_ref.shape[0] // 2

    def la_slot(zz, core, h=None):
        if h is None:
            return la_buf.at[zz, core], la_sem.at[zz, core, 0]
        return la_buf.at[zz, core, pl.ds(h * la_half, la_half)], la_sem.at[zz, core, h]

    lb_rows = lb_buf.shape[1]
    lb_half = lb_rows // 2

    def lb_slot(yy, h):
        return lb_buf.at[yy, pl.ds(h * lb_half, lb_half)], lb_sem.at[yy, h]

    def ring_start(slot, at, plus, minus):
        for h, other in ((0, plus), (1, minus), (1, plus), (0, minus)):
            ref, sem = slot(at, h)
            send(ref, ref, sem, other)

    def ring_forward(slot, at, plus, minus):
        for h, source, other in ((0, wrap(at - 1), plus), (1, wrap(at + 1), minus)):
            ref, sem = slot(source, h)
            arrived(ref, sem)
            send(ref, ref, sem, other)

    def ring_near(slot, at):
        arrived(*slot(wrap(at - 1), 1))
        arrived(*slot(wrap(at + 1), 0))

    def ring_far(slot, at):
        for h in range(2):
            arrived(*slot(wrap(at + 2), h))

    def share(ref, sem):
        send(ref, ref, sem, sibling)

    z_plus, z_minus = device(y, wrap(z + 1), x, c), device(y, wrap(z - 1), x, c)
    x_plus, x_minus = device(y, z, wrap(x + 1), c), device(y, z, wrap(x - 1), c)
    y_plus, y_minus = (wrap(y + 1), col), (wrap(y - 1), col)

    def swapped(g, along=None):
        along = z if along is None else along
        return (y + along) % 2 + 2 * ((y // 2 + along // 2 + g % 2) % 2)

    def group_rows(g):
        return pl.ds(g * group, group)

    def over_z(g, h):
        part = pl.ds(g * group + h * half, half)
        return pltpu.make_async_remote_copy(
            src_ref=s_ref.at[part],
            dst_ref=middle.at[part],
            send_sem=send_sem.at[SENDS - 1 - 2 * g - h],
            recv_sem=middle_sem.at[g, h],
            device_id=device(y, swapped(g), x, c),
            device_id_type=MESH,
        )

    def over_y(g, h, ref):
        part = pl.ds(g * group + h * half, half)
        return pltpu.make_async_remote_copy(
            src_ref=ref.at[part],
            dst_ref=a_buf.at[z, x, c, part],
            send_sem=send_sem.at[SENDS - 1 - 2 * GROUPS - 2 * g - h],
            recv_sem=a_sem.at[z, x, c, g, h],
            device_id=(swapped(g), col),
            device_id_type=MESH,
        )

    def start_over_z(g):
        if g > 0:
            permute(g)

        @pl.when(y != 2 * (g % 2))
        def _():
            for h in range(2):
                over_z(g, h).start()

    def start_over_y(g):
        still = 2 * (g % 2)

        def onward(h, ref):
            @pl.when(z != still)
            def _():
                over_y(g, h, ref).start()

            @pl.when(z == still)
            def _():
                part = pl.ds(g * group + h * half, half)
                a_buf[z, x, c, part, :] = ref[part, :]

        @pl.when(y != still)
        def _():
            for h in range(2):
                over_z(g, h).wait_recv()
                onward(h, middle)

        @pl.when(y == still)
        def _():
            for h in range(2):
                onward(h, s_ref)

    def end_over_y(g, h):
        @pl.when(z != 2 * (g % 2))
        def _():
            over_y(g, h, middle).wait_recv()

    width = lb_ref.shape[1]
    def lb_exchange():
        screen_integrals()
        keep_lb.start()
        for step in range(1, N):
            to = wrap(x + step)
            send(
                screened.at[pl.ds(pl.multiple_of(to * lb_rows, lb_rows), lb_rows)],
                lb_buf.at[y, :, pl.ds(pl.multiple_of(x * width, width), width)],
                lx_sem.at[x],
                device(y, z, to, c),
            )

    keep_lb = pltpu.make_async_copy(
        screened.at[pl.ds(pl.multiple_of(x * lb_rows, lb_rows), lb_rows)],
        lb_buf.at[y, :, pl.ds(pl.multiple_of(x * width, width), width)],
        local_sem.at[4],
    )

    def la_own(p, h=None):
        return la_slot(p, c, h)

    def la_start():
        screen_amps()
        ring_start(la_own, z, z_plus, z_minus)
        share(*la_slot(z, c))

    def la_forward():
        ring_forward(la_own, z, z_plus, z_minus)

    def la_near():
        ring_near(la_own, z)
        for q in (wrap(z - 1), wrap(z + 1)):
            share(*la_slot(q, c))

    def la_far():
        ring_far(la_own, z)
        share(*la_slot(wrap(z + 2), c))

    def lb_start():
        keep_lb.wait()
        for step in range(1, N):
            source = wrap(x + step)
            arrived(lb_buf.at[y, :, pl.ds(pl.multiple_of(source * width, width), width)], lx_sem.at[source])
        ring_start(lb_slot, y, y_plus, y_minus)

    def lb_forward():
        ring_forward(lb_slot, y, y_plus, y_minus)

    def lb_end():
        ring_near(lb_slot, y)
        ring_far(lb_slot, y)

    z_first = axis_order(c)

    def ring_of(is_z):
        dz, dx = is_z, 1 - is_z
        plus = device(y, wrap(z + dz), wrap(x + dx), c)
        minus = device(y, wrap(z - dz), wrap(x - dx), c)
        return is_z * z + (1 - is_z) * x, plus, minus

    def first(g):
        f = z_first[g]
        return (lambda q, h=None: a_slot(f * q + (1 - f) * z, f * x + (1 - f) * q, g, h)), ring_of(f)

    def second(g, k):
        f = z_first[g]
        p = wrap(f * z + (1 - f) * x + (0, 3, 1, 2)[k]) if g < LAST else swapped(g, k)
        return (lambda q, h=None: a_slot(f * p + (1 - f) * q, f * q + (1 - f) * p, g, h)), ring_of(1 - f)

    def second_start(g, k):
        slot, ring = second(g, k)
        ring_start(slot, *ring)
        share(*slot(ring[0]))

    def second_forward(g, k):
        slot, ring = second(g, k)
        ring_forward(slot, *ring)

    def second_near(g, k):
        slot, ring = second(g, k)
        ring_near(slot, ring[0])
        for p in (wrap(ring[0] - 1), wrap(ring[0] + 1)):
            share(*slot(p))

    def second_far(g, k):
        slot, ring = second(g, k)
        ring_far(slot, ring[0])
        share(*slot(wrap(ring[0] + 2)))

    def first_start(g):
        near = (first(g), second(g, 0)) if g < LAST else (first(g),)
        for h in range(2):
            end_over_y(g, h)
            for slot, (at, plus, minus) in near:
                ref, sem = slot(at, h)
                for other in (plus, minus) if h == 0 else (minus, plus):
                    send(ref, ref, sem, other)
        if g < LAST:
            slot, ring = near[1]
            share(*slot(ring[0]))

    def first_forward(g):
        slot, ring = first(g)
        ring_forward(slot, *ring)

    def first_near(g):
        slot, ring = first(g)
        ring_near(slot, ring[0])
        if g < LAST:
            second_start(g, 1)
            second_start(g, 2)

    def first_far(g):
        slot, ring = first(g)
        ring_far(slot, ring[0])
        if g < LAST:
            second_start(g, 3)

    tile = 256
    lk = la_ref.shape[1]

    def ladder():
        for step in range(N):
            arrived(*la_slot(wrap(z + step), 1 - c))

        @pl.loop(0, la_ref.shape[0] // tile)
        def _(m):
            part = pl.ds(pl.multiple_of(m * tile, tile), tile)
            total = jnp.zeros((tile, lb_buf.shape[2]), jnp.float32)
            for zz in range(N):
                for core in range(2):
                    total += jnp.dot(
                        la_buf[zz, core, part, :],
                        lb_buf[zz, pl.ds(core * lk, lk), :],
                        preferred_element_type=jnp.float32,
                    )
            for xx in range(N):
                lc[xx, part, :] = total[:, xx * width : (xx + 1) * width]

        reduce_start(lc, lc_a, lc_sem, x, x_plus, x_minus)

    def ladder_middle():
        reduce_middle(lc, lc_a, lc_b, lc_sem, x, x_plus, x_minus)

    def ladder_end():
        out_ref[...] = reduce_end(lc, lc_b, lc_sem, x)
        for j in range(pair_count):
            ladder_ji[j] = out_ref[pl.ds(j, 8, stride=pair_count), :]

    def reduce_start(ref, land, sem, at, plus, minus):
        size = ref.shape[1] // 2
        for h, other in ((0, plus), (1, minus)):
            send(ref.at[wrap(at + 2), pl.ds(h * size, size)], land.at[h], sem.at[h], other)

    def reduce_middle(ref, land_a, land_b, sem, at, plus, minus):
        size = ref.shape[1] // 2
        for h, to, other in ((0, wrap(at + 1), plus), (1, wrap(at - 1), minus)):
            arrived(land_a.at[h], sem.at[h])
            part = pl.ds(h * size, size)
            ref[to, part, :] = ref[to, part, :] + land_a[h]
            send(ref.at[to], land_b.at[h], sem.at[2 + h], other)

    def reduce_end(ref, land_b, sem, at):
        for h in range(2):
            arrived(land_b.at[h], sem.at[2 + h])
        return ref[at] + land_b[0] + land_b[1]

    quarter = group // N
    piece = quarter // pairs
    mine = x * 2 + c

    def cycle(g):
        for zz in range(N):
            for xx in range(N):
                arrived(a_buf.at[zz, xx, 1 - c, group_rows(g)], a_sem.at[zz, xx, 1 - c, g, 0])
        total = jnp.zeros((rows // GROUPS * N, cb_ref.shape[1]), jnp.float32)
        for xx in range(N):
            for core in range(2):
                left = jnp.concatenate([a_buf[zz, xx, core, group_rows(g), :] for zz in range(N)], axis=0)
                total += jnp.dot(
                    left,
                    cb_ref[pl.ds((xx * 2 + core) * depth, depth), :],
                    preferred_element_type=jnp.float32,
                )
        for zz in range(N):
            owner = swapped(g, zz)
            for n in range(N):
                cc[g, n, owner] = total[zz * group + n * quarter : zz * group + (n + 1) * quarter]
        reduce_start(cc.at[g], cc_a.at[g], cc_sem.at[g], y, y_plus, y_minus)

    def cycle_middle(g):
        reduce_middle(cc.at[g], cc_a.at[g], cc_b.at[g], cc_sem.at[g], y, y_plus, y_minus)

    def last_copy(g):
        turn = lax.rem(mine, pairs)
        return pltpu.make_async_remote_copy(
            src_ref=outb.at[g, z, pl.ds(pl.multiple_of(turn * piece, piece), piece)],
            dst_ref=fin.at[col],
            send_sem=send_sem.at[SENDS - 1 - 4 * GROUPS - g],
            recv_sem=fin_sem.at[col],
            device_id=(y, z * 8 + g * pairs + turn),
            device_id_type=MESH,
        )

    def cycle_end(g):
        outb[g] = reduce_end(cc.at[g], cc_b.at[g], cc_sem.at[g], y).astype(outb.dtype)
        for zstep in range(N):
            zz = wrap(z + zstep)
            for step in range(pairs):
                if zstep == 0 and step == 0:
                    continue
                turn = lax.rem(mine + step, pairs)
                send(
                    outb.at[g, zz, pl.ds(pl.multiple_of(turn * piece, piece), piece)],
                    fin.at[col],
                    fin_sem.at[col],
                    (y, zz * 8 + g * pairs + turn),
                )

        @pl.when(mine // pairs == g)
        def _():
            fin[col] = outb[g, z, pl.ds(pl.multiple_of(lax.rem(mine, pairs) * piece, piece), piece), :]

        @pl.when(mine // pairs != g)
        def _():
            last_copy(g).start()

    def block(k):
        zz = swapped(LAST, k)
        for xx in range(N):
            arrived(a_buf.at[zz, xx, 1 - c, group_rows(LAST)], a_sem.at[zz, xx, 1 - c, LAST, 0])
        total = jnp.zeros((group, cb_ref.shape[1]), jnp.float32)
        for xx in range(N):
            for core in range(2):
                total += jnp.dot(
                    a_buf[zz, xx, core, group_rows(LAST), :],
                    cb_ref[pl.ds((xx * 2 + core) * depth, depth), :],
                    preferred_element_type=jnp.float32,
                )
        for n in range(N):
            block_c[k, n] = total[n * quarter : (n + 1) * quarter]
        reduce_start(block_c.at[k], block_a.at[k], block_sem.at[k], y, y_plus, y_minus)

    def block_middle(k):
        reduce_middle(block_c.at[k], block_a.at[k], block_b.at[k], block_sem.at[k], y, y_plus, y_minus)

    def block_copy(k, n):
        other = k * 8 + LAST * pairs + n
        copy = pltpu.make_async_remote_copy(
            src_ref=outb.at[LAST, k, pl.ds(n * piece, piece)],
            dst_ref=fin.at[col],
            send_sem=send_sem.at[SENDS - 1 - 5 * GROUPS - pairs * k - n],
            recv_sem=fin_sem.at[col],
            device_id=(y, other),
            device_id_type=MESH,
        )
        return other, copy

    def block_end(k):
        outb[LAST, k] = reduce_end(block_c.at[k], block_b.at[k], block_sem.at[k], y).astype(outb.dtype)
        for n in range(pairs):
            other, copy = block_copy(k, n)

            @pl.when(col == other)
            def _():
                fin[col] = outb[LAST, k, pl.ds(n * piece, piece), :]

            @pl.when(col != other)
            def _():
                copy.start()

    start_over_z(0)
    lb_exchange()
    start_over_z(1)
    start_over_z(2)
    start_over_y(0)
    start_over_z(3)
    start_over_y(1)
    first_start(0)
    energies()
    first_start(1)
    start_over_y(3)
    first_forward(0)
    second_forward(1, 0)
    first_start(3)
    first_forward(1)
    first_near(1)
    start_over_y(2)
    first_forward(3)
    la_start()
    second_near(1, 0)
    second_forward(1, 1)
    first_far(1)
    second_forward(1, 3)
    second_near(1, 1)
    lb_start()
    first_near(3)
    second_forward(1, 2)
    second_near(1, 3)
    second_far(1, 0)
    first_far(3)
    second_start(3, 1)
    second_start(3, 0)
    second_far(1, 1)
    second_far(1, 3)
    first_near(0)
    second_far(1, 2)
    second_near(1, 2)
    second_forward(3, 1)
    la_forward()
    lb_forward()
    copies[3].wait()
    cycle(1)
    second_forward(3, 0)
    second_forward(0, 2)
    first_far(0)
    first_start(2)
    second_start(3, 3)
    second_near(0, 2)
    second_near(3, 1)
    lb_end()
    second_far(3, 0)
    second_far(3, 1)
    la_near()
    cycle_middle(1)
    second_near(3, 0)
    second_forward(0, 0)
    block(1)
    second_near(0, 0)
    second_forward(0, 1)
    second_near(0, 1)
    la_far()
    first_forward(2)
    block(0)
    second_forward(0, 3)
    first_near(2)
    second_forward(3, 3)
    second_start(3, 2)
    second_near(3, 3)
    ladder()
    second_far(0, 2)
    second_far(0, 1)
    second_far(0, 0)
    second_near(0, 3)
    block_middle(0)
    second_far(0, 3)
    second_forward(2, 0)
    second_forward(3, 2)
    block_middle(1)
    second_far(3, 3)
    first_far(2)
    cycle(0)
    second_forward(2, 2)
    block(3)
    second_near(3, 2)
    second_forward(2, 1)
    second_forward(2, 3)
    second_near(2, 1)
    second_near(2, 3)
    second_near(2, 0)
    ladder_middle()
    second_far(2, 0)
    second_near(2, 2)
    second_far(2, 2)
    cycle_middle(0)
    second_far(3, 2)
    second_far(2, 1)
    block_middle(3)
    second_far(2, 3)
    cycle(2)
    block(2)
    block_end(3)
    cycle_middle(2)
    block_end(1)
    block_end(0)
    block_middle(2)
    cycle_end(1)
    cycle_end(0)
    cycle_end(2)
    block_end(2)
    ladder_end()

    for step in range(1, 8 * N):
        source = lax.rem(col + step, 8 * N)
        arrived(fin.at[source], fin_sem.at[source])

    @pl.loop(0, 8 * N, unroll=4)
    def _(source):
        for m in range(fin.shape[2] // lanes):
            both = fin[source, :, m * lanes : (m + 1) * lanes].astype(jnp.float32)
            for n, value in enumerate(joined(both[:8], both[8:])):
                j = source * (fin.shape[2] // lanes * 2) + 2 * m + n
                out_ref[pl.ds(j, 8, stride=pair_count), :] = (ladder_ji[j] + value) / gaps[j]

    for copy in started:
        copy.wait_send()
    for g in range(GROUPS):

        @pl.when(y != 2 * (g % 2))
        def _():
            for h in range(2):
                over_z(g, h).wait_send()

        @pl.when(z != 2 * (g % 2))
        def _():
            for h in range(2):
                over_y(g, h, middle).wait_send()

        if g < LAST:

            @pl.when(mine // pairs != g)
            def _():
                last_copy(g).wait_send()

    for k in range(N):
        for n in range(pairs):
            other, copy = block_copy(k, n)

            @pl.when(col != other)
            def _():
                copy.wait_send()


def per_device(
    ladder_amps,
    ladder_integrals,
    cycle_amps,
    cycle_integrals,
    amp_screen,
    integral_screen,
    occupied_i,
    occupied_j,
    virtual_a,
    virtual_b,
):
    tile = virtual_b.shape[0]
    col_count = lax.axis_size("col")
    all_i, local_k, ac = cycle_amps.shape
    rows, depth = all_i * ac // tile, local_k * tile
    nc = cycle_integrals.shape[1]
    lm, lk = ladder_amps.shape
    lrows, ln = ladder_integrals.shape
    quarter = rows // GROUPS // N
    piece = rows // N // 8
    f32, bf16 = jnp.float32, jnp.bfloat16
    dma = pltpu.SemaphoreType.DMA
    hbm, smem = pl.BlockSpec(memory_space=pl.ANY), pl.BlockSpec(memory_space=pltpu.SMEM)
    return pl.pallas_call(
        functools.partial(kernel, tile * tile),
        out_shape=jax.ShapeDtypeStruct((lm, ln), f32),
        in_specs=[hbm] * 4 + [smem] * 6,
        out_specs=pl.BlockSpec(memory_space=pltpu.VMEM),
        scratch_shapes=[
            pltpu.VMEM((local_k, all_i, ac), bf16),
            pltpu.VMEM((lrows, ln), bf16),
            pltpu.VMEM((occupied_j.shape[0], occupied_i.shape[0], ln), f32),
            pltpu.VMEM((occupied_j.shape[0], occupied_i.shape[0], ln), f32),
            pltpu.VMEM((rows, depth), bf16),
            pltpu.VMEM((lm, lk), bf16),
            pltpu.VMEM((lrows, ln), bf16),
            pltpu.VMEM(cycle_integrals.shape, bf16),
            pltpu.VMEM((rows, depth), bf16),
            pltpu.VMEM((N, N, 2, rows, depth), bf16),
            pltpu.VMEM((N, 2, lm, lk), bf16),
            pltpu.VMEM((N, lrows // N, N * ln), bf16),
            pltpu.VMEM((N, lm, ln), f32),
            pltpu.VMEM((2, lm // 2, ln), f32),
            pltpu.VMEM((2, lm, ln), f32),
            pltpu.VMEM((LAST, N, N, quarter, nc), f32),
            pltpu.VMEM((LAST, 2, N // 2, quarter, nc), f32),
            pltpu.VMEM((LAST, 2, N, quarter, nc), f32),
            pltpu.VMEM((N, N, quarter, nc), f32),
            pltpu.VMEM((N, 2, quarter // 2, nc), f32),
            pltpu.VMEM((N, 2, quarter, nc), f32),
            pltpu.VMEM((GROUPS, N, quarter, nc), bf16),
            pltpu.VMEM((col_count, piece, nc), bf16),
            dma((SENDS,)),
            dma((GROUPS, 2)),
            dma((N, N, 2, GROUPS, 2)),
            dma((N, 2, 2)),
            dma((N,)),
            dma((N, 2)),
            dma((4,)),
            dma((LAST, 4)),
            dma((N, 4)),
            dma((col_count,)),
            dma((5,)),
        ],
        compiler_params=pltpu.CompilerParams(
            collective_id=0, has_side_effects=True, vmem_limit_bytes=56 * 2**20
        ),
        cost_estimate=pl.CostEstimate(
            flops=2 * (N * rows * N * 2 * depth * nc + lm * N * 2 * lk * N * ln),
            bytes_accessed=8 * 2**20,
            transcendentals=0,
        ),
    )(
        cycle_amps.transpose(1, 0, 2),
        ladder_amps,
        ladder_integrals,
        cycle_integrals,
        amp_screen.T,
        integral_screen.T,
        occupied_i,
        occupied_j,
        virtual_a,
        virtual_b,
    )


def solution(mesh):
    placed = (
        P("row", "col"),
        P("row", "col"),
        P(None, "col", "row"),
        P("row", "col"),
        P("row", None),
        P("row", "col"),
        P("row"),
        P(),
        P("col"),
        P(),
    )
    return jax.shard_map(
        per_device, mesh=mesh, in_specs=placed, out_specs=P("row", "col"), check_vma=False
    )
```

```python
import functools

import jax
import jax.numpy as jnp
from jax import lax
from jax.experimental import pallas as pl
from jax.experimental.pallas import tpu as pltpu
from jax.sharding import PartitionSpec as P

MESH = pl.DeviceIdType.MESH
N = 4
SENDS = 96
GROUPS = 4
LAST = GROUPS - 1


def axis_order(core):
    return (core, 1, 0, 1)


def kernel(
    tile_size,
    amps_hbm,
    la_hbm,
    lb_hbm,
    cb_hbm,
    amp_screen,
    integral_screen,
    occupied_i,
    occupied_j,
    virtual_a,
    virtual_b,
    out_ref,
    amps,
    screened,
    gaps,
    ladder_ji,
    s_ref,
    la_ref,
    lb_ref,
    cb_ref,
    middle,
    a_buf,
    la_buf,
    lb_buf,
    lc,
    lc_a,
    lc_b,
    cc,
    cc_a,
    cc_b,
    block_c,
    block_a,
    block_b,
    outb,
    fin,
    send_sem,
    sent,
    middle_sem,
    t_sem,
    a_sem,
    share_sem,
    la_sem,
    la_share_sem,
    lx_sem,
    lb_sem,
    lc_sem,
    cc_sem,
    block_sem,
    fin_sem,
    local_sem,
):
    y = lax.axis_index("row")
    col = lax.axis_index("col")
    z = col // 8
    x = (col // 2) % N
    c = col % 2

    def wrap(value):
        return lax.rem(value + 2 * N, N)

    def device(yy, zz, xx, core):
        return (yy, zz * 8 + xx * 2 + core)

    sibling = device(y, z, x, 1 - c)
    copies = [
        pltpu.make_async_copy(src, dst, local_sem.at[n])
        for n, (src, dst) in enumerate(((amps_hbm, amps), (la_hbm, la_ref), (lb_hbm, lb_ref), (cb_hbm, cb_ref)))
    ]
    for copy in copies:
        copy.start()

    rows, depth = s_ref.shape
    group = rows // GROUPS
    half = group // 2

    barrier = pltpu.get_barrier_semaphore()

    def greet(other):
        pl.semaphore_signal(barrier, inc=1, device_id=other, device_id_type=MESH)

    for step in range(1, N):
        greet(device(wrap(y + step), z, x, c))
        greet(device(y, wrap(z + step), x, c))
        greet(device(y, z, wrap(x + step), c))
    greet(sibling)

    local_k, blocks, lanes = amps.shape[0], amps.shape[1] // 8, 128
    low = lax.broadcasted_iota(jnp.int32, (1, lanes), 1) < lanes // 2

    def joined(left, right):
        first_halves = jnp.where(low, left, pltpu.roll(right, lanes // 2, 1))
        second_halves = jnp.where(low, pltpu.roll(left, lanes // 2, 1), right)
        return first_halves, second_halves

    pairs = 8 // GROUPS

    def permute(g):
        for t in range(g * pairs, (g + 1) * pairs):
            row = g * group + (t % pairs) * 16
            for m in range(local_k // 2):
                left, right = (
                    amps[k, :, t * lanes : (t + 1) * lanes].astype(jnp.float32) for k in (2 * m, 2 * m + 1)
                )
                both = joined(left, right)
                for ib in range(blocks):
                    s_ref[pl.ds(row + ib * (group // blocks), 16), m * lanes : (m + 1) * lanes] = jnp.concatenate(
                        [value[ib * 8 : (ib + 1) * 8] for value in both], axis=0
                    ).astype(s_ref.dtype)

    copies[0].wait()
    permute(0)

    pair_count = la_ref.shape[0] // amp_screen.shape[1]
    ladder_tile = (col * la_ref.shape[1]) // tile_size

    def screen_amps():
        copies[1].wait()
        for i in range(amp_screen.shape[1]):
            part = pl.ds(i * pair_count, pair_count)
            keep = amp_screen[ladder_tile, i].astype(jnp.float32).astype(la_ref.dtype)
            la_buf[z, c, part, :] = la_ref[part, :] * keep

    def screen_integrals():
        copies[2].wait()
        side = lb_ref.shape[0] // integral_screen.shape[1]
        for p in range(integral_screen.shape[1]):
            part = pl.ds(p * side, side)
            keep = jnp.where(low, integral_screen[0, p], integral_screen[1, p])
            screened[part, :] = lb_ref[part, :] * keep.astype(jnp.float32).astype(lb_ref.dtype)

    def energies():
        lane = lax.broadcasted_iota(jnp.int32, (8, lanes), 1)
        row = lax.broadcasted_iota(jnp.int32, (8, lanes), 0)
        side = virtual_b.shape[0]
        virtual = jnp.zeros((8, lanes), jnp.float32)
        for b in range(side):
            virtual = jnp.where(lax.rem(lane, side) == b, virtual_b[b], virtual)
        virtual = virtual + jnp.where(low, virtual_a[0], virtual_a[1])
        occupied = jnp.zeros((8, lanes), jnp.float32)
        for i in range(occupied_i.shape[0]):
            occupied = jnp.where(row == i, occupied_i[i], occupied)
        for j in range(occupied_j.shape[0]):
            gaps[j] = virtual - (occupied + occupied_j[j])

    pl.semaphore_wait(barrier, 3 * (N - 1) + 1)

    started = []

    def send(src, dst, sem, other, done=None):
        copy = pltpu.make_async_remote_copy(
            src_ref=src,
            dst_ref=dst,
            send_sem=send_sem.at[len(started)] if done is None else done,
            recv_sem=sem,
            device_id=other,
            device_id_type=MESH,
        )
        copy.start()
        if done is None:
            started.append(copy)

    def arrived(dst, sem):
        pltpu.make_async_remote_copy(
            src_ref=dst,
            dst_ref=dst,
            send_sem=send_sem.at[0],
            recv_sem=sem,
            device_id=sibling,
            device_id_type=MESH,
        ).wait_recv()

    def a_slot(zz, xx, g, h=None):
        if h is None:
            return a_buf.at[zz, xx, c, pl.ds(g * group, group)]
        return a_buf.at[zz, xx, c, pl.ds(g * group + h * half, half)]

    la_half = la_ref.shape[0] // 2

    def la_slot(zz, h=None):
        if h is None:
            return la_buf.at[zz, c]
        return la_buf.at[zz, c, pl.ds(h * la_half, la_half)]

    lb_rows = lb_buf.shape[1]
    lb_half = lb_rows // 2

    def lb_slot(yy, h=None):
        if h is None:
            return lb_buf.at[yy]
        return lb_buf.at[yy, pl.ds(h * lb_half, lb_half)]

    def ring_piece(slot, sems, at, h, other, sem, done):
        ref = slot(at, h)
        send(ref, ref, sems.at[sem], other, done)

    def ring_start(slot, sems, done, at, plus, minus):
        for h, other, sem in ((0, plus, 0), (1, minus, 1), (1, plus, 2), (0, minus, 2)):
            ring_piece(slot, sems, at, h, other, sem, done)

    def ring_forward(slot, sems, done, at, plus, minus):
        for h, source, other in ((0, wrap(at - 1), plus), (1, wrap(at + 1), minus)):
            arrived(slot(source, h), sems.at[h])
            ring_piece(slot, sems, source, h, other, 3, done)

    def ring_near(slot, sems, at):
        arrived(slot(wrap(at - 1)), sems.at[2])

    def ring_far(slot, sems, at):
        arrived(slot(wrap(at + 2)), sems.at[3])

    def share(ref, sem, done):
        send(ref, ref, sem, sibling, done)

    z_plus, z_minus = device(y, wrap(z + 1), x, c), device(y, wrap(z - 1), x, c)
    x_plus, x_minus = device(y, z, wrap(x + 1), c), device(y, z, wrap(x - 1), c)
    y_plus, y_minus = (wrap(y + 1), col), (wrap(y - 1), col)

    def swapped(g, along=None):
        along = z if along is None else along
        return (y + along) % 2 + 2 * ((y // 2 + along // 2 + g % 2) % 2)

    def group_rows(g):
        return pl.ds(g * group, group)

    def over_z(g, h):
        part = pl.ds(g * group + h * half, half)
        return pltpu.make_async_remote_copy(
            src_ref=s_ref.at[part],
            dst_ref=middle.at[part],
            send_sem=send_sem.at[SENDS - 1 - 2 * g - h],
            recv_sem=middle_sem.at[g, h],
            device_id=device(y, swapped(g), x, c),
            device_id_type=MESH,
        )

    def over_y(g, h, ref):
        part = pl.ds(g * group + h * half, half)
        return pltpu.make_async_remote_copy(
            src_ref=ref.at[part],
            dst_ref=a_buf.at[z, x, c, part],
            send_sem=send_sem.at[SENDS - 1 - 2 * GROUPS - 2 * g - h],
            recv_sem=t_sem.at[g, h],
            device_id=(swapped(g), col),
            device_id_type=MESH,
        )

    def start_over_z(g):
        if g > 0:
            permute(g)

        @pl.when(y != 2 * (g % 2))
        def _():
            for h in range(2):
                over_z(g, h).start()

    def start_over_y(g):
        still = 2 * (g % 2)

        def onward(h, ref):
            @pl.when(z != still)
            def _():
                over_y(g, h, ref).start()

            @pl.when(z == still)
            def _():
                part = pl.ds(g * group + h * half, half)
                a_buf[z, x, c, part, :] = ref[part, :]

        @pl.when(y != still)
        def _():
            for h in range(2):
                over_z(g, h).wait_recv()
                onward(h, middle)

        @pl.when(y == still)
        def _():
            for h in range(2):
                onward(h, s_ref)

    def end_over_y(g, h):
        @pl.when(z != 2 * (g % 2))
        def _():
            over_y(g, h, middle).wait_recv()

    width = lb_ref.shape[1]
    def lb_exchange():
        screen_integrals()
        keep_lb.start()
        for step in range(1, N):
            to = wrap(x + step)
            send(
                screened.at[pl.ds(pl.multiple_of(to * lb_rows, lb_rows), lb_rows)],
                lb_buf.at[y, :, pl.ds(pl.multiple_of(x * width, width), width)],
                lx_sem.at[x],
                device(y, z, to, c),
            )

    keep_lb = pltpu.make_async_copy(
        screened.at[pl.ds(pl.multiple_of(x * lb_rows, lb_rows), lb_rows)],
        lb_buf.at[y, :, pl.ds(pl.multiple_of(x * width, width), width)],
        local_sem.at[4],
    )

    la_ring = z, z_plus, z_minus

    def la_share(zz):
        share(la_slot(zz), la_share_sem.at[0], sent.at[2])

    def la_start():
        screen_amps()
        ring_start(la_slot, la_sem, sent.at[2], *la_ring)
        la_share(z)

    def la_forward():
        ring_forward(la_slot, la_sem, sent.at[2], *la_ring)

    def la_near():
        ring_near(la_slot, la_sem, z)
        la_share(wrap(z - 1))
        la_share(wrap(z + 1))

    def la_far():
        ring_far(la_slot, la_sem, z)
        la_share(wrap(z + 2))

    def lb_start():
        keep_lb.wait()
        for step in range(1, N):
            source = wrap(x + step)
            arrived(lb_buf.at[y, :, pl.ds(pl.multiple_of(source * width, width), width)], lx_sem.at[source])
        ring_start(lb_slot, lb_sem, None, y, y_plus, y_minus)

    def lb_forward():
        ring_forward(lb_slot, lb_sem, None, y, y_plus, y_minus)

    def lb_end():
        ring_near(lb_slot, lb_sem, y)
        ring_far(lb_slot, lb_sem, y)

    z_first = axis_order(c)

    def ring_of(is_z):
        dz, dx = is_z, 1 - is_z
        plus = device(y, wrap(z + dz), wrap(x + dx), c)
        minus = device(y, wrap(z - dz), wrap(x - dx), c)
        return is_z * z + (1 - is_z) * x, plus, minus

    def first(g):
        f = z_first[g]

        def slot(q, h=None):
            return a_slot(f * q + (1 - f) * z, f * x + (1 - f) * q, g, h)

        return slot, a_sem.at[g, 0], ring_of(f)

    def second(g, k):
        f = z_first[g]
        p = wrap(f * z + (1 - f) * x + (0, 3, 1, 2)[k]) if g < LAST else swapped(g, k)

        def slot(q, h=None):
            return a_slot(f * p + (1 - f) * q, f * q + (1 - f) * p, g, h)

        return slot, a_sem.at[g, 1 + k], ring_of(1 - f)

    def a_share(slot, at, g, k):
        share(slot(at), share_sem.at[g if g < LAST else LAST + k], sent.at[1])

    def second_start(g, k):
        slot, sems, ring = second(g, k)
        ring_start(slot, sems, sent.at[0], *ring)
        a_share(slot, ring[0], g, k)

    def second_forward(g, k):
        slot, sems, ring = second(g, k)
        ring_forward(slot, sems, sent.at[0], *ring)

    def second_near(g, k):
        slot, sems, ring = second(g, k)
        ring_near(slot, sems, ring[0])
        for p in (wrap(ring[0] - 1), wrap(ring[0] + 1)):
            a_share(slot, p, g, k)

    def second_far(g, k):
        slot, sems, ring = second(g, k)
        ring_far(slot, sems, ring[0])
        a_share(slot, wrap(ring[0] + 2), g, k)

    def first_start(g):
        both = (first(g), second(g, 0)) if g < LAST else (first(g),)
        for h in range(2):
            end_over_y(g, h)
            for slot, sems, (at, plus, minus) in both:
                for other, sem in ((plus, 0), (minus, 2)) if h == 0 else ((minus, 1), (plus, 2)):
                    ring_piece(slot, sems, at, h, other, sem, sent.at[0])
        if g < LAST:
            slot, _, ring = both[1]
            a_share(slot, ring[0], g, 0)

    def first_forward(g):
        slot, sems, ring = first(g)
        ring_forward(slot, sems, sent.at[0], *ring)

    def first_near(g):
        slot, sems, ring = first(g)
        ring_near(slot, sems, ring[0])
        if g < LAST:
            second_start(g, 1)
            second_start(g, 2)

    def first_far(g):
        slot, sems, ring = first(g)
        ring_far(slot, sems, ring[0])
        if g < LAST:
            second_start(g, 3)

    tile = 256
    lk = la_ref.shape[1]

    def ladder():
        arrived(la_buf.at[:, 1 - c], la_share_sem.at[0])

        @pl.loop(0, la_ref.shape[0] // tile)
        def _(m):
            part = pl.ds(pl.multiple_of(m * tile, tile), tile)
            total = jnp.zeros((tile, lb_buf.shape[2]), jnp.float32)
            for zz in range(N):
                for core in range(2):
                    total += jnp.dot(
                        la_buf[zz, core, part, :],
                        lb_buf[zz, pl.ds(core * lk, lk), :],
                        preferred_element_type=jnp.float32,
                    )
            for xx in range(N):
                lc[xx, part, :] = total[:, xx * width : (xx + 1) * width]

        reduce_start(lc, lc_a, lc_sem, x, x_plus, x_minus)

    def ladder_middle():
        reduce_middle(lc, lc_a, lc_b, lc_sem, x, x_plus, x_minus)

    def ladder_end():
        out_ref[...] = reduce_end(lc, lc_b, lc_sem, x)
        for j in range(pair_count):
            ladder_ji[j] = out_ref[pl.ds(j, 8, stride=pair_count), :]

    def reduce_start(ref, land, sem, at, plus, minus):
        size = ref.shape[1] // 2
        for h, other in ((0, plus), (1, minus)):
            send(ref.at[wrap(at + 2), pl.ds(h * size, size)], land.at[h], sem.at[h], other)

    def reduce_middle(ref, land_a, land_b, sem, at, plus, minus):
        size = ref.shape[1] // 2
        for h, to, other in ((0, wrap(at + 1), plus), (1, wrap(at - 1), minus)):
            arrived(land_a.at[h], sem.at[h])
            part = pl.ds(h * size, size)
            ref[to, part, :] = ref[to, part, :] + land_a[h]
            send(ref.at[to], land_b.at[h], sem.at[2 + h], other)

    def reduce_end(ref, land_b, sem, at):
        for h in range(2):
            arrived(land_b.at[h], sem.at[2 + h])
        return ref[at] + land_b[0] + land_b[1]

    quarter = group // N
    piece = quarter // pairs
    mine = x * 2 + c

    def cycle(g):
        arrived(a_buf.at[:, :, 1 - c, group_rows(g)], share_sem.at[g])
        total = jnp.zeros((rows // GROUPS * N, cb_ref.shape[1]), jnp.float32)
        for xx in range(N):
            for core in range(2):
                left = jnp.concatenate([a_buf[zz, xx, core, group_rows(g), :] for zz in range(N)], axis=0)
                total += jnp.dot(
                    left,
                    cb_ref[pl.ds((xx * 2 + core) * depth, depth), :],
                    preferred_element_type=jnp.float32,
                )
        for zz in range(N):
            owner = swapped(g, zz)
            for n in range(N):
                cc[g, n, owner] = total[zz * group + n * quarter : zz * group + (n + 1) * quarter]
        reduce_start(cc.at[g], cc_a.at[g], cc_sem.at[g], y, y_plus, y_minus)

    def cycle_middle(g):
        reduce_middle(cc.at[g], cc_a.at[g], cc_b.at[g], cc_sem.at[g], y, y_plus, y_minus)

    def last_copy(g):
        turn = lax.rem(mine, pairs)
        return pltpu.make_async_remote_copy(
            src_ref=outb.at[g, z, pl.ds(pl.multiple_of(turn * piece, piece), piece)],
            dst_ref=fin.at[col],
            send_sem=send_sem.at[SENDS - 1 - 4 * GROUPS - g],
            recv_sem=fin_sem.at[0],
            device_id=(y, z * 8 + g * pairs + turn),
            device_id_type=MESH,
        )

    def cycle_end(g):
        outb[g] = reduce_end(cc.at[g], cc_b.at[g], cc_sem.at[g], y).astype(outb.dtype)
        for zstep in range(N):
            zz = wrap(z + zstep)
            for step in range(pairs):
                if zstep == 0 and step == 0:
                    continue
                turn = lax.rem(mine + step, pairs)
                send(
                    outb.at[g, zz, pl.ds(pl.multiple_of(turn * piece, piece), piece)],
                    fin.at[col],
                    fin_sem.at[0],
                    (y, zz * 8 + g * pairs + turn),
                )

        @pl.when(mine // pairs == g)
        def _():
            fin[col] = outb[g, z, pl.ds(pl.multiple_of(lax.rem(mine, pairs) * piece, piece), piece), :]

        @pl.when(mine // pairs != g)
        def _():
            last_copy(g).start()

    def block(k):
        zz = swapped(LAST, k)
        arrived(a_buf.at[zz, :, 1 - c, group_rows(LAST)], share_sem.at[LAST + k])
        total = jnp.zeros((group, cb_ref.shape[1]), jnp.float32)
        for xx in range(N):
            for core in range(2):
                total += jnp.dot(
                    a_buf[zz, xx, core, group_rows(LAST), :],
                    cb_ref[pl.ds((xx * 2 + core) * depth, depth), :],
                    preferred_element_type=jnp.float32,
                )
        for n in range(N):
            block_c[k, n] = total[n * quarter : (n + 1) * quarter]
        reduce_start(block_c.at[k], block_a.at[k], block_sem.at[k], y, y_plus, y_minus)

    def block_middle(k):
        reduce_middle(block_c.at[k], block_a.at[k], block_b.at[k], block_sem.at[k], y, y_plus, y_minus)

    def block_copy(k, n):
        other = k * 8 + LAST * pairs + n
        copy = pltpu.make_async_remote_copy(
            src_ref=outb.at[LAST, k, pl.ds(n * piece, piece)],
            dst_ref=fin.at[col],
            send_sem=send_sem.at[SENDS - 1 - 5 * GROUPS - pairs * k - n],
            recv_sem=fin_sem.at[0],
            device_id=(y, other),
            device_id_type=MESH,
        )
        return other, copy

    def block_end(k):
        outb[LAST, k] = reduce_end(block_c.at[k], block_b.at[k], block_sem.at[k], y).astype(outb.dtype)
        for n in range(pairs):
            other, copy = block_copy(k, n)

            @pl.when(col == other)
            def _():
                fin[col] = outb[LAST, k, pl.ds(n * piece, piece), :]

            @pl.when(col != other)
            def _():
                copy.start()

    start_over_z(0)
    lb_exchange()
    start_over_z(1)
    start_over_z(2)
    start_over_y(0)
    start_over_z(3)
    start_over_y(1)
    first_start(0)
    energies()
    first_start(1)
    start_over_y(3)
    first_forward(0)
    second_forward(1, 0)
    first_start(3)
    first_forward(1)
    first_near(1)
    start_over_y(2)
    first_forward(3)
    la_start()
    second_near(1, 0)
    second_forward(1, 1)
    first_far(1)
    second_forward(1, 3)
    second_near(1, 1)
    lb_start()
    first_near(3)
    second_forward(1, 2)
    second_near(1, 3)
    second_far(1, 0)
    first_far(3)
    second_start(3, 1)
    second_start(3, 0)
    second_far(1, 1)
    second_far(1, 3)
    first_near(0)
    second_far(1, 2)
    second_near(1, 2)
    second_forward(3, 1)
    la_forward()
    lb_forward()
    copies[3].wait()
    cycle(1)
    second_forward(3, 0)
    second_forward(0, 2)
    first_far(0)
    first_start(2)
    second_start(3, 3)
    second_near(0, 2)
    second_near(3, 1)
    lb_end()
    second_far(3, 0)
    second_far(3, 1)
    la_near()
    cycle_middle(1)
    second_near(3, 0)
    second_forward(0, 0)
    block(1)
    second_near(0, 0)
    second_forward(0, 1)
    second_near(0, 1)
    la_far()
    first_forward(2)
    block(0)
    second_forward(0, 3)
    first_near(2)
    second_forward(3, 3)
    second_start(3, 2)
    second_near(3, 3)
    ladder()
    second_far(0, 2)
    second_far(0, 1)
    second_far(0, 0)
    second_near(0, 3)
    block_middle(0)
    second_far(0, 3)
    second_forward(2, 0)
    second_forward(3, 2)
    block_middle(1)
    second_far(3, 3)
    first_far(2)
    cycle(0)
    second_forward(2, 2)
    block(3)
    second_near(3, 2)
    second_forward(2, 1)
    second_forward(2, 3)
    second_near(2, 1)
    second_near(2, 3)
    second_near(2, 0)
    ladder_middle()
    second_far(2, 0)
    second_near(2, 2)
    second_far(2, 2)
    cycle_middle(0)
    second_far(3, 2)
    second_far(2, 1)
    block_middle(3)
    second_far(2, 3)
    cycle(2)
    block(2)
    block_end(3)
    cycle_middle(2)
    block_end(1)
    block_end(0)
    block_middle(2)
    cycle_end(1)
    cycle_end(0)
    cycle_end(2)
    block_end(2)
    ladder_end()

    arrived(fin.at[pl.ds(0, 8 * N - 1)], fin_sem.at[0])

    @pl.loop(0, 8 * N, unroll=4)
    def _(source):
        for m in range(fin.shape[2] // lanes):
            both = fin[source, :, m * lanes : (m + 1) * lanes].astype(jnp.float32)
            for n, value in enumerate(joined(both[:8], both[8:])):
                j = source * (fin.shape[2] // lanes * 2) + 2 * m + n
                out_ref[pl.ds(j, 8, stride=pair_count), :] = (ladder_ji[j] + value) / gaps[j]

    ring_rows = GROUPS * 6 * (1 + N) * half // (2 * N * N)
    share_rows = GROUPS * N * N * group // (2 * N * N)
    la_rows = (6 + 2 * N) * la_half // (2 * N)
    for n, ref in enumerate((a_buf.at[:, :, :, :ring_rows], a_buf.at[:, :, :, :share_rows], la_buf.at[:, :, :la_rows])):
        pltpu.make_async_remote_copy(
            src_ref=ref,
            dst_ref=ref,
            send_sem=sent.at[n],
            recv_sem=fin_sem.at[0],
            device_id=sibling,
            device_id_type=MESH,
        ).wait_send()
    for copy in started:
        copy.wait_send()
    for g in range(GROUPS):

        @pl.when(y != 2 * (g % 2))
        def _():
            for h in range(2):
                over_z(g, h).wait_send()

        @pl.when(z != 2 * (g % 2))
        def _():
            for h in range(2):
                over_y(g, h, middle).wait_send()

        if g < LAST:

            @pl.when(mine // pairs != g)
            def _():
                last_copy(g).wait_send()

    for k in range(N):
        for n in range(pairs):
            other, copy = block_copy(k, n)

            @pl.when(col != other)
            def _():
                copy.wait_send()


def per_device(
    ladder_amps,
    ladder_integrals,
    cycle_amps,
    cycle_integrals,
    amp_screen,
    integral_screen,
    occupied_i,
    occupied_j,
    virtual_a,
    virtual_b,
):
    tile = virtual_b.shape[0]
    col_count = lax.axis_size("col")
    all_i, local_k, ac = cycle_amps.shape
    rows, depth = all_i * ac // tile, local_k * tile
    nc = cycle_integrals.shape[1]
    lm, lk = ladder_amps.shape
    lrows, ln = ladder_integrals.shape
    quarter = rows // GROUPS // N
    piece = rows // N // 8
    f32, bf16 = jnp.float32, jnp.bfloat16
    dma = pltpu.SemaphoreType.DMA
    hbm, smem = pl.BlockSpec(memory_space=pl.ANY), pl.BlockSpec(memory_space=pltpu.SMEM)
    return pl.pallas_call(
        functools.partial(kernel, tile * tile),
        out_shape=jax.ShapeDtypeStruct((lm, ln), f32),
        in_specs=[hbm] * 4 + [smem] * 6,
        out_specs=pl.BlockSpec(memory_space=pltpu.VMEM),
        scratch_shapes=[
            pltpu.VMEM((local_k, all_i, ac), bf16),
            pltpu.VMEM((lrows, ln), bf16),
            pltpu.VMEM((occupied_j.shape[0], occupied_i.shape[0], ln), f32),
            pltpu.VMEM((occupied_j.shape[0], occupied_i.shape[0], ln), f32),
            pltpu.VMEM((rows, depth), bf16),
            pltpu.VMEM((lm, lk), bf16),
            pltpu.VMEM((lrows, ln), bf16),
            pltpu.VMEM(cycle_integrals.shape, bf16),
            pltpu.VMEM((rows, depth), bf16),
            pltpu.VMEM((N, N, 2, rows, depth), bf16),
            pltpu.VMEM((N, 2, lm, lk), bf16),
            pltpu.VMEM((N, lrows // N, N * ln), bf16),
            pltpu.VMEM((N, lm, ln), f32),
            pltpu.VMEM((2, lm // 2, ln), f32),
            pltpu.VMEM((2, lm, ln), f32),
            pltpu.VMEM((LAST, N, N, quarter, nc), f32),
            pltpu.VMEM((LAST, 2, N // 2, quarter, nc), f32),
            pltpu.VMEM((LAST, 2, N, quarter, nc), f32),
            pltpu.VMEM((N, N, quarter, nc), f32),
            pltpu.VMEM((N, 2, quarter // 2, nc), f32),
            pltpu.VMEM((N, 2, quarter, nc), f32),
            pltpu.VMEM((GROUPS, N, quarter, nc), bf16),
            pltpu.VMEM((col_count, piece, nc), bf16),
            dma((SENDS,)),
            dma((3,)),
            dma((GROUPS, 2)),
            dma((GROUPS, 2)),
            dma((GROUPS, 1 + N, 4)),
            dma((LAST + N,)),
            dma((4,)),
            dma((1,)),
            dma((N,)),
            dma((4,)),
            dma((4,)),
            dma((LAST, 4)),
            dma((N, 4)),
            dma((1,)),
            dma((5,)),
        ],
        compiler_params=pltpu.CompilerParams(
            collective_id=0, has_side_effects=True, vmem_limit_bytes=56 * 2**20
        ),
        cost_estimate=pl.CostEstimate(
            flops=2 * (N * rows * N * 2 * depth * nc + lm * N * 2 * lk * N * ln),
            bytes_accessed=8 * 2**20,
            transcendentals=0,
        ),
    )(
        cycle_amps.transpose(1, 0, 2),
        ladder_amps,
        ladder_integrals,
        cycle_integrals,
        amp_screen.T,
        integral_screen.T,
        occupied_i,
        occupied_j,
        virtual_a,
        virtual_b,
    )


def solution(mesh):
    placed = (
        P("row", "col"),
        P("row", "col"),
        P(None, "col", "row"),
        P("row", "col"),
        P("row", None),
        P("row", "col"),
        P("row"),
        P(),
        P("col"),
        P(),
    )
    return jax.shard_map(
        per_device, mesh=mesh, in_specs=placed, out_specs=P("row", "col"), check_vma=False
    )
```

```python
import functools

import jax
import jax.numpy as jnp
from jax import lax
from jax.experimental import pallas as pl
from jax.experimental.pallas import tpu as pltpu
from jax.sharding import PartitionSpec as P

MESH = pl.DeviceIdType.MESH
N = 4
SENDS = 96
GROUPS = 4
LAST = GROUPS - 1


def axis_order(core):
    return (core, 1, 0, 1)


def kernel(
    tile_size,
    amps_hbm,
    la_hbm,
    lb_hbm,
    cb_hbm,
    amp_screen,
    integral_screen,
    occupied_i,
    occupied_j,
    virtual_a,
    virtual_b,
    out_any,
    out_ref,
    amps,
    screened,
    gaps,
    ladder_ji,
    s_ref,
    la_ref,
    lb_ref,
    cb_ref,
    middle,
    a_buf,
    la_buf,
    lb_buf,
    lc,
    lc_a,
    lc_b,
    cc,
    cc_a,
    cc_b,
    block_c,
    block_a,
    block_b,
    outb,
    fin,
    send_sem,
    sent,
    middle_sem,
    t_sem,
    a_sem,
    share_sem,
    la_sem,
    la_share_sem,
    lx_sem,
    lb_sem,
    lc_sem,
    cc_sem,
    block_sem,
    fin_sem,
    local_sem,
):
    y = lax.axis_index("row")
    col = lax.axis_index("col")
    z = col // 8
    x = (col // 2) % N
    c = col % 2

    def wrap(value):
        return lax.rem(value + 2 * N, N)

    def device(yy, zz, xx, core):
        return (yy, zz * 8 + xx * 2 + core)

    sibling = device(y, z, x, 1 - c)
    copies = [
        pltpu.make_async_copy(src, dst, local_sem.at[n])
        for n, (src, dst) in enumerate(((amps_hbm, amps), (la_hbm, la_ref), (lb_hbm, lb_ref), (cb_hbm, cb_ref)))
    ]
    for copy in copies:
        copy.start()

    rows, depth = s_ref.shape
    group = rows // GROUPS
    half = group // 2

    barrier = pltpu.get_barrier_semaphore()

    def greet(other):
        pl.semaphore_signal(barrier, inc=1, device_id=other, device_id_type=MESH)

    for step in range(1, N):
        greet(device(wrap(y + step), z, x, c))
        greet(device(y, wrap(z + step), x, c))
        greet(device(y, z, wrap(x + step), c))
    greet(sibling)

    local_k, blocks, lanes = amps.shape[0], amps.shape[1] // 8, 128
    low = lax.broadcasted_iota(jnp.int32, (1, lanes), 1) < lanes // 2

    def joined(left, right):
        first_halves = jnp.where(low, left, pltpu.roll(right, lanes // 2, 1))
        second_halves = jnp.where(low, pltpu.roll(left, lanes // 2, 1), right)
        return first_halves, second_halves

    pairs = 8 // GROUPS

    def permute(g):
        for t in range(g * pairs, (g + 1) * pairs):
            row = g * group + (t % pairs) * 16
            for m in range(local_k // 2):
                left, right = (
                    amps[k, :, t * lanes : (t + 1) * lanes].astype(jnp.float32) for k in (2 * m, 2 * m + 1)
                )
                both = joined(left, right)
                for ib in range(blocks):
                    s_ref[pl.ds(row + ib * (group // blocks), 16), m * lanes : (m + 1) * lanes] = jnp.concatenate(
                        [value[ib * 8 : (ib + 1) * 8] for value in both], axis=0
                    ).astype(s_ref.dtype)

    copies[0].wait()
    permute(0)

    pair_count = la_ref.shape[0] // amp_screen.shape[1]
    ladder_tile = (col * la_ref.shape[1]) // tile_size

    def screen_amps():
        copies[1].wait()
        for i in range(amp_screen.shape[1]):
            part = pl.ds(i * pair_count, pair_count)
            keep = amp_screen[ladder_tile, i].astype(jnp.float32).astype(la_ref.dtype)
            la_buf[z, c, part, :] = la_ref[part, :] * keep

    def screen_integrals():
        copies[2].wait()
        side = lb_ref.shape[0] // integral_screen.shape[1]
        for p in range(integral_screen.shape[1]):
            part = pl.ds(p * side, side)
            keep = jnp.where(low, integral_screen[0, p], integral_screen[1, p])
            screened[part, :] = lb_ref[part, :] * keep.astype(jnp.float32).astype(lb_ref.dtype)

    def energies():
        lane = lax.broadcasted_iota(jnp.int32, (8, lanes), 1)
        row = lax.broadcasted_iota(jnp.int32, (8, lanes), 0)
        side = virtual_b.shape[0]
        virtual = jnp.zeros((8, lanes), jnp.float32)
        for b in range(side):
            virtual = jnp.where(lax.rem(lane, side) == b, virtual_b[b], virtual)
        virtual = virtual + jnp.where(low, virtual_a[0], virtual_a[1])
        occupied = jnp.zeros((8, lanes), jnp.float32)
        for i in range(occupied_i.shape[0]):
            occupied = jnp.where(row == i, occupied_i[i], occupied)
        for j in range(occupied_j.shape[0]):
            gaps[j] = virtual - (occupied + occupied_j[j])

    pl.semaphore_wait(barrier, 3 * (N - 1) + 1)

    started = []

    def send(src, dst, sem, other, done=None):
        copy = pltpu.make_async_remote_copy(
            src_ref=src,
            dst_ref=dst,
            send_sem=send_sem.at[len(started)] if done is None else done,
            recv_sem=sem,
            device_id=other,
            device_id_type=MESH,
        )
        copy.start()
        if done is None:
            started.append(copy)

    def arrived(dst, sem):
        pltpu.make_async_remote_copy(
            src_ref=dst,
            dst_ref=dst,
            send_sem=send_sem.at[0],
            recv_sem=sem,
            device_id=sibling,
            device_id_type=MESH,
        ).wait_recv()

    def a_slot(zz, xx, g, h=None):
        if h is None:
            return a_buf.at[zz, xx, c, pl.ds(g * group, group)]
        return a_buf.at[zz, xx, c, pl.ds(g * group + h * half, half)]

    la_half = la_ref.shape[0] // 2

    def la_slot(zz, h=None):
        if h is None:
            return la_buf.at[zz, c]
        return la_buf.at[zz, c, pl.ds(h * la_half, la_half)]

    lb_rows = lb_buf.shape[1]
    lb_half = lb_rows // 2

    def lb_slot(yy, h=None):
        if h is None:
            return lb_buf.at[yy]
        return lb_buf.at[yy, pl.ds(h * lb_half, lb_half)]

    def ring_piece(slot, sems, at, h, other, sem, done):
        ref = slot(at, h)
        send(ref, ref, sems.at[sem], other, done)

    def ring_start(slot, sems, done, at, plus, minus):
        for h, other, sem in ((0, plus, 0), (1, minus, 1), (1, plus, 2), (0, minus, 2)):
            ring_piece(slot, sems, at, h, other, sem, done)

    def ring_forward(slot, sems, done, at, plus, minus):
        for h, source, other in ((0, wrap(at - 1), plus), (1, wrap(at + 1), minus)):
            arrived(slot(source, h), sems.at[h])
            ring_piece(slot, sems, source, h, other, 3, done)

    def ring_near(slot, sems, at):
        arrived(slot(wrap(at - 1)), sems.at[2])

    def ring_far(slot, sems, at):
        arrived(slot(wrap(at + 2)), sems.at[3])

    def share(ref, sem, done):
        send(ref, ref, sem, sibling, done)

    z_plus, z_minus = device(y, wrap(z + 1), x, c), device(y, wrap(z - 1), x, c)
    x_plus, x_minus = device(y, z, wrap(x + 1), c), device(y, z, wrap(x - 1), c)
    y_plus, y_minus = (wrap(y + 1), col), (wrap(y - 1), col)

    def swapped(g, along=None):
        along = z if along is None else along
        return (y + along) % 2 + 2 * ((y // 2 + along // 2 + g % 2) % 2)

    def group_rows(g):
        return pl.ds(g * group, group)

    def over_z(g, h):
        part = pl.ds(g * group + h * half, half)
        return pltpu.make_async_remote_copy(
            src_ref=s_ref.at[part],
            dst_ref=middle.at[part],
            send_sem=send_sem.at[SENDS - 1 - 2 * g - h],
            recv_sem=middle_sem.at[g, h],
            device_id=device(y, swapped(g), x, c),
            device_id_type=MESH,
        )

    def over_y(g, h, ref):
        part = pl.ds(g * group + h * half, half)
        return pltpu.make_async_remote_copy(
            src_ref=ref.at[part],
            dst_ref=a_buf.at[z, x, c, part],
            send_sem=send_sem.at[SENDS - 1 - 2 * GROUPS - 2 * g - h],
            recv_sem=t_sem.at[g, h],
            device_id=(swapped(g), col),
            device_id_type=MESH,
        )

    def start_over_z(g):
        if g > 0:
            permute(g)

        @pl.when(y != 2 * (g % 2))
        def _():
            for h in range(2):
                over_z(g, h).start()

    def start_over_y(g):
        still = 2 * (g % 2)

        def onward(h, ref):
            @pl.when(z != still)
            def _():
                over_y(g, h, ref).start()

            @pl.when(z == still)
            def _():
                part = pl.ds(g * group + h * half, half)
                a_buf[z, x, c, part, :] = ref[part, :]

        @pl.when(y != still)
        def _():
            for h in range(2):
                over_z(g, h).wait_recv()
                onward(h, middle)

        @pl.when(y == still)
        def _():
            for h in range(2):
                onward(h, s_ref)

    def end_over_y(g, h):
        @pl.when(z != 2 * (g % 2))
        def _():
            over_y(g, h, middle).wait_recv()

    width = lb_ref.shape[1]
    def lb_exchange():
        screen_integrals()
        keep_lb.start()
        for step in range(1, N):
            to = wrap(x + step)
            send(
                screened.at[pl.ds(pl.multiple_of(to * lb_rows, lb_rows), lb_rows)],
                lb_buf.at[y, :, pl.ds(pl.multiple_of(x * width, width), width)],
                lx_sem.at[x],
                device(y, z, to, c),
            )

    keep_lb = pltpu.make_async_copy(
        screened.at[pl.ds(pl.multiple_of(x * lb_rows, lb_rows), lb_rows)],
        lb_buf.at[y, :, pl.ds(pl.multiple_of(x * width, width), width)],
        local_sem.at[4],
    )

    la_ring = z, z_plus, z_minus

    def la_share(zz):
        share(la_slot(zz), la_share_sem.at[0], sent.at[2])

    def la_start():
        screen_amps()
        ring_start(la_slot, la_sem, sent.at[2], *la_ring)
        la_share(z)

    def la_forward():
        ring_forward(la_slot, la_sem, sent.at[2], *la_ring)

    def la_near():
        ring_near(la_slot, la_sem, z)
        la_share(wrap(z - 1))
        la_share(wrap(z + 1))

    def la_far():
        ring_far(la_slot, la_sem, z)
        la_share(wrap(z + 2))

    def lb_start():
        keep_lb.wait()
        for step in range(1, N):
            source = wrap(x + step)
            arrived(lb_buf.at[y, :, pl.ds(pl.multiple_of(source * width, width), width)], lx_sem.at[source])
        ring_start(lb_slot, lb_sem, None, y, y_plus, y_minus)

    def lb_forward():
        ring_forward(lb_slot, lb_sem, None, y, y_plus, y_minus)

    def lb_end():
        ring_near(lb_slot, lb_sem, y)
        ring_far(lb_slot, lb_sem, y)

    z_first = axis_order(c)

    def ring_of(is_z):
        dz, dx = is_z, 1 - is_z
        plus = device(y, wrap(z + dz), wrap(x + dx), c)
        minus = device(y, wrap(z - dz), wrap(x - dx), c)
        return is_z * z + (1 - is_z) * x, plus, minus

    def first(g):
        f = z_first[g]

        def slot(q, h=None):
            return a_slot(f * q + (1 - f) * z, f * x + (1 - f) * q, g, h)

        return slot, a_sem.at[g, 0], ring_of(f)

    def second(g, k):
        f = z_first[g]
        p = wrap(f * z + (1 - f) * x + (0, 3, 1, 2)[k]) if g < LAST else swapped(g, k)

        def slot(q, h=None):
            return a_slot(f * p + (1 - f) * q, f * q + (1 - f) * p, g, h)

        return slot, a_sem.at[g, 1 + k], ring_of(1 - f)

    def a_share(slot, at, g, k):
        share(slot(at), share_sem.at[g if g < LAST else LAST + k], sent.at[1])

    def second_start(g, k):
        slot, sems, ring = second(g, k)
        ring_start(slot, sems, sent.at[0], *ring)
        a_share(slot, ring[0], g, k)

    def second_forward(g, k):
        slot, sems, ring = second(g, k)
        ring_forward(slot, sems, sent.at[0], *ring)

    def second_near(g, k):
        slot, sems, ring = second(g, k)
        ring_near(slot, sems, ring[0])
        for p in (wrap(ring[0] - 1), wrap(ring[0] + 1)):
            a_share(slot, p, g, k)

    def second_far(g, k):
        slot, sems, ring = second(g, k)
        ring_far(slot, sems, ring[0])
        a_share(slot, wrap(ring[0] + 2), g, k)

    def first_start(g):
        both = (first(g), second(g, 0)) if g < LAST else (first(g),)
        for h in range(2):
            end_over_y(g, h)
            for slot, sems, (at, plus, minus) in both:
                for other, sem in ((plus, 0), (minus, 2)) if h == 0 else ((minus, 1), (plus, 2)):
                    ring_piece(slot, sems, at, h, other, sem, sent.at[0])
        if g < LAST:
            slot, _, ring = both[1]
            a_share(slot, ring[0], g, 0)

    def first_forward(g):
        slot, sems, ring = first(g)
        ring_forward(slot, sems, sent.at[0], *ring)

    def first_near(g):
        slot, sems, ring = first(g)
        ring_near(slot, sems, ring[0])
        if g < LAST:
            second_start(g, 1)
            second_start(g, 2)

    def first_far(g):
        slot, sems, ring = first(g)
        ring_far(slot, sems, ring[0])
        if g < LAST:
            second_start(g, 3)

    tile = 256
    lk = la_ref.shape[1]

    def ladder():
        arrived(la_buf.at[:, 1 - c], la_share_sem.at[0])

        @pl.loop(0, la_ref.shape[0] // tile)
        def _(m):
            part = pl.ds(pl.multiple_of(m * tile, tile), tile)
            total = jnp.zeros((tile, lb_buf.shape[2]), jnp.float32)
            for zz in range(N):
                for core in range(2):
                    total += jnp.dot(
                        la_buf[zz, core, part, :],
                        lb_buf[zz, pl.ds(core * lk, lk), :],
                        preferred_element_type=jnp.float32,
                    )
            for xx in range(N):
                lc[xx, part, :] = total[:, xx * width : (xx + 1) * width]

        reduce_start(lc, lc_a, lc_sem, x, x_plus, x_minus)

    def ladder_middle():
        reduce_middle(lc, lc_a, lc_b, lc_sem, x, x_plus, x_minus)

    def ladder_end():
        out_ref[pl.ds(0, out_any.shape[0]), :] = reduce_end(lc, lc_b, lc_sem, x)
        for j in range(pair_count):
            ladder_ji[j] = out_ref[pl.ds(j, 8, stride=pair_count), :]

    def reduce_start(ref, land, sem, at, plus, minus):
        size = ref.shape[1] // 2
        for h, other in ((0, plus), (1, minus)):
            send(ref.at[wrap(at + 2), pl.ds(h * size, size)], land.at[h], sem.at[h], other)

    def reduce_middle(ref, land_a, land_b, sem, at, plus, minus):
        size = ref.shape[1] // 2
        for h, to, other in ((0, wrap(at + 1), plus), (1, wrap(at - 1), minus)):
            arrived(land_a.at[h], sem.at[h])
            part = pl.ds(h * size, size)
            ref[to, part, :] = ref[to, part, :] + land_a[h]
            send(ref.at[to], land_b.at[h], sem.at[2 + h], other)

    def reduce_end(ref, land_b, sem, at):
        for h in range(2):
            arrived(land_b.at[h], sem.at[2 + h])
        return ref[at] + land_b[0] + land_b[1]

    quarter = group // N
    piece = quarter // pairs
    mine = x * 2 + c

    def cycle(g):
        arrived(a_buf.at[:, :, 1 - c, group_rows(g)], share_sem.at[g])
        total = jnp.zeros((rows // GROUPS * N, cb_ref.shape[1]), jnp.float32)
        for xx in range(N):
            for core in range(2):
                left = jnp.concatenate([a_buf[zz, xx, core, group_rows(g), :] for zz in range(N)], axis=0)
                total += jnp.dot(
                    left,
                    cb_ref[pl.ds((xx * 2 + core) * depth, depth), :],
                    preferred_element_type=jnp.float32,
                )
        for zz in range(N):
            owner = swapped(g, zz)
            for n in range(N):
                cc[g, n, owner] = total[zz * group + n * quarter : zz * group + (n + 1) * quarter]
        reduce_start(cc.at[g], cc_a.at[g], cc_sem.at[g], y, y_plus, y_minus)

    def cycle_middle(g):
        reduce_middle(cc.at[g], cc_a.at[g], cc_b.at[g], cc_sem.at[g], y, y_plus, y_minus)

    def last_copy(g):
        turn = lax.rem(mine, pairs)
        return pltpu.make_async_remote_copy(
            src_ref=outb.at[g, z, pl.ds(pl.multiple_of(turn * piece, piece), piece)],
            dst_ref=fin.at[col],
            send_sem=send_sem.at[SENDS - 1 - 4 * GROUPS - g],
            recv_sem=fin_sem.at[0],
            device_id=(y, z * 8 + g * pairs + turn),
            device_id_type=MESH,
        )

    def cycle_end(g):
        outb[g] = reduce_end(cc.at[g], cc_b.at[g], cc_sem.at[g], y).astype(outb.dtype)
        for zstep in range(N):
            zz = wrap(z + zstep)
            for step in range(pairs):
                if zstep == 0 and step == 0:
                    continue
                turn = lax.rem(mine + step, pairs)
                send(
                    outb.at[g, zz, pl.ds(pl.multiple_of(turn * piece, piece), piece)],
                    fin.at[col],
                    fin_sem.at[0],
                    (y, zz * 8 + g * pairs + turn),
                )

        @pl.when(mine // pairs == g)
        def _():
            fin[col] = outb[g, z, pl.ds(pl.multiple_of(lax.rem(mine, pairs) * piece, piece), piece), :]

        @pl.when(mine // pairs != g)
        def _():
            last_copy(g).start()

    def block(k):
        zz = swapped(LAST, k)
        arrived(a_buf.at[zz, :, 1 - c, group_rows(LAST)], share_sem.at[LAST + k])
        total = jnp.zeros((group, cb_ref.shape[1]), jnp.float32)
        for xx in range(N):
            for core in range(2):
                total += jnp.dot(
                    a_buf[zz, xx, core, group_rows(LAST), :],
                    cb_ref[pl.ds((xx * 2 + core) * depth, depth), :],
                    preferred_element_type=jnp.float32,
                )
        for n in range(N):
            block_c[k, n] = total[n * quarter : (n + 1) * quarter]
        reduce_start(block_c.at[k], block_a.at[k], block_sem.at[k], y, y_plus, y_minus)

    def block_middle(k):
        reduce_middle(block_c.at[k], block_a.at[k], block_b.at[k], block_sem.at[k], y, y_plus, y_minus)

    def block_copy(k, n):
        other = k * 8 + LAST * pairs + n
        copy = pltpu.make_async_remote_copy(
            src_ref=outb.at[LAST, k, pl.ds(n * piece, piece)],
            dst_ref=fin.at[col],
            send_sem=send_sem.at[SENDS - 1 - 5 * GROUPS - pairs * k - n],
            recv_sem=fin_sem.at[0],
            device_id=(y, other),
            device_id_type=MESH,
        )
        return other, copy

    def block_end(k):
        outb[LAST, k] = reduce_end(block_c.at[k], block_b.at[k], block_sem.at[k], y).astype(outb.dtype)
        for n in range(pairs):
            other, copy = block_copy(k, n)

            @pl.when(col == other)
            def _():
                fin[col] = outb[LAST, k, pl.ds(n * piece, piece), :]

            @pl.when(col != other)
            def _():
                copy.start()

    start_over_z(0)
    lb_exchange()
    start_over_z(1)
    start_over_z(2)
    start_over_y(0)
    start_over_z(3)
    start_over_y(1)
    first_start(0)
    energies()
    first_start(1)
    start_over_y(3)
    first_forward(0)
    second_forward(1, 0)
    first_start(3)
    first_forward(1)
    first_near(1)
    start_over_y(2)
    first_forward(3)
    la_start()
    second_near(1, 0)
    second_forward(1, 1)
    first_far(1)
    second_forward(1, 3)
    second_near(1, 1)
    lb_start()
    first_near(3)
    second_forward(1, 2)
    second_near(1, 3)
    second_far(1, 0)
    first_far(3)
    second_start(3, 1)
    second_start(3, 0)
    second_far(1, 1)
    second_far(1, 3)
    first_near(0)
    second_far(1, 2)
    second_near(1, 2)
    second_forward(3, 1)
    la_forward()
    lb_forward()
    copies[3].wait()
    cycle(1)
    second_forward(3, 0)
    second_forward(0, 2)
    first_far(0)
    first_start(2)
    second_start(3, 3)
    second_near(0, 2)
    second_near(3, 1)
    lb_end()
    second_far(3, 0)
    second_far(3, 1)
    la_near()
    cycle_middle(1)
    second_near(3, 0)
    second_forward(0, 0)
    block(1)
    second_near(0, 0)
    second_forward(0, 1)
    second_near(0, 1)
    la_far()
    first_forward(2)
    block(0)
    second_forward(0, 3)
    first_near(2)
    second_forward(3, 3)
    second_start(3, 2)
    second_near(3, 3)
    ladder()
    second_far(0, 2)
    second_far(0, 1)
    second_far(0, 0)
    second_near(0, 3)
    block_middle(0)
    second_far(0, 3)
    second_forward(2, 0)
    second_forward(3, 2)
    block_middle(1)
    second_far(3, 3)
    first_far(2)
    cycle(0)
    second_forward(2, 2)
    block(3)
    second_near(3, 2)
    second_forward(2, 1)
    second_forward(2, 3)
    second_near(2, 1)
    second_near(2, 3)
    second_near(2, 0)
    ladder_middle()
    second_far(2, 0)
    second_near(2, 2)
    second_far(2, 2)
    cycle_middle(0)
    second_far(3, 2)
    second_far(2, 1)
    block_middle(3)
    second_far(2, 3)
    cycle(2)
    block(2)
    block_end(3)
    cycle_middle(2)
    block_end(1)
    block_end(0)
    block_middle(2)
    cycle_end(1)
    cycle_end(0)
    cycle_end(2)
    block_end(2)
    ladder_end()

    arrived(fin.at[pl.ds(0, 8 * N - 1)], fin_sem.at[0])

    @pl.loop(0, 8 * N, unroll=4)
    def _(source):
        for m in range(fin.shape[2] // lanes):
            both = fin[source, :, m * lanes : (m + 1) * lanes].astype(jnp.float32)
            for n, value in enumerate(joined(both[:8], both[8:])):
                j = source * (fin.shape[2] // lanes * 2) + 2 * m + n
                out_ref[pl.ds(j, 8, stride=pair_count), :] = (ladder_ji[j] + value) / gaps[j]

    result = pltpu.make_async_copy(out_ref.at[pl.ds(0, out_any.shape[0])], out_any, local_sem.at[5])
    result.start()

    ring_rows = GROUPS * 6 * (1 + N) * half // (2 * N * N)
    share_rows = GROUPS * N * N * group // (2 * N * N)
    la_rows = (6 + 2 * N) * la_half // (2 * N)
    for n, ref in enumerate((a_buf.at[:, :, :, :ring_rows], a_buf.at[:, :, :, :share_rows], la_buf.at[:, :, :la_rows])):
        pltpu.make_async_remote_copy(
            src_ref=ref,
            dst_ref=ref,
            send_sem=sent.at[n],
            recv_sem=fin_sem.at[0],
            device_id=sibling,
            device_id_type=MESH,
        ).wait_send()
    for copy in started:
        copy.wait_send()
    result.wait()
    for g in range(GROUPS):

        @pl.when(y != 2 * (g % 2))
        def _():
            for h in range(2):
                over_z(g, h).wait_send()

        @pl.when(z != 2 * (g % 2))
        def _():
            for h in range(2):
                over_y(g, h, middle).wait_send()

        if g < LAST:

            @pl.when(mine // pairs != g)
            def _():
                last_copy(g).wait_send()

    for k in range(N):
        for n in range(pairs):
            other, copy = block_copy(k, n)

            @pl.when(col != other)
            def _():
                copy.wait_send()


def per_device(
    ladder_amps,
    ladder_integrals,
    cycle_amps,
    cycle_integrals,
    amp_screen,
    integral_screen,
    occupied_i,
    occupied_j,
    virtual_a,
    virtual_b,
):
    tile = virtual_b.shape[0]
    col_count = lax.axis_size("col")
    all_i, local_k, ac = cycle_amps.shape
    rows, depth = all_i * ac // tile, local_k * tile
    nc = cycle_integrals.shape[1]
    lm, lk = ladder_amps.shape
    lrows, ln = ladder_integrals.shape
    quarter = rows // GROUPS // N
    piece = rows // N // 8
    f32, bf16 = jnp.float32, jnp.bfloat16
    dma = pltpu.SemaphoreType.DMA
    hbm, smem = pl.BlockSpec(memory_space=pl.ANY), pl.BlockSpec(memory_space=pltpu.SMEM)
    return pl.pallas_call(
        functools.partial(kernel, tile * tile),
        out_shape=jax.ShapeDtypeStruct((lm, ln), f32),
        in_specs=[hbm] * 4 + [smem] * 6,
        out_specs=hbm,
        scratch_shapes=[
            pltpu.VMEM((lm + occupied_j.shape[0], ln), f32),
            pltpu.VMEM((local_k, all_i, ac), bf16),
            pltpu.VMEM((lrows, ln), bf16),
            pltpu.VMEM((occupied_j.shape[0], occupied_i.shape[0], ln), f32),
            pltpu.VMEM((occupied_j.shape[0], occupied_i.shape[0], ln), f32),
            pltpu.VMEM((rows, depth), bf16),
            pltpu.VMEM((lm, lk), bf16),
            pltpu.VMEM((lrows, ln), bf16),
            pltpu.VMEM(cycle_integrals.shape, bf16),
            pltpu.VMEM((rows, depth), bf16),
            pltpu.VMEM((N, N, 2, rows, depth), bf16),
            pltpu.VMEM((N, 2, lm, lk), bf16),
            pltpu.VMEM((N, lrows // N, N * ln), bf16),
            pltpu.VMEM((N, lm, ln), f32),
            pltpu.VMEM((2, lm // 2, ln), f32),
            pltpu.VMEM((2, lm, ln), f32),
            pltpu.VMEM((LAST, N, N, quarter, nc), f32),
            pltpu.VMEM((LAST, 2, N // 2, quarter, nc), f32),
            pltpu.VMEM((LAST, 2, N, quarter, nc), f32),
            pltpu.VMEM((N, N, quarter, nc), f32),
            pltpu.VMEM((N, 2, quarter // 2, nc), f32),
            pltpu.VMEM((N, 2, quarter, nc), f32),
            pltpu.VMEM((GROUPS, N, quarter, nc), bf16),
            pltpu.VMEM((col_count, piece, nc), bf16),
            dma((SENDS,)),
            dma((3,)),
            dma((GROUPS, 2)),
            dma((GROUPS, 2)),
            dma((GROUPS, 1 + N, 4)),
            dma((LAST + N,)),
            dma((4,)),
            dma((1,)),
            dma((N,)),
            dma((4,)),
            dma((4,)),
            dma((LAST, 4)),
            dma((N, 4)),
            dma((1,)),
            dma((6,)),
        ],
        compiler_params=pltpu.CompilerParams(
            collective_id=0, has_side_effects=True, vmem_limit_bytes=56 * 2**20
        ),
        cost_estimate=pl.CostEstimate(
            flops=2 * (N * rows * N * 2 * depth * nc + lm * N * 2 * lk * N * ln),
            bytes_accessed=8 * 2**20,
            transcendentals=0,
        ),
    )(
        cycle_amps.transpose(1, 0, 2),
        ladder_amps,
        ladder_integrals,
        cycle_integrals,
        amp_screen.T,
        integral_screen.T,
        occupied_i,
        occupied_j,
        virtual_a,
        virtual_b,
    )


def solution(mesh):
    placed = (
        P("row", "col"),
        P("row", "col"),
        P(None, "col", "row"),
        P("row", "col"),
        P("row", None),
        P("row", "col"),
        P("row"),
        P(),
        P("col"),
        P(),
    )
    return jax.shard_map(
        per_device, mesh=mesh, in_specs=placed, out_specs=P("row", "col"), check_vma=False
    )
```
